128 devices in a mesh: seq: 32 (over x, z_hi, y), chan: 4 (over z_lo, core).
Axes of the slice: x: 4, y: 4, z: 4 (z_hi: 2, z_lo: 2; z = z_hi * 2 + z_lo), core: 2. Of those that a mesh axis runs over, the one named last changes fastest.
Arguments:
- layer_input: bfloat16 [4096, 16384], P('chan', 'seq'), may hold values from -6 to 6
- query_proj: bfloat16 [4096, 16384], P('chan', 'seq'), may hold values from -6 to 6
- key_proj: bfloat16 [4096, 16384], P('chan', 'seq'), may hold values from -6 to 6
- value_proj: bfloat16 [4096, 16384], P('chan', 'seq'), may hold values from -6 to 6
- filter_taps: float32 [8, 16384], P('chan', 'seq'), may hold values from -1 to 1
- grad_out: bfloat16 [4096, 16384], P('chan', 'seq'), may hold values from -6 to 6
Outputs:
- mixed_out: bfloat16 [4096, 16384], P('chan', 'seq')
- grad_query: bfloat16 [4096, 16384], P('chan', 'seq')
- grad_key: bfloat16 [4096, 16384], P('chan', 'seq')
- grad_value: bfloat16 [4096, 16384], P('chan', 'seq')
- filter_grad: float32 [8, 16384], P('chan', 'seq')
- weight_grad: float32 [4096, 4096], P('seq', 'chan')
The draws below stay inside these ranges and needn't reach their ends.
All inputs are finite; a program needn't handle non-finite values.
Results may differ from the reference program's by a relative error of at most 0.0058.
Values may be sent and summed in bfloat16 or wider, within the bound.
A program may use at most 128 MiB of HBM per device.

```python
import math
import jax
import jax.numpy as jnp
from jax import lax

D = 4096
GROUP = 512
LENGTH = 16384
GROUPS = 8


def draw_filter_taps(key, part):
    first_key, second_key = jax.random.split(jax.random.fold_in(key, 7))
    positions = jnp.arange(LENGTH, dtype=jnp.int32).astype(jnp.float32)
    envelope = 0.45 / jnp.sqrt(positions + 8.0)
    noise = jnp.clip(jax.random.normal(first_key, (GROUPS, LENGTH), jnp.float32), -4.0, 4.0)
    gains = jax.random.uniform(second_key, (GROUPS, 1), jnp.float32, 0.7, 1.4)
    return gains * envelope[None, :] * noise


def strengthened(result, own_key, source, target, shards_of, factor):
    owner, partner = [(jnp.arange(result.shape[position]) // (result.shape[position] // shards_of)).reshape([-1 if axis == position else 1 for axis in range(result.ndim)]) for position in (source, target)]
    chosen = jax.random.permutation(own_key, shards_of)[partner]
    strong = (owner == chosen) | (owner == (partner + shards_of // 2) % shards_of)
    return jnp.where(strong, factor * result, result)


def steps_of(stream_key, dims, shards, least, largest):
    level, own = 1.0, jax.random.fold_in(stream_key, 6)
    for dim, blocks in shards:
        steps = jnp.exp(jax.random.uniform(jax.random.fold_in(own, dim), (blocks,), jnp.float32, least / len(shards), largest / len(shards)))
        level = level * jnp.repeat(steps, dims[dim] // blocks).reshape([-1 if axis == dim else 1 for axis in range(len(dims))])
    return level


def normal_values(key, shape, width, most, cuts=(), kind=jnp.bfloat16):
    drawn = width * jax.random.normal(key, shape, jnp.float32)
    if cuts:
        drawn = drawn * steps_of(key, shape, cuts, -0.22, 0.18)
    return jnp.clip(drawn, -most, most).astype(kind)


def noise_with(key, dims, deviation, bound, shards, heavy, kind=jnp.bfloat16):
    drawn = deviation * jax.random.normal(key, dims, jnp.float32)
    if shards:
        drawn = drawn * steps_of(key, dims, shards, -0.22, 0.18)
    return jnp.clip(strengthened(drawn, jax.random.fold_in(key, 3), *heavy), -bound, bound).astype(kind)


def setup_inputs(seed: int = 0) -> dict:
    arg_keys = jax.random.split(jax.random.key(seed), 7)
    layer_input = noise_with(arg_keys[0], (D, LENGTH), 1.0, 6.0, ((0, 4), (1, 32)), (1, 0, 32, 2.75))
    query_proj = normal_values(arg_keys[1], (D, LENGTH), 1.0, 6.0, ((0, 4), (1, 32)))
    key_proj = normal_values(arg_keys[2], (D, LENGTH), 1.0, 6.0, ((0, 4), (1, 32)))
    value_proj = normal_values(arg_keys[3], (D, LENGTH), 1.0, 6.0, ((0, 4), (1, 32)))
    filter_taps = draw_filter_taps(jax.random.fold_in(arg_keys[6], 71), 0)
    grad_out = normal_values(arg_keys[5], (D, LENGTH), 1.0, 6.0, ((0, 4), (1, 32)))
    return {"layer_input": layer_input, "query_proj": query_proj, "key_proj": key_proj, "value_proj": value_proj, "filter_taps": filter_taps, "grad_out": grad_out}


def group_terms(group_block):
    query_rows, key_rows, value_rows, grad_rows, taps = group_block
    float_type = jnp.float32
    mixed_in = (key_rows.astype(float_type) * value_rows.astype(float_type)).astype(jnp.bfloat16)
    upstream = (grad_rows.astype(float_type) * query_rows.astype(float_type)).astype(jnp.bfloat16)
    padded = 2 * LENGTH
    spectrum_in = jnp.fft.rfft(mixed_in.astype(float_type), n=padded, axis=1)
    spectrum_up = jnp.fft.rfft(upstream.astype(float_type), n=padded, axis=1)
    spectrum_taps = jnp.fft.rfft(taps, n=padded)
    conv_out = jnp.fft.irfft(spectrum_in * spectrum_taps[None, :], n=padded, axis=1)[:, :LENGTH]
    conv_out = conv_out.astype(jnp.bfloat16)
    grad_mixed = jnp.fft.irfft(spectrum_up * jnp.conj(spectrum_taps)[None, :], n=padded, axis=1)[:, :LENGTH]
    grad_mixed = grad_mixed.astype(jnp.bfloat16)
    taps_grad = jnp.fft.irfft(lax.optimization_barrier(jnp.sum(spectrum_up * jnp.conj(spectrum_in), axis=0)), n=padded)[:LENGTH]
    taps_grad = taps_grad * (1.0 / math.sqrt(GROUP * LENGTH))
    conv_float = conv_out.astype(float_type)
    grad_float = grad_mixed.astype(float_type)
    mixed_out = (query_rows.astype(float_type) * conv_float).astype(jnp.bfloat16)
    grad_query = (grad_rows.astype(float_type) * conv_float).astype(jnp.bfloat16)
    grad_key = (grad_float * value_rows.astype(float_type)).astype(jnp.bfloat16)
    grad_value = (grad_float * key_rows.astype(float_type)).astype(jnp.bfloat16)
    return (mixed_out, grad_query, grad_key, grad_value, taps_grad)

def reference(layer_input, query_proj, key_proj, value_proj, filter_taps, grad_out):
    groups = D // GROUP
    shaped = (query_proj.reshape(groups, GROUP, LENGTH), key_proj.reshape(groups, GROUP, LENGTH), value_proj.reshape(groups, GROUP, LENGTH), grad_out.reshape(groups, GROUP, LENGTH), filter_taps)
    mixed_out, grad_query, grad_key, grad_value, filter_grad = lax.map(group_terms, shaped)
    mixed_out = mixed_out.reshape(D, LENGTH)
    grad_query = grad_query.reshape(D, LENGTH)
    grad_key = grad_key.reshape(D, LENGTH)
    grad_value = grad_value.reshape(D, LENGTH)
    weight_grad = jnp.dot(layer_input, grad_query.T, preferred_element_type=jnp.float32)
    weight_grad = weight_grad * (1.0 / math.sqrt(LENGTH))
    return (mixed_out, grad_query, grad_key, grad_value, filter_grad, weight_grad)
```

```python
import functools
import math

import jax
import jax.numpy as jnp
from jax import lax
from jax.experimental import pallas as pl
from jax.experimental.pallas import tpu as pltpu
from jax.sharding import PartitionSpec as P

GROUP = 512
F32 = jnp.float32
BF16 = jnp.bfloat16
MESH = pl.DeviceIdType.MESH

N = 32
CH = 32
T = 512
B = 256
NB = N * T // B
PAD = 8
ROWS = N * CH
KINDS = 6
MIXED, UP, TAPS, CONV, BACK, FILT = range(KINDS)


def seq_copy(src, dst, kind, peer, sems, me):
    send, recv = sems
    return pltpu.make_async_remote_copy(
        src_ref=src,
        dst_ref=dst,
        send_sem=send.at[kind, peer],
        recv_sem=recv.at[kind, me],
        device_id={"seq": peer},
        device_id_type=MESH,
    )


def for_peers(me, body):
    def step(i, carry):
        body(lax.rem(me + i, N))
        return carry

    lax.fori_loop(1, N, step, 0)


def loop(n, body, start=0):
    def step(i, carry):
        body(i)
        return carry

    lax.fori_loop(start, n, step, 0)


def kernel(
    x_ref,
    q_ref,
    k_ref,
    v_ref,
    taps_ref,
    g_ref,
    mixed_out_ref,
    grad_query_ref,
    grad_key_ref,
    grad_value_ref,
    filter_grad_ref,
    weight_grad_ref,
    mixed_send,
    up_send,
    taps_send,
    taps_all,
    mixed_all,
    up_all,
    mixed_flip,
    toeplitz,
    acc,
    conv_send,
    back_send,
    conv_all,
    back_all,
    filt_part,
    filt_send,
    filt_all,
    x_all,
    part_a,
    part_b,
    first_in,
    first_out,
    second_in,
    second_out,
    third_in,
    send_sem,
    recv_sem,
    x_send_sem,
    x_recv_sem,
    r_send_sem,
    r_recv_sem,
    z_send_sem,
    z_recv_sem,
):
    me = lax.axis_index("seq")
    chan = lax.axis_index("chan")
    ix = me // 8
    iz = lax.rem(me // 4, 2)
    iy = lax.rem(me, 4)
    sems = (send_sem, recv_sem)

    barrier = pltpu.get_barrier_semaphore()
    for_peers(
        me,
        lambda peer: pl.semaphore_signal(
            barrier, inc=1, device_id={"seq": peer}, device_id_type=MESH
        ),
    )
    core_peer = chan + 1 - 2 * lax.rem(chan, 2)
    near_peer = lax.rem(chan + 2, 4)
    for peer in (core_peer, near_peer):
        pl.semaphore_signal(barrier, inc=1, device_id={"chan": peer}, device_id_type=MESH)

    def make_mixed(r):
        rows = pl.ds(pl.multiple_of(r * 128, 128), 128)
        prod = (k_ref[rows, :].astype(F32) * v_ref[rows, :].astype(F32)).astype(BF16)
        mixed_send[0, rows, :] = prod[:, :B]
        mixed_send[1, rows, :] = prod[:, B:]

    def make_up(r):
        rows = pl.ds(pl.multiple_of(r * 128, 128), 128)
        prod = (g_ref[rows, :].astype(F32) * q_ref[rows, :].astype(F32)).astype(BF16)
        up_send[0, rows, :] = prod[:, :B]
        up_send[1, rows, :] = prod[:, B:]

    for g in range(2):
        for c in range(4):
            taps_send[g, c : c + 1, :] = taps_ref[g : g + 1, c * 128 : (c + 1) * 128]
        taps_send[g, 4:8, :] = jnp.zeros((4, 128), F32)
    loop(ROWS // 128, make_mixed)
    pl.semaphore_wait(barrier, N + 1)

    def chan_rows(peer):
        return pl.ds(pl.multiple_of(peer * CH, CH), CH)

    def taps_copy(peer):
        return seq_copy(taps_send.at[peer // 16], taps_all.at[me], TAPS, peer, sems, me)

    def mixed_copy(peer):
        return seq_copy(
            mixed_send.at[:, chan_rows(peer), :],
            mixed_all.at[pl.ds(PAD + 2 * me, 2)],
            MIXED,
            peer,
            sems,
            me,
        )

    def up_copy(peer):
        return seq_copy(
            up_send.at[:, chan_rows(peer), :],
            up_all.at[pl.ds(2 * me, 2)],
            UP,
            peer,
            sems,
            me,
        )

    def conv_copy(peer):
        return seq_copy(
            conv_send.at[pl.ds(2 * peer, 2)],
            conv_all.at[:, chan_rows(me), :],
            CONV,
            peer,
            sems,
            me,
        )

    def back_copy(peer):
        return seq_copy(
            back_send.at[pl.ds(2 * peer, 2)],
            back_all.at[:, chan_rows(me), :],
            BACK,
            peer,
            sems,
            me,
        )

    def filt_copy(peer):
        return seq_copy(filt_send.at[peer], filt_all.at[me], FILT, peer, sems, me)

    def wait_all(kind, dst_of, src_any):
        def one(peer):
            pltpu.make_async_remote_copy(
                src_ref=src_any,
                dst_ref=dst_of(peer),
                send_sem=send_sem.at[kind, peer],
                recv_sem=recv_sem.at[kind, peer],
                device_id={"seq": peer},
                device_id_type=MESH,
            ).wait_recv()

        for_peers(me, one)

    for_peers(me, lambda peer: taps_copy(peer).start())
    for_peers(me, lambda peer: mixed_copy(peer).start())
    loop(ROWS // 128, make_up)
    for_peers(me, lambda peer: up_copy(peer).start())

    taps_all[me] = taps_send[me // 16]
    mixed_all[pl.ds(PAD + 2 * me, 2)] = mixed_send[:, chan_rows(me), :]
    up_all[pl.ds(2 * me, 2)] = up_send[:, chan_rows(me), :]
    mixed_all[:PAD] = jnp.zeros((PAD, CH, B), BF16)
    up_all[NB:] = jnp.zeros((PAD, CH, B), BF16)

    wait_all(TAPS, lambda peer: taps_all.at[peer], taps_send.at[0])
    row_id = lax.broadcasted_iota(jnp.int32, (B, B), 0)
    col_id = lax.broadcasted_iota(jnp.int32, (B, B), 1)

    def sheared(src, half):
        piece = taps_all[src]
        wide = jnp.concatenate(
            [piece[2 * half : 2 * half + 1, :], piece[2 * half + 1 : 2 * half + 2, :]], axis=1
        )
        return pltpu.roll(jnp.broadcast_to(wide, (B, B)), 0, 1, stride=1, stride_axis=0)

    acc[...] = jnp.zeros((B, B), F32)

    def make_tiles(s):
        for half in range(2):
            now = sheared(s, half)
            toeplitz[2 * s + half] = jnp.where(col_id >= row_id, now, acc[...]).astype(BF16)
            acc[...] = now

    loop(N, make_tiles)

    wait_all(MIXED, lambda peer: mixed_all.at[pl.ds(PAD + 2 * peer, 2)], mixed_send.at[:, :CH, :])

    def hand_back(i, copy, send, dest):
        for r in range(4):
            peer = 4 * i + r

            @pl.when(peer != me)
            def _():
                copy(peer).start()

            @pl.when(peer == me)
            def _():
                dest[:, chan_rows(me), :] = send[pl.ds(2 * me, 2)]

    def conv_chunk(step):
        i = lax.rem(me // 4 + step, 8)
        acc[...] = jnp.zeros((B, B), F32)

        def some(j):
            part = None
            for u in range(8):
                m = 8 * j + u
                lhs = mixed_all[pl.ds(PAD + 8 * i - m, 8)].reshape(B, B)
                term = jnp.dot(lhs, toeplitz[m], preferred_element_type=F32)
                part = term if part is None else part + term
            acc[...] += part

        loop(i + 1, some)
        conv_send[pl.ds(8 * i, 8)] = acc[...].astype(BF16).reshape(8, CH, B)
        hand_back(i, conv_copy, conv_send, conv_all)

    own_x = pl.ds(pl.multiple_of(chan * ROWS, ROWS), ROWS)
    near_x = pl.ds(pl.multiple_of(near_peer * ROWS, ROWS), ROWS)

    def x_copy(slot, src, rows, peer):
        return pltpu.make_async_remote_copy(
            src_ref=src,
            dst_ref=x_all.at[rows, :],
            send_sem=x_send_sem.at[slot],
            recv_sem=x_recv_sem.at[slot],
            device_id={"chan": peer},
            device_id_type=MESH,
        )

    x_core = x_copy(0, x_ref, own_x, core_peer)
    x_near = x_copy(1, x_ref, own_x, near_peer)
    x_pass = x_copy(2, x_all.at[near_x, :], near_x, core_peer)
    x_core.start()
    x_near.start()
    x_all[own_x, :] = x_ref[...]
    loop(8, conv_chunk)

    wait_all(UP, lambda peer: up_all.at[pl.ds(2 * peer, 2)], up_send.at[:, :CH, :])

    def back_chunk(step):
        i = lax.rem(me // 4 + step, 8)
        acc[...] = jnp.zeros((B, B), F32)

        def some(j):
            part = None
            for u in range(8):
                m = 8 * j + u
                lhs = up_all[pl.ds(8 * i + m, 8)].reshape(B, B)
                term = lax.dot_general(
                    lhs, toeplitz[m], (((1,), (1,)), ((), ())), preferred_element_type=F32
                )
                part = term if part is None else part + term
            acc[...] += part

        loop(8 - i, some)
        back_send[pl.ds(8 * i, 8)] = acc[...].astype(BF16).reshape(8, CH, B)
        hand_back(i, back_copy, back_send, back_all)

    loop(8, back_chunk)
    x_near.wait_recv()
    x_pass.start()

    wait_all(CONV, lambda peer: conv_all.at[:, chan_rows(peer), :], conv_send.at[:2])

    def use_conv(r):
        rows = pl.ds(pl.multiple_of(r * 128, 128), 128)
        for half in range(2):
            cols = slice(half * B, (half + 1) * B)
            conv = conv_all[half, rows, :].astype(F32)
            grad_query_ref[rows, cols] = (g_ref[rows, cols].astype(F32) * conv).astype(BF16)
            mixed_out_ref[rows, cols] = (q_ref[rows, cols].astype(F32) * conv).astype(BF16)

    loop(ROWS // 128, use_conv)
    x_core.wait_recv()
    x_pass.wait_recv()

    def weight_share(r):
        px, pz = r // 2, lax.rem(r, 2)
        rows = pl.ds(pl.multiple_of(r * 512, 512), 512)
        for half in range(2):
            share = lax.dot_general(
                x_all[rows, :],
                grad_query_ref[half * 512 : (half + 1) * 512, :],
                (((1,), (1,)), ((), ())),
                preferred_element_type=F32,
            ).astype(BF16)
            if half == 0:
                part_a[px, pz] = share.reshape(4, 128, 512)
            else:
                for py in range(4):
                    part_b[py, pz, px] = share[py * 128 : (py + 1) * 128, :]

    loop(8, weight_share)

    def x_peer(d):
        return lax.rem(ix + d, 4) * 8 + iz * 4 + iy

    def y_peer(d):
        return ix * 8 + iz * 4 + lax.rem(iy + d, 4)

    def ring_copy(half, stage, slot, src, dst, peer):
        return pltpu.make_async_remote_copy(
            src_ref=src,
            dst_ref=dst,
            send_sem=r_send_sem.at[half, stage, slot],
            recv_sem=r_recv_sem.at[half, stage, slot],
            device_id={"seq": peer},
            device_id_type=MESH,
        )

    def ring_copies(half, stage, part, inbox, index, peer_of):
        up, down, far = (lax.rem(index + d, 4) for d in (1, 3, 2))
        return (
            ring_copy(half, stage, 0, part.at[far, 0], inbox.at[0], peer_of(1)),
            ring_copy(half, stage, 1, part.at[far, 1], inbox.at[1], peer_of(3)),
            ring_copy(half, stage, 2, part.at[up, 1], inbox.at[2], peer_of(1)),
            ring_copy(half, stage, 3, part.at[down, 0], inbox.at[3], peer_of(3)),
            ring_copy(half, stage, 4, part.at[up, 0], inbox.at[4], peer_of(1)),
            ring_copy(half, stage, 5, part.at[down, 1], inbox.at[5], peer_of(3)),
        )

    def ring_start(copies):
        for c in copies[:4]:
            c.start()

    def ring_middle(copies, part, inbox, index, blocks):
        for slot, there, side in ((0, 1, 0), (1, 3, 1)):
            copies[slot].wait_recv()
            target = lax.rem(index + there, 4)

            def add(e):
                total = part[target, side, e].astype(F32) + inbox[slot, e].astype(F32)
                part[target, side, e] = total.astype(BF16)

            loop(blocks, add)
            copies[4 + slot].start()

    def ring_end(copies, part, inbox, index, blocks, store):
        for slot in (2, 3, 4, 5):
            copies[slot].wait_recv()

        def add(e):
            for side, one, two in ((0, 4, 3), (1, 5, 2)):
                total = part[index, side, e].astype(F32) + (
                    inbox[one, e].astype(F32) + inbox[two, e].astype(F32)
                )
                store(side, e, total)

        loop(blocks, add)

    halves = (
        (part_a, ix, x_peer, iy, y_peer),
        (part_b, iy, y_peer, ix, x_peer),
    )
    firsts = []
    for half, (part, index, peer_of, _, _) in enumerate(halves):
        copies = ring_copies(half, 0, part, first_in.at[half], index, peer_of)
        ring_start(copies)
        firsts.append(copies)

    flip = (row_id + col_id == B - 1).astype(BF16)
    for c in range(8):
        piece = mixed_all[PAD + 8 * c : PAD + 8 * c + 8].reshape(B, B)
        mixed_flip[:, c * B : (c + 1) * B] = lax.dot_general(
            flip, piece, (((1,), (1,)), ((), ())), preferred_element_type=F32
        ).astype(BF16)

    def filter_tile(i, m):
        depth = (8 - i) * B
        corr = jnp.dot(
            mixed_flip[:, :depth],
            up_all[pl.ds(m, 8 * (8 - i))].reshape(depth, B),
            preferred_element_type=F32,
        )
        turned = pltpu.roll(corr, 1, 1, stride=1, stride_axis=0)
        above = jnp.where(col_id <= row_id, turned, 0.0)
        below = turned - above
        filt_part[0, m] = jnp.sum(above.reshape(B // 8, 8, B), axis=0)
        filt_part[1, m] = jnp.sum(below.reshape(B // 8, 8, B), axis=0)

    def filter_some(i):
        loop(8, lambda u: filter_tile(i, 8 * i + u))

    for i in range(4):
        filter_some(i)
    for half, (part, index, _, _, _) in enumerate(halves):
        ring_middle(firsts[half], part, first_in.at[half], index, 4)
    for i in range(4, 8):
        filter_some(i)

    filt_part[1, NB] = jnp.zeros((8, B), F32)
    taps_factor = 1.0 / math.sqrt(GROUP * N * T)

    def filter_rows(s):
        for half in range(2):
            m = 2 * s + half
            both = jnp.sum(filt_part[0, m] + filt_part[1, m + 1], axis=0, keepdims=True)
            filt_send[s, 2 * half : 2 * half + 1, :] = both[:, :128] * taps_factor
            filt_send[s, 2 * half + 1 : 2 * half + 2, :] = both[:, 128:] * taps_factor
        filt_send[s, 4:8, :] = jnp.zeros((4, 128), F32)

    loop(N, filter_rows)
    for_peers(me, lambda peer: filt_copy(peer).start())
    filt_all[me] = filt_send[me]

    wait_all(BACK, lambda peer: back_all.at[:, chan_rows(peer), :], back_send.at[:2])

    def use_back(r):
        rows = pl.ds(pl.multiple_of(r * 128, 128), 128)
        for half in range(2):
            cols = slice(half * B, (half + 1) * B)
            back = back_all[half, rows, :].astype(F32)
            grad_key_ref[rows, cols] = (v_ref[rows, cols].astype(F32) * back).astype(BF16)
            grad_value_ref[rows, cols] = (k_ref[rows, cols].astype(F32) * back).astype(BF16)

    loop(ROWS // 128, use_back)

    seconds = []
    for half, (part, index, _, across, across_peer) in enumerate(halves):

        def store(side, e, total):
            first_out[half, e, side, 0] = total.astype(BF16)

        ring_end(firsts[half], part, first_in.at[half], index, 4, store)
        copies = ring_copies(
            half, 1, first_out.at[half], second_in.at[half], across, across_peer
        )
        ring_start(copies)
        seconds.append(copies)
    for half, (_, _, _, across, _) in enumerate(halves):
        ring_middle(seconds[half], first_out.at[half], second_in.at[half], across, 1)

    wait_all(FILT, lambda peer: filt_all.at[peer], filt_send.at[0])
    for g in range(2):
        total = jnp.sum(filt_all[16 * g : 16 * g + 16], axis=0)
        for c in range(4):
            filter_grad_ref[g : g + 1, c * 128 : (c + 1) * 128] = total[c : c + 1, :]

    thirds = []
    other = ix * 8 + (1 - iz) * 4 + iy
    for half, (_, _, _, across, _) in enumerate(halves):

        def keep(side, e, total):
            second_out[half, side] = total.astype(BF16)

        ring_end(seconds[half], first_out.at[half], second_in.at[half], across, 1, keep)
        copy = pltpu.make_async_remote_copy(
            src_ref=second_out.at[half, 1 - iz],
            dst_ref=third_in.at[half],
            send_sem=z_send_sem.at[half],
            recv_sem=z_recv_sem.at[half],
            device_id={"seq": other},
            device_id_type=MESH,
        )
        copy.start()
        thirds.append(copy)
    weight_factor = 1.0 / math.sqrt(N * T)
    for half in range(2):
        thirds[half].wait_recv()
        total = second_out[half, iz].astype(F32) + third_in[half].astype(F32)
        weight_grad_ref[:, half * 512 : (half + 1) * 512] = total * weight_factor

    for make in (taps_copy, mixed_copy, up_copy, conv_copy, back_copy, filt_copy):
        for_peers(me, lambda peer: make(peer).wait_send())
    for c in (x_core, x_near, x_pass, *firsts[0], *firsts[1], *seconds[0], *seconds[1], *thirds):
        c.wait_send()


def per_device(layer_input, query_proj, key_proj, value_proj, filter_taps, grad_out):
    vmem = pl.BlockSpec(memory_space=pltpu.VMEM)
    rows = jax.ShapeDtypeStruct((ROWS, T), BF16)
    return tuple(
        pl.pallas_call(
            kernel,
            out_shape=(
                rows,
                rows,
                rows,
                rows,
                jax.ShapeDtypeStruct((2, T), F32),
                jax.ShapeDtypeStruct((128, ROWS), F32),
            ),
            in_specs=[vmem] * 6,
            out_specs=[vmem] * 6,
            scratch_shapes=[
                pltpu.VMEM((2, ROWS, B), BF16),
                pltpu.VMEM((2, ROWS, B), BF16),
                pltpu.VMEM((2, 8, 128), F32),
                pltpu.VMEM((N, 8, 128), F32),
                pltpu.VMEM((PAD + NB, CH, B), BF16),
                pltpu.VMEM((NB + PAD, CH, B), BF16),
                pltpu.VMEM((B, NB * CH), BF16),
                pltpu.VMEM((NB, B, B), BF16),
                pltpu.VMEM((B, B), F32),
                pltpu.VMEM((NB, CH, B), BF16),
                pltpu.VMEM((NB, CH, B), BF16),
                pltpu.VMEM((2, ROWS, B), BF16),
                pltpu.VMEM((2, ROWS, B), BF16),
                pltpu.VMEM((2, NB + 1, 8, B), F32),
                pltpu.VMEM((N, 8, 128), F32),
                pltpu.VMEM((N, 8, 128), F32),
                pltpu.VMEM((4 * ROWS, T), BF16),
                pltpu.VMEM((4, 2, 4, 128, 512), BF16),
                pltpu.VMEM((4, 2, 4, 128, 512), BF16),
                pltpu.VMEM((2, 6, 4, 128, 512), BF16),
                pltpu.VMEM((2, 4, 2, 1, 128, 512), BF16),
                pltpu.VMEM((2, 6, 1, 128, 512), BF16),
                pltpu.VMEM((2, 2, 128, 512), BF16),
                pltpu.VMEM((2, 128, 512), BF16),
                pltpu.SemaphoreType.DMA((KINDS, N)),
                pltpu.SemaphoreType.DMA((KINDS, N)),
                pltpu.SemaphoreType.DMA((3,)),
                pltpu.SemaphoreType.DMA((3,)),
                pltpu.SemaphoreType.DMA((2, 2, 6)),
                pltpu.SemaphoreType.DMA((2, 2, 6)),
                pltpu.SemaphoreType.DMA((2,)),
                pltpu.SemaphoreType.DMA((2,)),
            ],
            compiler_params=pltpu.CompilerParams(
                collective_id=0, has_side_effects=True, vmem_limit_bytes=60 * 2**20
            ),
        )(layer_input, query_proj, key_proj, value_proj, filter_taps, grad_out)
    )


def solution(mesh):
    placed = (P("chan", "seq"),) * 6
    return jax.shard_map(
        per_device,
        mesh=mesh,
        in_specs=placed,
        out_specs=(P("chan", "seq"),) * 5 + (P("seq", "chan"),),
        check_vma=False,
    )
```

```python
import functools
import math

import jax
import jax.numpy as jnp
from jax import lax
from jax.experimental import pallas as pl
from jax.experimental.pallas import tpu as pltpu
from jax.sharding import PartitionSpec as P

GROUP = 512
F32 = jnp.float32
BF16 = jnp.bfloat16
MESH = pl.DeviceIdType.MESH

N = 32
CH = 32
T = 512
B = 256
NB = N * T // B
PAD = 8
ROWS = N * CH
KINDS = 6
MIXED, UP, TAPS, CONV, BACK, FILT = range(KINDS)


def seq_copy(src, dst, kind, peer, sems, me):
    send, recv = sems
    return pltpu.make_async_remote_copy(
        src_ref=src,
        dst_ref=dst,
        send_sem=send.at[kind, peer],
        recv_sem=recv.at[kind, me],
        device_id={"seq": peer},
        device_id_type=MESH,
    )


def for_peers(me, body):
    def step(i, carry):
        body(lax.rem(me + i, N))
        return carry

    lax.fori_loop(1, N, step, 0)


def loop(n, body, start=0):
    def step(i, carry):
        body(i)
        return carry

    lax.fori_loop(start, n, step, 0)


def kernel(
    x_hbm,
    q_hbm,
    k_hbm,
    v_hbm,
    taps_ref,
    g_hbm,
    mixed_out_hbm,
    grad_query_hbm,
    grad_key_hbm,
    grad_value_hbm,
    filter_grad_ref,
    weight_grad_ref,
    q_ref,
    k_ref,
    v_ref,
    g_ref,
    mixed_out_ref,
    grad_query_ref,
    grad_key_ref,
    grad_value_ref,
    mixed_send,
    up_send,
    taps_send,
    taps_all,
    mixed_all,
    up_all,
    mixed_flip,
    toeplitz,
    acc,
    conv_send,
    back_send,
    conv_all,
    back_all,
    filt_part,
    filt_send,
    filt_all,
    x_all,
    part_a,
    part_b,
    first_in,
    first_out,
    second_in,
    second_out,
    third_in,
    send_sem,
    recv_sem,
    x_send_sem,
    x_recv_sem,
    r_send_sem,
    r_recv_sem,
    z_send_sem,
    z_recv_sem,
    in_sem,
    out_sem,
):
    me = lax.axis_index("seq")
    chan = lax.axis_index("chan")
    ix = me // 8
    iz = lax.rem(me // 4, 2)
    iy = lax.rem(me, 4)
    sems = (send_sem, recv_sem)

    own_x = pl.ds(chan * 8, 8)
    loads = [
        pltpu.make_async_copy(src, dst, in_sem.at[slot])
        for slot, (src, dst) in enumerate(
            (
                (k_hbm, k_ref),
                (v_hbm, v_ref),
                (g_hbm, g_ref),
                (q_hbm, q_ref),
                (x_hbm, x_all.at[own_x]),
            )
        )
    ]
    for load in loads:
        load.start()
    stores = [
        pltpu.make_async_copy(src, dst, out_sem.at[slot])
        for slot, (src, dst) in enumerate(
            (
                (mixed_out_ref, mixed_out_hbm),
                (grad_query_ref, grad_query_hbm),
                (grad_key_ref, grad_key_hbm),
                (grad_value_ref, grad_value_hbm),
            )
        )
    ]

    barrier = pltpu.get_barrier_semaphore()
    for_peers(
        me,
        lambda peer: pl.semaphore_signal(
            barrier, inc=1, device_id={"seq": peer}, device_id_type=MESH
        ),
    )
    core_peer = chan + 1 - 2 * lax.rem(chan, 2)
    near_peer = lax.rem(chan + 2, 4)
    for peer in (core_peer, near_peer):
        pl.semaphore_signal(barrier, inc=1, device_id={"chan": peer}, device_id_type=MESH)

    def make_mixed(r):
        rows = pl.ds(pl.multiple_of(r * 128, 128), 128)
        prod = (k_ref[rows, :].astype(F32) * v_ref[rows, :].astype(F32)).astype(BF16)
        mixed_send[0, rows, :] = prod[:, :B]
        mixed_send[1, rows, :] = prod[:, B:]

    def make_up(r):
        rows = pl.ds(pl.multiple_of(r * 128, 128), 128)
        prod = (g_ref[rows, :].astype(F32) * q_ref[rows, :].astype(F32)).astype(BF16)
        up_send[0, rows, :] = prod[:, :B]
        up_send[1, rows, :] = prod[:, B:]

    for g in range(2):
        for c in range(4):
            taps_send[g, c : c + 1, :] = taps_ref[g : g + 1, c * 128 : (c + 1) * 128]
        taps_send[g, 4:8, :] = jnp.zeros((4, 128), F32)
    loads[0].wait()
    loads[1].wait()
    loop(ROWS // 128, make_mixed)
    pl.semaphore_wait(barrier, N + 1)

    def chan_rows(peer):
        return pl.ds(pl.multiple_of(peer * CH, CH), CH)

    def taps_copy(peer):
        return seq_copy(taps_send.at[peer // 16], taps_all.at[me], TAPS, peer, sems, me)

    def mixed_copy(peer):
        return seq_copy(
            mixed_send.at[:, chan_rows(peer), :],
            mixed_all.at[pl.ds(PAD + 2 * me, 2)],
            MIXED,
            peer,
            sems,
            me,
        )

    def up_copy(peer):
        return seq_copy(
            up_send.at[:, chan_rows(peer), :],
            up_all.at[pl.ds(2 * me, 2)],
            UP,
            peer,
            sems,
            me,
        )

    def conv_copy(peer):
        return seq_copy(
            conv_send.at[pl.ds(2 * peer, 2)],
            conv_all.at[:, chan_rows(me), :],
            CONV,
            peer,
            sems,
            me,
        )

    def back_copy(peer):
        return seq_copy(
            back_send.at[pl.ds(2 * peer, 2)],
            back_all.at[:, chan_rows(me), :],
            BACK,
            peer,
            sems,
            me,
        )

    def filt_copy(peer):
        return seq_copy(filt_send.at[peer], filt_all.at[me], FILT, peer, sems, me)

    def wait_all(kind, dst_of, src_any):
        def one(peer):
            pltpu.make_async_remote_copy(
                src_ref=src_any,
                dst_ref=dst_of(peer),
                send_sem=send_sem.at[kind, peer],
                recv_sem=recv_sem.at[kind, peer],
                device_id={"seq": peer},
                device_id_type=MESH,
            ).wait_recv()

        for_peers(me, one)

    near_x = pl.ds(near_peer * 8, 8)

    def x_copy(slot, src, rows, peer):
        return pltpu.make_async_remote_copy(
            src_ref=src,
            dst_ref=x_all.at[rows],
            send_sem=x_send_sem.at[slot],
            recv_sem=x_recv_sem.at[slot],
            device_id={"chan": peer},
            device_id_type=MESH,
        )

    x_core = x_copy(0, x_hbm, own_x, core_peer)
    x_near = x_copy(1, x_hbm, own_x, near_peer)
    x_pass = x_copy(2, x_all.at[near_x], near_x, core_peer)

    for_peers(me, lambda peer: taps_copy(peer).start())
    for_peers(me, lambda peer: mixed_copy(peer).start())
    x_core.start()
    loads[2].wait()
    loads[3].wait()
    loop(ROWS // 128, make_up)

    taps_all[me] = taps_send[me // 16]
    mixed_all[pl.ds(PAD + 2 * me, 2)] = mixed_send[:, chan_rows(me), :]
    up_all[pl.ds(2 * me, 2)] = up_send[:, chan_rows(me), :]
    mixed_all[:PAD] = jnp.zeros((PAD, CH, B), BF16)
    up_all[NB:] = jnp.zeros((PAD, CH, B), BF16)

    wait_all(TAPS, lambda peer: taps_all.at[peer], taps_send.at[0])
    row_id = lax.broadcasted_iota(jnp.int32, (B, B), 0)
    col_id = lax.broadcasted_iota(jnp.int32, (B, B), 1)

    def sheared(src, half):
        piece = taps_all[src]
        wide = jnp.concatenate(
            [piece[2 * half : 2 * half + 1, :], piece[2 * half + 1 : 2 * half + 2, :]], axis=1
        )
        return pltpu.roll(jnp.broadcast_to(wide, (B, B)), 0, 1, stride=1, stride_axis=0)

    acc[:B] = jnp.zeros((B, B), F32)

    def make_tiles(s):
        for half in range(2):
            now = sheared(s, half)
            toeplitz[2 * s + half] = jnp.where(col_id >= row_id, now, acc[:B]).astype(BF16)
            acc[:B] = now

    loop(N, make_tiles)

    for_peers(me, lambda peer: mixed_copy(peer).wait_send())
    for_peers(me, lambda peer: up_copy(peer).start())
    x_near.start()

    wait_all(MIXED, lambda peer: mixed_all.at[pl.ds(PAD + 2 * peer, 2)], mixed_send.at[:, :CH, :])

    def hand_back(i, copy, send, dest):
        for r in range(8):
            peer = 8 * i + r

            @pl.when(peer != me)
            def _():
                copy(peer).start()

            @pl.when(peer == me)
            def _():
                dest[:, chan_rows(me), :] = send[pl.ds(2 * me, 2)]

    def conv_chunk(step):
        i = lax.rem(ix + step, 4)
        acc[...] = jnp.zeros((2 * B, B), F32)

        def some(j, first, blocks):
            part = None
            for u in range(8):
                m = 8 * j + u
                lhs = mixed_all[pl.ds(PAD + first - m, blocks)].reshape(blocks * CH, B)
                term = jnp.dot(lhs, toeplitz[m], preferred_element_type=F32)
                part = term if part is None else part + term
            return part

        def full(j):
            acc[...] += some(j, 16 * i, 16)

        loop(2 * i + 1, full)
        acc[B:] += some(2 * i + 1, 16 * i + 8, 8)
        conv_send[pl.ds(16 * i, 16)] = acc[...].astype(BF16).reshape(16, CH, B)
        hand_back(i, conv_copy, conv_send, conv_all)

    loop(4, conv_chunk)

    wait_all(UP, lambda peer: up_all.at[pl.ds(2 * peer, 2)], up_send.at[:, :CH, :])

    def back_chunk(step):
        i = lax.rem(ix + step, 4)
        acc[...] = jnp.zeros((2 * B, B), F32)

        def some(j, blocks):
            part = None
            for u in range(8):
                m = 8 * j + u
                lhs = up_all[pl.ds(16 * i + m, blocks)].reshape(blocks * CH, B)
                term = lax.dot_general(
                    lhs, toeplitz[m], (((1,), (1,)), ((), ())), preferred_element_type=F32
                )
                part = term if part is None else part + term
            return part

        def full(j):
            acc[...] += some(j, 16)

        loop(7 - 2 * i, full)
        acc[:B] += some(7 - 2 * i, 8)
        back_send[pl.ds(16 * i, 16)] = acc[...].astype(BF16).reshape(16, CH, B)
        hand_back(i, back_copy, back_send, back_all)

    loop(4, back_chunk)
    x_near.wait_recv()
    x_pass.start()

    wait_all(CONV, lambda peer: conv_all.at[:, chan_rows(peer), :], conv_send.at[:2])

    def use_conv(r):
        rows = pl.ds(pl.multiple_of(r * 128, 128), 128)
        for half in range(2):
            cols = slice(half * B, (half + 1) * B)
            conv = conv_all[half, rows, :].astype(F32)
            grad_query_ref[rows, cols] = (g_ref[rows, cols].astype(F32) * conv).astype(BF16)
            mixed_out_ref[rows, cols] = (q_ref[rows, cols].astype(F32) * conv).astype(BF16)

    loop(ROWS // 128, use_conv)
    stores[0].start()
    stores[1].start()
    loads[4].wait()
    x_core.wait_recv()
    x_pass.wait_recv()

    def share(lhs, half):
        return lax.dot_general(
            lhs,
            grad_query_ref[half * 512 : (half + 1) * 512, :],
            (((1,), (1,)), ((), ())),
            preferred_element_type=F32,
        ).astype(BF16)

    def share_a(px, pz):
        lhs = x_all[pl.ds(8 * px + 4 * pz, 4)].reshape(512, T)
        part_a[px, pz] = share(lhs, 0).reshape(4, 128, 512)

    def share_b(py, pz):
        lhs = jnp.concatenate([x_all[8 * px + 4 * pz + py] for px in range(4)], axis=0)
        part_b[py, pz] = share(lhs, 1).reshape(4, 128, 512)

    def x_peer(d):
        return lax.rem(ix + d, 4) * 8 + iz * 4 + iy

    def y_peer(d):
        return ix * 8 + iz * 4 + lax.rem(iy + d, 4)

    def ring_copy(half, stage, slot, src, dst, peer):
        return pltpu.make_async_remote_copy(
            src_ref=src,
            dst_ref=dst,
            send_sem=r_send_sem.at[half, stage, slot],
            recv_sem=r_recv_sem.at[half, stage, slot],
            device_id={"seq": peer},
            device_id_type=MESH,
        )

    def ring_copies(half, stage, part, inbox, index, peer_of):
        up, down, far = (lax.rem(index + d, 4) for d in (1, 3, 2))
        return (
            ring_copy(half, stage, 0, part.at[far, 0], inbox.at[0], peer_of(1)),
            ring_copy(half, stage, 1, part.at[far, 1], inbox.at[1], peer_of(3)),
            ring_copy(half, stage, 2, part.at[up, 1], inbox.at[2], peer_of(1)),
            ring_copy(half, stage, 3, part.at[down, 0], inbox.at[3], peer_of(3)),
            ring_copy(half, stage, 4, part.at[up, 0], inbox.at[4], peer_of(1)),
            ring_copy(half, stage, 5, part.at[down, 1], inbox.at[5], peer_of(3)),
        )

    def ring_start(copies, first=0, last=4):
        for c in copies[first:last]:
            c.start()

    def ring_middle(copies, part, inbox, index, blocks):
        for slot, there, side in ((0, 1, 0), (1, 3, 1)):
            copies[slot].wait_recv()
            target = lax.rem(index + there, 4)

            def add(e):
                total = part[target, side, e].astype(F32) + inbox[slot, e].astype(F32)
                part[target, side, e] = total.astype(BF16)

            loop(blocks, add)
            copies[4 + slot].start()

    def ring_end(copies, part, inbox, index, blocks, store):
        for slot in (2, 3, 4, 5):
            copies[slot].wait_recv()

        def add(e):
            for side, one, two in ((0, 4, 3), (1, 5, 2)):
                total = part[index, side, e].astype(F32) + (
                    inbox[one, e].astype(F32) + inbox[two, e].astype(F32)
                )
                store(side, e, total)

        loop(blocks, add)

    halves = (
        (part_a, ix, x_peer, iy, y_peer),
        (part_b, iy, y_peer, ix, x_peer),
    )
    firsts = []
    for half, (part, index, peer_of, _, _) in enumerate(halves):
        copies = ring_copies(half, 0, part, first_in.at[half], index, peer_of)
        firsts.append(copies)

    shares = ((share_a, ix), (share_b, iy))
    for half, (make, index) in enumerate(shares):
        loop(2, lambda z: make(lax.rem(index + 2, 4), z))
        ring_start(firsts[half], 0, 2)
    for half, (make, index) in enumerate(shares):
        loop(2, lambda z: make(lax.rem(index + 3 - 2 * z, 4), z))
        ring_start(firsts[half], 2, 4)
    for make, index in shares:
        loop(2, lambda z: make(lax.rem(index + 1 + 2 * z, 4), z))
    for make, index in shares:
        loop(2, lambda z: make(index, z))

    flip = (row_id + col_id == B - 1).astype(BF16)
    for c in range(8):
        piece = mixed_all[PAD + 8 * c : PAD + 8 * c + 8].reshape(B, B)
        mixed_flip[:, c * B : (c + 1) * B] = lax.dot_general(
            flip, piece, (((1,), (1,)), ((), ())), preferred_element_type=F32
        ).astype(BF16)

    def filter_tile(i, m):
        depth = (8 - i) * B
        corr = jnp.dot(
            mixed_flip[:, :depth],
            up_all[pl.ds(m, 8 * (8 - i))].reshape(depth, B),
            preferred_element_type=F32,
        )
        turned = pltpu.roll(corr, 1, 1, stride=1, stride_axis=0)
        above = jnp.where(col_id <= row_id, turned, 0.0)
        below = turned - above
        filt_part[0, m] = jnp.sum(above.reshape(B // 8, 8, B), axis=0)
        filt_part[1, m] = jnp.sum(below.reshape(B // 8, 8, B), axis=0)

    def filter_some(i):
        loop(8, lambda u: filter_tile(i, 8 * i + u))

    for i in range(2):
        filter_some(i)
    for half, (part, index, _, _, _) in enumerate(halves):
        ring_middle(firsts[half], part, first_in.at[half], index, 4)
    for i in range(2, 8):
        filter_some(i)

    filt_part[1, NB] = jnp.zeros((8, B), F32)
    taps_factor = 1.0 / math.sqrt(GROUP * N * T)

    def filter_rows(s):
        for half in range(2):
            m = 2 * s + half
            both = jnp.sum(filt_part[0, m] + filt_part[1, m + 1], axis=0, keepdims=True)
            filt_send[s, 2 * half : 2 * half + 1, :] = both[:, :128] * taps_factor
            filt_send[s, 2 * half + 1 : 2 * half + 2, :] = both[:, 128:] * taps_factor
        filt_send[s, 4:8, :] = jnp.zeros((4, 128), F32)

    loop(N, filter_rows)
    for_peers(me, lambda peer: filt_copy(peer).start())
    filt_all[me] = filt_send[me]

    wait_all(BACK, lambda peer: back_all.at[:, chan_rows(peer), :], back_send.at[:2])

    def use_back(r):
        rows = pl.ds(pl.multiple_of(r * 128, 128), 128)
        for half in range(2):
            cols = slice(half * B, (half + 1) * B)
            back = back_all[half, rows, :].astype(F32)
            grad_key_ref[rows, cols] = (v_ref[rows, cols].astype(F32) * back).astype(BF16)
            grad_value_ref[rows, cols] = (k_ref[rows, cols].astype(F32) * back).astype(BF16)

    loop(ROWS // 128, use_back)
    stores[2].start()
    stores[3].start()

    seconds = []
    for half, (part, index, _, across, across_peer) in enumerate(halves):

        def store(side, e, total):
            first_out[half, e, side, 0] = total.astype(BF16)

        ring_end(firsts[half], part, first_in.at[half], index, 4, store)
        copies = ring_copies(
            half, 1, first_out.at[half], second_in.at[half], across, across_peer
        )
        ring_start(copies)
        seconds.append(copies)
    for half, (_, _, _, across, _) in enumerate(halves):
        ring_middle(seconds[half], first_out.at[half], second_in.at[half], across, 1)

    wait_all(FILT, lambda peer: filt_all.at[peer], filt_send.at[0])
    for g in range(2):
        total = jnp.sum(filt_all[16 * g : 16 * g + 16], axis=0)
        for c in range(4):
            filter_grad_ref[g : g + 1, c * 128 : (c + 1) * 128] = total[c : c + 1, :]

    thirds = []
    other = ix * 8 + (1 - iz) * 4 + iy
    for half, (_, _, _, across, _) in enumerate(halves):

        def keep(side, e, total):
            second_out[half, side] = total.astype(BF16)

        ring_end(seconds[half], first_out.at[half], second_in.at[half], across, 1, keep)
        copy = pltpu.make_async_remote_copy(
            src_ref=second_out.at[half, 1 - iz],
            dst_ref=third_in.at[half],
            send_sem=z_send_sem.at[half],
            recv_sem=z_recv_sem.at[half],
            device_id={"seq": other},
            device_id_type=MESH,
        )
        copy.start()
        thirds.append(copy)
    weight_factor = 1.0 / math.sqrt(N * T)
    for half in range(2):
        thirds[half].wait_recv()
        total = second_out[half, iz].astype(F32) + third_in[half].astype(F32)
        weight_grad_ref[:, half * 512 : (half + 1) * 512] = total * weight_factor

    for store_out in stores:
        store_out.wait()
    for make in (taps_copy, up_copy, conv_copy, back_copy, filt_copy):
        for_peers(me, lambda peer: make(peer).wait_send())
    for c in (x_core, x_near, x_pass, *firsts[0], *firsts[1], *seconds[0], *seconds[1], *thirds):
        c.wait_send()


def hand_over(*refs):
    count = len(refs) // 2
    copies = [
        pltpu.make_async_copy(refs[c], refs[count + c], refs[2 * count].at[c])
        for c in range(count)
    ]
    for c in copies:
        c.start()
    for c in copies:
        c.wait()


def per_device(layer_input, query_proj, key_proj, value_proj, filter_taps, grad_out):
    vmem = pl.BlockSpec(memory_space=pltpu.VMEM)
    hbm = pl.BlockSpec(memory_space=pl.ANY)
    rows = jax.ShapeDtypeStruct((ROWS, T), BF16)
    shapes = (
        rows,
        rows,
        rows,
        rows,
        jax.ShapeDtypeStruct((2, T), F32),
        jax.ShapeDtypeStruct((128, ROWS), F32),
    )
    results = pl.pallas_call(
        kernel,
        out_shape=shapes,
        in_specs=[hbm] * 4 + [vmem, hbm],
        out_specs=[hbm] * 4 + [vmem] * 2,
        scratch_shapes=[pltpu.VMEM((ROWS, T), BF16)] * 8
        + [
            pltpu.VMEM((2, ROWS, B), BF16),
            pltpu.VMEM((2, ROWS, B), BF16),
            pltpu.VMEM((2, 8, 128), F32),
            pltpu.VMEM((N, 8, 128), F32),
            pltpu.VMEM((PAD + NB, CH, B), BF16),
            pltpu.VMEM((NB + PAD, CH, B), BF16),
            pltpu.VMEM((B, NB * CH), BF16),
            pltpu.VMEM((NB, B, B), BF16),
            pltpu.VMEM((2 * B, B), F32),
            pltpu.VMEM((NB, CH, B), BF16),
            pltpu.VMEM((NB, CH, B), BF16),
            pltpu.VMEM((2, ROWS, B), BF16),
            pltpu.VMEM((2, ROWS, B), BF16),
            pltpu.VMEM((2, NB + 1, 8, B), F32),
            pltpu.VMEM((N, 8, 128), F32),
            pltpu.VMEM((N, 8, 128), F32),
            pltpu.VMEM((N, 128, T), BF16),
            pltpu.VMEM((4, 2, 4, 128, 512), BF16),
            pltpu.VMEM((4, 2, 4, 128, 512), BF16),
            pltpu.VMEM((2, 6, 4, 128, 512), BF16),
            pltpu.VMEM((2, 4, 2, 1, 128, 512), BF16),
            pltpu.VMEM((2, 6, 1, 128, 512), BF16),
            pltpu.VMEM((2, 2, 128, 512), BF16),
            pltpu.VMEM((2, 128, 512), BF16),
            pltpu.SemaphoreType.DMA((KINDS, N)),
            pltpu.SemaphoreType.DMA((KINDS, N)),
            pltpu.SemaphoreType.DMA((3,)),
            pltpu.SemaphoreType.DMA((3,)),
            pltpu.SemaphoreType.DMA((2, 2, 6)),
            pltpu.SemaphoreType.DMA((2, 2, 6)),
            pltpu.SemaphoreType.DMA((2,)),
            pltpu.SemaphoreType.DMA((2,)),
            pltpu.SemaphoreType.DMA((5,)),
            pltpu.SemaphoreType.DMA((4,)),
        ],
        compiler_params=pltpu.CompilerParams(
            collective_id=0, has_side_effects=True, vmem_limit_bytes=62 * 2**20
        ),
    )(
        layer_input.reshape(8, 128, T),
        query_proj,
        key_proj,
        value_proj,
        filter_taps,
        grad_out,
    )
    return tuple(
        pl.pallas_call(
            hand_over,
            out_shape=shapes,
            in_specs=[hbm] * 6,
            out_specs=[hbm] * 6,
            scratch_shapes=[pltpu.SemaphoreType.DMA((6,))],
        )(*results)
    )


def solution(mesh):
    placed = (P("chan", "seq"),) * 6
    return jax.shard_map(
        per_device,
        mesh=mesh,
        in_specs=placed,
        out_specs=(P("chan", "seq"),) * 5 + (P("seq", "chan"),),
        check_vma=False,
    )
```

```python
import functools
import math

import jax
import jax.numpy as jnp
from jax import lax
from jax.experimental import pallas as pl
from jax.experimental.pallas import tpu as pltpu
from jax.sharding import PartitionSpec as P

GROUP = 512
F32 = jnp.float32
BF16 = jnp.bfloat16
MESH = pl.DeviceIdType.MESH

N = 32
CH = 32
T = 512
B = 256
NB = N * T // B
PAD = 8
ROWS = N * CH
KINDS = 6
MIXED, UP, TAPS, CONV, BACK, FILT = range(KINDS)


def seq_copy(src, dst, kind, peer, sems, me):
    send, recv = sems
    return pltpu.make_async_remote_copy(
        src_ref=src,
        dst_ref=dst,
        send_sem=send.at[kind, peer],
        recv_sem=recv.at[kind, me],
        device_id={"seq": peer},
        device_id_type=MESH,
    )


def for_peers(me, body):
    def step(i, carry):
        body(lax.rem(me + i, N))
        return carry

    lax.fori_loop(1, N, step, 0)


def loop(n, body, start=0):
    def step(i, carry):
        body(i)
        return carry

    lax.fori_loop(start, n, step, 0)


def kernel(
    x_hbm,
    q_hbm,
    k_hbm,
    v_hbm,
    taps_ref,
    g_hbm,
    mixed_out_hbm,
    grad_query_hbm,
    grad_key_hbm,
    grad_value_hbm,
    filter_grad_ref,
    weight_grad_ref,
    q_ref,
    k_ref,
    v_ref,
    g_ref,
    mixed_out_ref,
    grad_query_ref,
    grad_key_ref,
    grad_value_ref,
    mixed_send,
    up_send,
    taps_send,
    taps_all,
    mixed_all,
    up_all,
    mixed_flip,
    toeplitz,
    acc,
    conv_send,
    back_send,
    conv_all,
    back_all,
    filt_part,
    filt_send,
    filt_all,
    x_all,
    part_a,
    part_b,
    first_in,
    first_out,
    second_in,
    second_out,
    third_in,
    send_sem,
    recv_sem,
    x_send_sem,
    x_recv_sem,
    r_send_sem,
    r_recv_sem,
    z_send_sem,
    z_recv_sem,
    in_sem,
    out_sem,
):
    me = lax.axis_index("seq")
    chan = lax.axis_index("chan")
    ix = me // 8
    iz = lax.rem(me // 4, 2)
    iy = lax.rem(me, 4)
    sems = (send_sem, recv_sem)

    own_x = pl.ds(chan * 8, 8)
    loads = [
        pltpu.make_async_copy(src, dst, in_sem.at[slot])
        for slot, (src, dst) in enumerate(
            (
                (k_hbm, k_ref),
                (v_hbm, v_ref),
                (g_hbm, g_ref),
                (q_hbm, q_ref),
                (x_hbm, x_all.at[own_x]),
            )
        )
    ]
    for load in loads:
        load.start()
    stores = [
        pltpu.make_async_copy(src, dst, out_sem.at[slot])
        for slot, (src, dst) in enumerate(
            (
                (mixed_out_ref, mixed_out_hbm),
                (grad_query_ref, grad_query_hbm),
                (grad_key_ref, grad_key_hbm),
                (grad_value_ref, grad_value_hbm),
            )
        )
    ]

    barrier = pltpu.get_barrier_semaphore()
    for_peers(
        me,
        lambda peer: pl.semaphore_signal(
            barrier, inc=1, device_id={"seq": peer}, device_id_type=MESH
        ),
    )
    core_peer = chan + 1 - 2 * lax.rem(chan, 2)
    near_peer = lax.rem(chan + 2, 4)
    for peer in (core_peer, near_peer):
        pl.semaphore_signal(barrier, inc=1, device_id={"chan": peer}, device_id_type=MESH)

    def make_mixed(r):
        rows = pl.ds(pl.multiple_of(r * 128, 128), 128)
        prod = (k_ref[rows, :].astype(F32) * v_ref[rows, :].astype(F32)).astype(BF16)
        mixed_send[0, rows, :] = prod[:, :B]
        mixed_send[1, rows, :] = prod[:, B:]

    def make_up(r):
        rows = pl.ds(pl.multiple_of(r * 128, 128), 128)
        prod = (g_ref[rows, :].astype(F32) * q_ref[rows, :].astype(F32)).astype(BF16)
        up_send[0, rows, :] = prod[:, :B]
        up_send[1, rows, :] = prod[:, B:]

    for g in range(2):
        for c in range(4):
            taps_send[g, c : c + 1, :] = taps_ref[g : g + 1, c * 128 : (c + 1) * 128]
        taps_send[g, 4:8, :] = jnp.zeros((4, 128), F32)
    loads[0].wait()
    loads[1].wait()
    loop(ROWS // 128, make_mixed)
    pl.semaphore_wait(barrier, N + 1)

    def chan_rows(peer):
        return pl.ds(pl.multiple_of(peer * CH, CH), CH)

    def taps_copy(peer):
        return seq_copy(taps_send.at[peer // 16], taps_all.at[me], TAPS, peer, sems, me)

    def mixed_copy(peer):
        return seq_copy(
            mixed_send.at[:, chan_rows(peer), :],
            mixed_all.at[pl.ds(PAD + 2 * me, 2)],
            MIXED,
            peer,
            sems,
            me,
        )

    def up_copy(peer):
        return seq_copy(
            up_send.at[:, chan_rows(peer), :],
            up_all.at[pl.ds(2 * me, 2)],
            UP,
            peer,
            sems,
            me,
        )

    def conv_copy(peer):
        return seq_copy(
            conv_send.at[pl.ds(2 * peer, 2)],
            conv_all.at[:, chan_rows(me), :],
            CONV,
            peer,
            sems,
            me,
        )

    def back_copy(peer):
        return seq_copy(
            back_send.at[pl.ds(2 * peer, 2)],
            back_all.at[:, chan_rows(me), :],
            BACK,
            peer,
            sems,
            me,
        )

    def filt_copy(peer):
        return seq_copy(filt_send.at[peer], filt_all.at[me], FILT, peer, sems, me)

    def wait_all(kind, dst_of, src_any):
        def one(peer):
            pltpu.make_async_remote_copy(
                src_ref=src_any,
                dst_ref=dst_of(peer),
                send_sem=send_sem.at[kind, peer],
                recv_sem=recv_sem.at[kind, peer],
                device_id={"seq": peer},
                device_id_type=MESH,
            ).wait_recv()

        for_peers(me, one)

    near_x = pl.ds(near_peer * 8, 8)

    def x_copy(slot, src, rows, peer):
        return pltpu.make_async_remote_copy(
            src_ref=src,
            dst_ref=x_all.at[rows],
            send_sem=x_send_sem.at[slot],
            recv_sem=x_recv_sem.at[slot],
            device_id={"chan": peer},
            device_id_type=MESH,
        )

    x_core = x_copy(0, x_hbm, own_x, core_peer)
    x_near = x_copy(1, x_hbm, own_x, near_peer)
    x_pass = x_copy(2, x_all.at[near_x], near_x, core_peer)

    for_peers(me, lambda peer: taps_copy(peer).start())
    for_peers(me, lambda peer: mixed_copy(peer).start())
    x_core.start()
    loads[2].wait()
    loads[3].wait()
    loop(ROWS // 128, make_up)

    taps_all[me] = taps_send[me // 16]
    mixed_all[pl.ds(PAD + 2 * me, 2)] = mixed_send[:, chan_rows(me), :]
    up_all[pl.ds(2 * me, 2)] = up_send[:, chan_rows(me), :]
    mixed_all[:PAD] = jnp.zeros((PAD, CH, B), BF16)
    up_all[NB:] = jnp.zeros((PAD, CH, B), BF16)

    wait_all(TAPS, lambda peer: taps_all.at[peer], taps_send.at[0])
    row_id = lax.broadcasted_iota(jnp.int32, (B, B), 0)
    col_id = lax.broadcasted_iota(jnp.int32, (B, B), 1)

    def sheared(src, half):
        piece = taps_all[src]
        wide = jnp.concatenate(
            [piece[2 * half : 2 * half + 1, :], piece[2 * half + 1 : 2 * half + 2, :]], axis=1
        )
        return pltpu.roll(jnp.broadcast_to(wide, (B, B)), 0, 1, stride=1, stride_axis=0)

    acc[:B] = jnp.zeros((B, B), F32)

    def make_tiles(s):
        for half in range(2):
            now = sheared(s, half)
            toeplitz[2 * s + half] = jnp.where(col_id >= row_id, now, acc[:B]).astype(BF16)
            acc[:B] = now

    loop(N, make_tiles)

    for_peers(me, lambda peer: mixed_copy(peer).wait_send())
    for_peers(me, lambda peer: up_copy(peer).start())
    x_near.start()

    wait_all(MIXED, lambda peer: mixed_all.at[pl.ds(PAD + 2 * peer, 2)], mixed_send.at[:, :CH, :])

    def hand_back(i, copy, send, dest):
        for r in range(8):
            peer = 8 * i + r

            @pl.when(peer != me)
            def _():
                copy(peer).start()

            @pl.when(peer == me)
            def _():
                dest[:, chan_rows(me), :] = send[pl.ds(2 * me, 2)]

    def conv_chunk(step):
        i = lax.rem(ix + step, 4)
        acc[...] = jnp.zeros((2 * B, B), F32)

        def some(j, first, blocks):
            part = None
            for u in range(8):
                m = 8 * j + u
                lhs = mixed_all[pl.ds(PAD + first - m, blocks)].reshape(blocks * CH, B)
                term = jnp.dot(lhs, toeplitz[m], preferred_element_type=F32)
                part = term if part is None else part + term
            return part

        def full(j):
            acc[...] += some(j, 16 * i, 16)

        loop(2 * i + 1, full)
        acc[B:] += some(2 * i + 1, 16 * i + 8, 8)
        conv_send[pl.ds(16 * i, 16)] = acc[...].astype(BF16).reshape(16, CH, B)
        hand_back(i, conv_copy, conv_send, conv_all)

    loop(4, conv_chunk)

    wait_all(UP, lambda peer: up_all.at[pl.ds(2 * peer, 2)], up_send.at[:, :CH, :])

    def back_chunk(step):
        i = lax.rem(ix + step, 4)
        acc[...] = jnp.zeros((2 * B, B), F32)

        def some(j, blocks):
            part = None
            for u in range(8):
                m = 8 * j + u
                lhs = up_all[pl.ds(16 * i + m, blocks)].reshape(blocks * CH, B)
                term = lax.dot_general(
                    lhs, toeplitz[m], (((1,), (1,)), ((), ())), preferred_element_type=F32
                )
                part = term if part is None else part + term
            return part

        def full(j):
            acc[...] += some(j, 16)

        loop(7 - 2 * i, full)
        acc[:B] += some(7 - 2 * i, 8)
        back_send[pl.ds(16 * i, 16)] = acc[...].astype(BF16).reshape(16, CH, B)
        hand_back(i, back_copy, back_send, back_all)

    loop(4, back_chunk)
    x_near.wait_recv()
    x_pass.start()

    wait_all(CONV, lambda peer: conv_all.at[:, chan_rows(peer), :], conv_send.at[:2])

    def use_conv(r):
        rows = pl.ds(pl.multiple_of(r * 128, 128), 128)
        for half in range(2):
            cols = slice(half * B, (half + 1) * B)
            conv = conv_all[half, rows, :].astype(F32)
            grad_query_ref[rows, cols] = (g_ref[rows, cols].astype(F32) * conv).astype(BF16)
            mixed_out_ref[rows, cols] = (q_ref[rows, cols].astype(F32) * conv).astype(BF16)

    loop(ROWS // 128, use_conv)
    stores[0].start()
    stores[1].start()
    loads[4].wait()
    x_core.wait_recv()
    x_pass.wait_recv()

    def share(lhs, half):
        return lax.dot_general(
            lhs,
            grad_query_ref[half * 512 : (half + 1) * 512, :],
            (((1,), (1,)), ((), ())),
            preferred_element_type=F32,
        ).astype(BF16)

    def share_a(px, pz):
        lhs = x_all[pl.ds(8 * px + 4 * pz, 4)].reshape(512, T)
        part_a[px, pz] = share(lhs, 0).reshape(4, 128, 512)

    def share_b(py, pz):
        lhs = jnp.concatenate([x_all[8 * px + 4 * pz + py] for px in range(4)], axis=0)
        part_b[py, pz] = share(lhs, 1).reshape(4, 128, 512)

    def x_peer(d):
        return lax.rem(ix + d, 4) * 8 + iz * 4 + iy

    def y_peer(d):
        return ix * 8 + iz * 4 + lax.rem(iy + d, 4)

    def ring_copy(half, stage, slot, src, dst, peer):
        return pltpu.make_async_remote_copy(
            src_ref=src,
            dst_ref=dst,
            send_sem=r_send_sem.at[half, stage, slot],
            recv_sem=r_recv_sem.at[half, stage, slot],
            device_id={"seq": peer},
            device_id_type=MESH,
        )

    def ring_copies(half, stage, part, inbox, index, peer_of):
        up, down, far = (lax.rem(index + d, 4) for d in (1, 3, 2))
        return (
            ring_copy(half, stage, 0, part.at[far, 0], inbox.at[0], peer_of(1)),
            ring_copy(half, stage, 1, part.at[far, 1], inbox.at[1], peer_of(3)),
            ring_copy(half, stage, 2, part.at[up, 1], inbox.at[2], peer_of(1)),
            ring_copy(half, stage, 3, part.at[down, 0], inbox.at[3], peer_of(3)),
            ring_copy(half, stage, 4, part.at[up, 0], inbox.at[4], peer_of(1)),
            ring_copy(half, stage, 5, part.at[down, 1], inbox.at[5], peer_of(3)),
        )

    def ring_start(copies, first=0, last=4):
        for c in copies[first:last]:
            c.start()

    def ring_middle(copies, part, inbox, index, blocks):
        for slot, there, side in ((0, 1, 0), (1, 3, 1)):
            copies[slot].wait_recv()
            target = lax.rem(index + there, 4)

            def add(e):
                total = part[target, side, e].astype(F32) + inbox[slot, e].astype(F32)
                part[target, side, e] = total.astype(BF16)

            loop(blocks, add)
            copies[4 + slot].start()

    def ring_end(copies, part, inbox, index, blocks, store):
        for slot in (2, 3, 4, 5):
            copies[slot].wait_recv()

        def add(e):
            for side, one, two in ((0, 4, 3), (1, 5, 2)):
                total = part[index, side, e].astype(F32) + (
                    inbox[one, e].astype(F32) + inbox[two, e].astype(F32)
                )
                store(side, e, total)

        loop(blocks, add)

    halves = (
        (part_a, ix, x_peer, iy, y_peer),
        (part_b, iy, y_peer, ix, x_peer),
    )
    firsts = []
    for half, (part, index, peer_of, _, _) in enumerate(halves):
        copies = ring_copies(half, 0, part, first_in.at[half], index, peer_of)
        firsts.append(copies)

    shares = ((share_a, ix), (share_b, iy))
    for half, (make, index) in enumerate(shares):
        loop(2, lambda z: make(lax.rem(index + 2, 4), z))
        ring_start(firsts[half], 0, 2)
    for half, (make, index) in enumerate(shares):
        loop(2, lambda z: make(lax.rem(index + 3 - 2 * z, 4), z))
        ring_start(firsts[half], 2, 4)
    for make, index in shares:
        loop(2, lambda z: make(lax.rem(index + 1 + 2 * z, 4), z))
    for make, index in shares:
        loop(2, lambda z: make(index, z))

    flip = (row_id + col_id == B - 1).astype(BF16)
    for c in range(8):
        piece = mixed_all[PAD + 8 * c : PAD + 8 * c + 8].reshape(B, B)
        mixed_flip[:, c * B : (c + 1) * B] = lax.dot_general(
            flip, piece, (((1,), (1,)), ((), ())), preferred_element_type=F32
        ).astype(BF16)

    def filter_tile(i, m):
        depth = (8 - i) * B
        corr = jnp.dot(
            mixed_flip[:, :depth],
            up_all[pl.ds(m, 8 * (8 - i))].reshape(depth, B),
            preferred_element_type=F32,
        )
        turned = pltpu.roll(corr, 1, 1, stride=1, stride_axis=0)
        above = jnp.where(col_id <= row_id, turned, 0.0)
        below = turned - above
        filt_part[0, m] = jnp.sum(above.reshape(B // 8, 8, B), axis=0)
        filt_part[1, m] = jnp.sum(below.reshape(B // 8, 8, B), axis=0)

    def filter_some(i):
        loop(8, lambda u: filter_tile(i, 8 * i + u))

    for i in range(2):
        filter_some(i)
    for half, (part, index, _, _, _) in enumerate(halves):
        ring_middle(firsts[half], part, first_in.at[half], index, 4)
    for i in range(2, 8):
        filter_some(i)

    filt_part[1, NB] = jnp.zeros((8, B), F32)
    taps_factor = 1.0 / math.sqrt(GROUP * N * T)

    def filter_rows(s):
        for half in range(2):
            m = 2 * s + half
            both = jnp.sum(filt_part[0, m] + filt_part[1, m + 1], axis=0, keepdims=True)
            filt_send[s, 2 * half : 2 * half + 1, :] = both[:, :128] * taps_factor
            filt_send[s, 2 * half + 1 : 2 * half + 2, :] = both[:, 128:] * taps_factor
        filt_send[s, 4:8, :] = jnp.zeros((4, 128), F32)

    loop(N, filter_rows)
    for_peers(me, lambda peer: filt_copy(peer).start())
    filt_all[me] = filt_send[me]

    wait_all(BACK, lambda peer: back_all.at[:, chan_rows(peer), :], back_send.at[:2])

    def use_back(r):
        rows = pl.ds(pl.multiple_of(r * 128, 128), 128)
        for half in range(2):
            cols = slice(half * B, (half + 1) * B)
            back = back_all[half, rows, :].astype(F32)
            grad_key_ref[rows, cols] = (v_ref[rows, cols].astype(F32) * back).astype(BF16)
            grad_value_ref[rows, cols] = (k_ref[rows, cols].astype(F32) * back).astype(BF16)

    loop(ROWS // 128, use_back)
    stores[2].start()
    stores[3].start()

    seconds = []
    for half, (part, index, _, across, across_peer) in enumerate(halves):

        def store(side, e, total):
            first_out[half, e, side, 0] = total.astype(BF16)

        ring_end(firsts[half], part, first_in.at[half], index, 4, store)
        copies = ring_copies(
            half, 1, first_out.at[half], second_in.at[half], across, across_peer
        )
        ring_start(copies)
        seconds.append(copies)
    for half, (_, _, _, across, _) in enumerate(halves):
        ring_middle(seconds[half], first_out.at[half], second_in.at[half], across, 1)

    wait_all(FILT, lambda peer: filt_all.at[peer], filt_send.at[0])
    for g in range(2):
        total = jnp.sum(filt_all[16 * g : 16 * g + 16], axis=0)
        for c in range(4):
            filter_grad_ref[g : g + 1, c * 128 : (c + 1) * 128] = total[c : c + 1, :]

    thirds = []
    other = ix * 8 + (1 - iz) * 4 + iy
    for half, (_, _, _, across, _) in enumerate(halves):

        def keep(side, e, total):
            second_out[half, side] = total.astype(BF16)

        ring_end(seconds[half], first_out.at[half], second_in.at[half], across, 1, keep)
        copy = pltpu.make_async_remote_copy(
            src_ref=second_out.at[half, 1 - iz],
            dst_ref=third_in.at[half],
            send_sem=z_send_sem.at[half],
            recv_sem=z_recv_sem.at[half],
            device_id={"seq": other},
            device_id_type=MESH,
        )
        copy.start()
        thirds.append(copy)
    weight_factor = 1.0 / math.sqrt(N * T)
    for half in range(2):
        thirds[half].wait_recv()
        total = second_out[half, iz].astype(F32) + third_in[half].astype(F32)
        weight_grad_ref[:, half * 512 : (half + 1) * 512] = total * weight_factor

    for store_out in stores:
        store_out.wait()
    for make in (taps_copy, up_copy, conv_copy, back_copy, filt_copy):
        for_peers(me, lambda peer: make(peer).wait_send())
    for c in (x_core, x_near, x_pass, *firsts[0], *firsts[1], *seconds[0], *seconds[1], *thirds):
        c.wait_send()


def hand_over(*refs):
    count = len(refs) // 3
    sources, targets, held = refs[:count], refs[count : 2 * count], refs[2 * count : 3 * count]
    sems = refs[3 * count]
    loads = [pltpu.make_async_copy(sources[c], held[c], sems.at[0, c]) for c in range(count)]
    stores = [pltpu.make_async_copy(held[c], targets[c], sems.at[1, c]) for c in range(count)]
    for load in loads:
        load.start()
    for load, store in zip(loads, stores):
        load.wait()
        store.start()
    for store in stores:
        store.wait()


def per_device(layer_input, query_proj, key_proj, value_proj, filter_taps, grad_out):
    vmem = pl.BlockSpec(memory_space=pltpu.VMEM)
    hbm = pl.BlockSpec(memory_space=pl.ANY)
    rows = jax.ShapeDtypeStruct((ROWS, T), BF16)
    shapes = (
        rows,
        rows,
        rows,
        rows,
        jax.ShapeDtypeStruct((2, T), F32),
        jax.ShapeDtypeStruct((128, ROWS), F32),
    )
    results = pl.pallas_call(
        kernel,
        out_shape=shapes,
        in_specs=[hbm] * 4 + [vmem, hbm],
        out_specs=[hbm] * 4 + [vmem] * 2,
        scratch_shapes=[pltpu.VMEM((ROWS, T), BF16)] * 8
        + [
            pltpu.VMEM((2, ROWS, B), BF16),
            pltpu.VMEM((2, ROWS, B), BF16),
            pltpu.VMEM((2, 8, 128), F32),
            pltpu.VMEM((N, 8, 128), F32),
            pltpu.VMEM((PAD + NB, CH, B), BF16),
            pltpu.VMEM((NB + PAD, CH, B), BF16),
            pltpu.VMEM((B, NB * CH), BF16),
            pltpu.VMEM((NB, B, B), BF16),
            pltpu.VMEM((2 * B, B), F32),
            pltpu.VMEM((NB, CH, B), BF16),
            pltpu.VMEM((NB, CH, B), BF16),
            pltpu.VMEM((2, ROWS, B), BF16),
            pltpu.VMEM((2, ROWS, B), BF16),
            pltpu.VMEM((2, NB + 1, 8, B), F32),
            pltpu.VMEM((N, 8, 128), F32),
            pltpu.VMEM((N, 8, 128), F32),
            pltpu.VMEM((N, 128, T), BF16),
            pltpu.VMEM((4, 2, 4, 128, 512), BF16),
            pltpu.VMEM((4, 2, 4, 128, 512), BF16),
            pltpu.VMEM((2, 6, 4, 128, 512), BF16),
            pltpu.VMEM((2, 4, 2, 1, 128, 512), BF16),
            pltpu.VMEM((2, 6, 1, 128, 512), BF16),
            pltpu.VMEM((2, 2, 128, 512), BF16),
            pltpu.VMEM((2, 128, 512), BF16),
            pltpu.SemaphoreType.DMA((KINDS, N)),
            pltpu.SemaphoreType.DMA((KINDS, N)),
            pltpu.SemaphoreType.DMA((3,)),
            pltpu.SemaphoreType.DMA((3,)),
            pltpu.SemaphoreType.DMA((2, 2, 6)),
            pltpu.SemaphoreType.DMA((2, 2, 6)),
            pltpu.SemaphoreType.DMA((2,)),
            pltpu.SemaphoreType.DMA((2,)),
            pltpu.SemaphoreType.DMA((5,)),
            pltpu.SemaphoreType.DMA((4,)),
        ],
        compiler_params=pltpu.CompilerParams(
            collective_id=0, has_side_effects=True, vmem_limit_bytes=62 * 2**20
        ),
    )(
        layer_input.reshape(8, 128, T),
        query_proj,
        key_proj,
        value_proj,
        filter_taps,
        grad_out,
    )
    return tuple(
        pl.pallas_call(
            hand_over,
            out_shape=shapes,
            in_specs=[hbm] * 6,
            out_specs=[hbm] * 6,
            scratch_shapes=[pltpu.VMEM(shape.shape, shape.dtype) for shape in shapes]
            + [pltpu.SemaphoreType.DMA((2, 6))],
        )(*results)
    )


def solution(mesh):
    placed = (P("chan", "seq"),) * 6
    return jax.shard_map(
        per_device,
        mesh=mesh,
        in_specs=placed,
        out_specs=(P("chan", "seq"),) * 5 + (P("seq", "chan"),),
        check_vma=False,
    )
```

```python
import functools
import math

import jax
import jax.numpy as jnp
from jax import lax
from jax.experimental import pallas as pl
from jax.experimental.pallas import tpu as pltpu
from jax.sharding import PartitionSpec as P

GROUP = 512
F32 = jnp.float32
BF16 = jnp.bfloat16
MESH = pl.DeviceIdType.MESH

N = 32
CH = 32
T = 512
B = 256
NB = N * T // B
PAD = 8
ROWS = N * CH
WA = 384
WB = ROWS - WA
KINDS = 6
MIXED, UP, TAPS, CONV, BACK, FILT = range(KINDS)


def seq_copy(src, dst, kind, peer, sems, me):
    send, recv = sems
    return pltpu.make_async_remote_copy(
        src_ref=src,
        dst_ref=dst,
        send_sem=send.at[kind, peer],
        recv_sem=recv.at[kind, me],
        device_id={"seq": peer},
        device_id_type=MESH,
    )


def for_peers(me, body):
    def step(i, carry):
        body(lax.rem(me + i, N))
        return carry

    lax.fori_loop(1, N, step, 0)


def loop(n, body, start=0):
    def step(i, carry):
        body(i)
        return carry

    lax.fori_loop(start, n, step, 0)


def kernel(
    x_hbm,
    q_hbm,
    k_hbm,
    v_hbm,
    taps_ref,
    g_hbm,
    mixed_out_hbm,
    grad_query_hbm,
    grad_key_hbm,
    grad_value_hbm,
    filter_grad_ref,
    weight_grad_ref,
    q_ref,
    k_ref,
    v_ref,
    g_ref,
    mixed_out_ref,
    grad_query_ref,
    grad_key_ref,
    grad_value_ref,
    mixed_send,
    up_send,
    taps_send,
    taps_all,
    mixed_all,
    up_all,
    mixed_flip,
    toeplitz,
    acc,
    conv_send,
    back_send,
    conv_all,
    back_all,
    filt_part,
    filt_send,
    filt_all,
    x_all,
    part_a,
    part_b,
    first_in_a,
    first_in_b,
    first_out_a,
    first_out_b,
    second_in_a,
    second_in_b,
    second_out_a,
    second_out_b,
    third_in_a,
    third_in_b,
    send_sem,
    recv_sem,
    x_send_sem,
    x_recv_sem,
    r_send_sem,
    r_recv_sem,
    z_send_sem,
    z_recv_sem,
    in_sem,
    out_sem,
):
    me = lax.axis_index("seq")
    chan = lax.axis_index("chan")
    ix = me // 8
    iz = lax.rem(me // 4, 2)
    iy = lax.rem(me, 4)
    sems = (send_sem, recv_sem)

    own_x = pl.ds(chan * 8, 8)
    loads = [
        pltpu.make_async_copy(src, dst, in_sem.at[slot])
        for slot, (src, dst) in enumerate(
            (
                (k_hbm, k_ref),
                (v_hbm, v_ref),
                (g_hbm, g_ref),
                (q_hbm, q_ref),
                (x_hbm, x_all.at[own_x]),
            )
        )
    ]
    for load in loads:
        load.start()
    stores = [
        pltpu.make_async_copy(src, dst, out_sem.at[slot])
        for slot, (src, dst) in enumerate(
            (
                (mixed_out_ref, mixed_out_hbm),
                (grad_query_ref, grad_query_hbm),
                (grad_key_ref, grad_key_hbm),
                (grad_value_ref, grad_value_hbm),
            )
        )
    ]

    barrier = pltpu.get_barrier_semaphore()
    for_peers(
        me,
        lambda peer: pl.semaphore_signal(
            barrier, inc=1, device_id={"seq": peer}, device_id_type=MESH
        ),
    )
    core_peer = chan + 1 - 2 * lax.rem(chan, 2)
    near_peer = lax.rem(chan + 2, 4)
    for peer in (core_peer, near_peer):
        pl.semaphore_signal(barrier, inc=1, device_id={"chan": peer}, device_id_type=MESH)

    def make_mixed(r):
        rows = pl.ds(pl.multiple_of(r * 128, 128), 128)
        prod = (k_ref[rows, :].astype(F32) * v_ref[rows, :].astype(F32)).astype(BF16)
        mixed_send[0, rows, :] = prod[:, :B]
        mixed_send[1, rows, :] = prod[:, B:]

    def make_up(r):
        rows = pl.ds(pl.multiple_of(r * 128, 128), 128)
        prod = (g_ref[rows, :].astype(F32) * q_ref[rows, :].astype(F32)).astype(BF16)
        up_send[0, rows, :] = prod[:, :B]
        up_send[1, rows, :] = prod[:, B:]

    for g in range(2):
        for c in range(4):
            taps_send[g, c : c + 1, :] = taps_ref[g : g + 1, c * 128 : (c + 1) * 128]
        taps_send[g, 4:8, :] = jnp.zeros((4, 128), F32)
    loads[0].wait()
    loads[1].wait()
    loop(ROWS // 128, make_mixed)
    pl.semaphore_wait(barrier, N + 1)

    def chan_rows(peer):
        return pl.ds(pl.multiple_of(peer * CH, CH), CH)

    def taps_copy(peer):
        return seq_copy(taps_send.at[peer // 16], taps_all.at[me], TAPS, peer, sems, me)

    def mixed_copy(peer):
        return seq_copy(
            mixed_send.at[:, chan_rows(peer), :],
            mixed_all.at[pl.ds(PAD + 2 * me, 2)],
            MIXED,
            peer,
            sems,
            me,
        )

    def up_copy(peer):
        return seq_copy(
            up_send.at[:, chan_rows(peer), :],
            up_all.at[pl.ds(2 * me, 2)],
            UP,
            peer,
            sems,
            me,
        )

    def conv_copy(peer):
        return seq_copy(
            conv_send.at[pl.ds(2 * peer, 2)],
            conv_all.at[:, chan_rows(me), :],
            CONV,
            peer,
            sems,
            me,
        )

    def back_copy(peer):
        return seq_copy(
            back_send.at[pl.ds(2 * peer, 2)],
            back_all.at[:, chan_rows(me), :],
            BACK,
            peer,
            sems,
            me,
        )

    def filt_copy(peer):
        return seq_copy(filt_send.at[peer], filt_all.at[me], FILT, peer, sems, me)

    def wait_all(kind, dst_of, src_any):
        def one(peer):
            pltpu.make_async_remote_copy(
                src_ref=src_any,
                dst_ref=dst_of(peer),
                send_sem=send_sem.at[kind, peer],
                recv_sem=recv_sem.at[kind, peer],
                device_id={"seq": peer},
                device_id_type=MESH,
            ).wait_recv()

        for_peers(me, one)

    near_x = pl.ds(near_peer * 8, 8)

    def x_copy(slot, src, rows, peer):
        return pltpu.make_async_remote_copy(
            src_ref=src,
            dst_ref=x_all.at[rows],
            send_sem=x_send_sem.at[slot],
            recv_sem=x_recv_sem.at[slot],
            device_id={"chan": peer},
            device_id_type=MESH,
        )

    x_core = x_copy(0, x_hbm, own_x, core_peer)
    x_near = x_copy(1, x_hbm, own_x, near_peer)
    x_pass = x_copy(2, x_all.at[near_x], near_x, core_peer)

    for_peers(me, lambda peer: taps_copy(peer).start())
    for_peers(me, lambda peer: mixed_copy(peer).start())
    x_core.start()
    loads[2].wait()
    loads[3].wait()
    loop(ROWS // 128, make_up)

    taps_all[me] = taps_send[me // 16]
    mixed_all[pl.ds(PAD + 2 * me, 2)] = mixed_send[:, chan_rows(me), :]
    up_all[pl.ds(2 * me, 2)] = up_send[:, chan_rows(me), :]
    mixed_all[:PAD] = jnp.zeros((PAD, CH, B), BF16)
    up_all[NB:] = jnp.zeros((PAD, CH, B), BF16)

    wait_all(TAPS, lambda peer: taps_all.at[peer], taps_send.at[0])
    row_id = lax.broadcasted_iota(jnp.int32, (B, B), 0)
    col_id = lax.broadcasted_iota(jnp.int32, (B, B), 1)

    def sheared(src, half):
        piece = taps_all[src]
        wide = jnp.concatenate(
            [piece[2 * half : 2 * half + 1, :], piece[2 * half + 1 : 2 * half + 2, :]], axis=1
        )
        return pltpu.roll(jnp.broadcast_to(wide, (B, B)), 0, 1, stride=1, stride_axis=0)

    acc[:B] = jnp.zeros((B, B), F32)

    def make_tiles(s):
        for half in range(2):
            now = sheared(s, half)
            toeplitz[2 * s + half] = jnp.where(col_id >= row_id, now, acc[:B]).astype(BF16)
            acc[:B] = now

    loop(N, make_tiles)

    for_peers(me, lambda peer: mixed_copy(peer).wait_send())
    for_peers(me, lambda peer: up_copy(peer).start())

    wait_all(MIXED, lambda peer: mixed_all.at[pl.ds(PAD + 2 * peer, 2)], mixed_send.at[:, :CH, :])

    def hand_back(i, copy, send, dest):
        for r in range(8):
            peer = 8 * i + r

            @pl.when(peer != me)
            def _():
                copy(peer).start()

            @pl.when(peer == me)
            def _():
                dest[:, chan_rows(me), :] = send[pl.ds(2 * me, 2)]

    def conv_chunk(step):
        i = lax.rem(ix + step, 4)
        acc[...] = jnp.zeros((2 * B, B), F32)

        def some(j, first, blocks):
            part = None
            for u in range(8):
                m = 8 * j + u
                lhs = mixed_all[pl.ds(PAD + first - m, blocks)].reshape(blocks * CH, B)
                term = jnp.dot(lhs, toeplitz[m], preferred_element_type=F32)
                part = term if part is None else part + term
            return part

        def full(j):
            acc[...] += some(j, 16 * i, 16)

        loop(2 * i + 1, full)
        acc[B:] += some(2 * i + 1, 16 * i + 8, 8)
        conv_send[pl.ds(16 * i, 16)] = acc[...].astype(BF16).reshape(16, CH, B)
        hand_back(i, conv_copy, conv_send, conv_all)

    loop(4, conv_chunk)
    x_near.start()

    wait_all(UP, lambda peer: up_all.at[pl.ds(2 * peer, 2)], up_send.at[:, :CH, :])

    def back_chunk(step):
        i = lax.rem(ix + step, 4)
        acc[...] = jnp.zeros((2 * B, B), F32)

        def some(j, blocks):
            part = None
            for u in range(8):
                m = 8 * j + u
                lhs = up_all[pl.ds(16 * i + m, blocks)].reshape(blocks * CH, B)
                term = lax.dot_general(
                    lhs, toeplitz[m], (((1,), (1,)), ((), ())), preferred_element_type=F32
                )
                part = term if part is None else part + term
            return part

        def full(j):
            acc[...] += some(j, 16)

        loop(7 - 2 * i, full)
        acc[:B] += some(7 - 2 * i, 8)
        back_send[pl.ds(16 * i, 16)] = acc[...].astype(BF16).reshape(16, CH, B)

    loop(4, back_chunk)

    wait_all(CONV, lambda peer: conv_all.at[:, chan_rows(peer), :], conv_send.at[:2])

    def use_conv(r):
        rows = pl.ds(pl.multiple_of(r * 128, 128), 128)
        for half in range(2):
            cols = slice(half * B, (half + 1) * B)
            conv = conv_all[half, rows, :].astype(F32)
            grad_query_ref[rows, cols] = (g_ref[rows, cols].astype(F32) * conv).astype(BF16)
            mixed_out_ref[rows, cols] = (q_ref[rows, cols].astype(F32) * conv).astype(BF16)

    loop(ROWS // 128, use_conv)
    stores[0].start()
    stores[1].start()
    loads[4].wait()
    x_core.wait_recv()

    def share(lhs, first, count):
        return lax.dot_general(
            lhs,
            grad_query_ref[first : first + count, :],
            (((1,), (1,)), ((), ())),
            preferred_element_type=F32,
        ).astype(BF16)

    def share_a(px, pz):
        lhs = x_all[pl.ds(8 * px + 4 * pz, 4)].reshape(512, T)
        part_a[px, pz] = share(lhs, 0, WA).reshape(4, 128, WA)

    def share_b(py, pz, pair):
        lhs = jnp.concatenate([x_all[16 * pair + 8 * e + 4 * pz + py] for e in range(2)], axis=0)
        part_b[py, pz, pl.ds(2 * pair, 2)] = share(lhs, WA, WB).reshape(2, 128, WB)

    def x_peer(d):
        return lax.rem(ix + d, 4) * 8 + iz * 4 + iy

    def y_peer(d):
        return ix * 8 + iz * 4 + lax.rem(iy + d, 4)

    def ring_copies(bank, view, inbox, index, peer_of):
        up, down, far = (lax.rem(index + d, 4) for d in (1, 3, 2))

        def ring_copy(slot, target, side, hop):
            return pltpu.make_async_remote_copy(
                src_ref=view(target, side),
                dst_ref=inbox.at[slot],
                send_sem=r_send_sem.at[bank, slot],
                recv_sem=r_recv_sem.at[bank, slot],
                device_id={"seq": peer_of(hop)},
                device_id_type=MESH,
            )

        return (
            ring_copy(0, far, 0, 1),
            ring_copy(1, far, 1, 3),
            ring_copy(2, up, 1, 1),
            ring_copy(3, down, 0, 3),
            ring_copy(4, up, 0, 1),
            ring_copy(5, down, 1, 3),
        )

    def ring_start(copies, first=0, last=4):
        for c in copies[first:last]:
            c.start()

    def ring_middle(copies, view, inbox, index, blocks):
        for slot, there, side in ((0, 1, 0), (1, 3, 1)):
            copies[slot].wait_recv()
            held = view(lax.rem(index + there, 4), side)

            def add(e):
                total = held[e].astype(F32) + inbox[slot, e].astype(F32)
                held[e] = total.astype(BF16)

            loop(blocks, add)
            copies[4 + slot].start()

    def ring_end(copies, view, inbox, index, blocks, store):
        for slot in (2, 3, 4, 5):
            copies[slot].wait_recv()

        def add(e):
            for side, one, two in ((0, 4, 3), (1, 5, 2)):
                total = view(index, side)[e].astype(F32) + (
                    inbox[one, e].astype(F32) + inbox[two, e].astype(F32)
                )
                store(side, e, total)

        loop(blocks, add)

    def view_a(target, side):
        return part_a.at[target, side]

    def view_b(pair):
        return lambda target, side: part_b.at[target, side, pl.ds(2 * pair, 2)]

    here = chan // 2
    there = 1 - here
    ring_a = (view_a, first_in_a, ix)
    ring_b0 = (view_b(here), first_in_b.at[0], iy)
    ring_b1 = (view_b(there), first_in_b.at[1], iy)
    copies_a = ring_copies(0, *ring_a, x_peer)
    copies_b0 = ring_copies(1, *ring_b0, y_peer)
    copies_b1 = ring_copies(2, *ring_b1, y_peer)

    def shares_b(copies, pair):
        loop(2, lambda z: share_b(lax.rem(iy + 2, 4), z, pair))
        ring_start(copies, 0, 2)
        loop(2, lambda z: share_b(lax.rem(iy + 3 - 2 * z, 4), z, pair))
        ring_start(copies, 2, 4)
        loop(2, lambda z: share_b(lax.rem(iy + 1 + 2 * z, 4), z, pair))

    shares_b(copies_b0, here)
    loop(2, lambda z: share_b(iy, z, here))

    flip = (row_id + col_id == B - 1).astype(BF16)
    for c in range(8):
        piece = mixed_all[PAD + 8 * c : PAD + 8 * c + 8].reshape(B, B)
        mixed_flip[:, c * B : (c + 1) * B] = lax.dot_general(
            flip, piece, (((1,), (1,)), ((), ())), preferred_element_type=F32
        ).astype(BF16)

    def filter_tile(i, m):
        depth = (8 - i) * B
        corr = jnp.dot(
            mixed_flip[:, :depth],
            up_all[pl.ds(m, 8 * (8 - i))].reshape(depth, B),
            preferred_element_type=F32,
        )
        turned = pltpu.roll(corr, 1, 1, stride=1, stride_axis=0)
        above = jnp.where(col_id <= row_id, turned, 0.0)
        below = turned - above
        filt_part[0, m] = jnp.sum(above.reshape(B // 8, 8, B), axis=0)
        filt_part[1, m] = jnp.sum(below.reshape(B // 8, 8, B), axis=0)

    def filter_some(i):
        loop(8, lambda u: filter_tile(i, 8 * i + u))

    filter_some(0)
    ring_middle(copies_b0, *ring_b0, 2)

    x_near.wait_recv()
    x_pass.start()
    filter_some(7)
    filter_some(6)
    x_pass.wait_recv()
    loop(2, lambda z: share_a(lax.rem(ix + 2, 4), z))
    ring_start(copies_a, 0, 2)
    loop(2, lambda z: share_a(lax.rem(ix + 3 - 2 * z, 4), z))
    ring_start(copies_a, 2, 4)
    loop(2, lambda z: share_a(lax.rem(ix + 1 + 2 * z, 4), z))
    shares_b(copies_b1, there)
    for_peers(me, lambda peer: back_copy(peer).start())
    back_all[:, chan_rows(me), :] = back_send[pl.ds(2 * me, 2)]
    loop(2, lambda z: share_a(ix, z))
    loop(2, lambda z: share_b(iy, z, there))
    filter_some(1)
    ring_middle(copies_a, *ring_a, 4)
    ring_middle(copies_b1, *ring_b1, 2)
    for i in range(2, 6):
        filter_some(i)

    filt_part[1, NB] = jnp.zeros((8, B), F32)
    taps_factor = 1.0 / math.sqrt(GROUP * N * T)

    def filter_rows(s):
        for half in range(2):
            m = 2 * s + half
            both = jnp.sum(filt_part[0, m] + filt_part[1, m + 1], axis=0, keepdims=True)
            filt_send[s, 2 * half : 2 * half + 1, :] = both[:, :128] * taps_factor
            filt_send[s, 2 * half + 1 : 2 * half + 2, :] = both[:, 128:] * taps_factor
        filt_send[s, 4:8, :] = jnp.zeros((4, 128), F32)

    loop(N, filter_rows)
    for_peers(me, lambda peer: filt_copy(peer).start())
    filt_all[me] = filt_send[me]

    wait_all(BACK, lambda peer: back_all.at[:, chan_rows(peer), :], back_send.at[:2])

    def use_back(r):
        rows = pl.ds(pl.multiple_of(r * 128, 128), 128)
        for half in range(2):
            cols = slice(half * B, (half + 1) * B)
            back = back_all[half, rows, :].astype(F32)
            grad_key_ref[rows, cols] = (v_ref[rows, cols].astype(F32) * back).astype(BF16)
            grad_value_ref[rows, cols] = (k_ref[rows, cols].astype(F32) * back).astype(BF16)

    loop(ROWS // 128, use_back)
    stores[2].start()
    stores[3].start()

    def second_view(held):
        return lambda target, side: held.at[target, side]

    ring_c = (second_view(first_out_a), second_in_a, iy)
    ring_d = (second_view(first_out_b), second_in_b, ix)
    copies_c = ring_copies(3, *ring_c, y_peer)
    copies_d = ring_copies(4, *ring_d, x_peer)

    def store_a(side, e, total):
        first_out_a[e, side, 0] = total.astype(BF16)

    def store_b(pair):
        def store(side, e, total):
            first_out_b[2 * pair + e, side, 0] = total.astype(BF16)

        return store

    ring_end(copies_b0, *ring_b0, 2, store_b(here))
    ring_end(copies_b1, *ring_b1, 2, store_b(there))
    ring_start(copies_d)
    ring_end(copies_a, *ring_a, 4, store_a)
    ring_start(copies_c)
    ring_middle(copies_d, *ring_d, 1)
    ring_middle(copies_c, *ring_c, 1)

    wait_all(FILT, lambda peer: filt_all.at[peer], filt_send.at[0])
    for g in range(2):
        total = jnp.sum(filt_all[16 * g : 16 * g + 16], axis=0)
        for c in range(4):
            filter_grad_ref[g : g + 1, c * 128 : (c + 1) * 128] = total[c : c + 1, :]

    other = ix * 8 + (1 - iz) * 4 + iy

    def z_copy(slot, held, inbox):
        return pltpu.make_async_remote_copy(
            src_ref=held.at[1 - iz],
            dst_ref=inbox,
            send_sem=z_send_sem.at[slot],
            recv_sem=z_recv_sem.at[slot],
            device_id={"seq": other},
            device_id_type=MESH,
        )

    def keep(held):
        def store(side, e, total):
            held[side] = total.astype(BF16)

        return store

    copy_b = z_copy(1, second_out_b, third_in_b)
    copy_a = z_copy(0, second_out_a, third_in_a)
    ring_end(copies_d, *ring_d, 1, keep(second_out_b))
    copy_b.start()
    ring_end(copies_c, *ring_c, 1, keep(second_out_a))
    copy_a.start()
    weight_factor = 1.0 / math.sqrt(N * T)
    copy_b.wait_recv()
    total = second_out_b[iz].astype(F32) + third_in_b[...].astype(F32)
    weight_grad_ref[:, WA:] = total * weight_factor
    copy_a.wait_recv()
    total = second_out_a[iz].astype(F32) + third_in_a[...].astype(F32)
    weight_grad_ref[:, :WA] = total * weight_factor

    for store_out in stores:
        store_out.wait()
    for make in (taps_copy, up_copy, conv_copy, back_copy, filt_copy):
        for_peers(me, lambda peer: make(peer).wait_send())
    rings = (*copies_a, *copies_b0, *copies_b1, *copies_c, *copies_d)
    for c in (x_core, x_near, x_pass, *rings, copy_a, copy_b):
        c.wait_send()


def hand_over(*refs):
    count = len(refs) // 3
    sources, targets, held = refs[:count], refs[count : 2 * count], refs[2 * count : 3 * count]
    sems = refs[3 * count]
    loads = [pltpu.make_async_copy(sources[c], held[c], sems.at[0, c]) for c in range(count)]
    stores = [pltpu.make_async_copy(held[c], targets[c], sems.at[1, c]) for c in range(count)]
    for load in loads:
        load.start()
    for load, store in zip(loads, stores):
        load.wait()
        store.start()
    for store in stores:
        store.wait()


def per_device(layer_input, query_proj, key_proj, value_proj, filter_taps, grad_out):
    vmem = pl.BlockSpec(memory_space=pltpu.VMEM)
    hbm = pl.BlockSpec(memory_space=pl.ANY)
    rows = jax.ShapeDtypeStruct((ROWS, T), BF16)
    shapes = (
        rows,
        rows,
        rows,
        rows,
        jax.ShapeDtypeStruct((2, T), F32),
        jax.ShapeDtypeStruct((128, ROWS), F32),
    )
    results = pl.pallas_call(
        kernel,
        out_shape=shapes,
        in_specs=[hbm] * 4 + [vmem, hbm],
        out_specs=[hbm] * 4 + [vmem] * 2,
        scratch_shapes=[pltpu.VMEM((ROWS, T), BF16)] * 8
        + [
            pltpu.VMEM((2, ROWS, B), BF16),
            pltpu.VMEM((2, ROWS, B), BF16),
            pltpu.VMEM((2, 8, 128), F32),
            pltpu.VMEM((N, 8, 128), F32),
            pltpu.VMEM((PAD + NB, CH, B), BF16),
            pltpu.VMEM((NB + PAD, CH, B), BF16),
            pltpu.VMEM((B, NB * CH), BF16),
            pltpu.VMEM((NB, B, B), BF16),
            pltpu.VMEM((2 * B, B), F32),
            pltpu.VMEM((NB, CH, B), BF16),
            pltpu.VMEM((NB, CH, B), BF16),
            pltpu.VMEM((2, ROWS, B), BF16),
            pltpu.VMEM((2, ROWS, B), BF16),
            pltpu.VMEM((2, NB + 1, 8, B), F32),
            pltpu.VMEM((N, 8, 128), F32),
            pltpu.VMEM((N, 8, 128), F32),
            pltpu.VMEM((N, 128, T), BF16),
            pltpu.VMEM((4, 2, 4, 128, WA), BF16),
            pltpu.VMEM((4, 2, 4, 128, WB), BF16),
            pltpu.VMEM((6, 4, 128, WA), BF16),
            pltpu.VMEM((2, 6, 2, 128, WB), BF16),
            pltpu.VMEM((4, 2, 1, 128, WA), BF16),
            pltpu.VMEM((4, 2, 1, 128, WB), BF16),
            pltpu.VMEM((6, 1, 128, WA), BF16),
            pltpu.VMEM((6, 1, 128, WB), BF16),
            pltpu.VMEM((2, 128, WA), BF16),
            pltpu.VMEM((2, 128, WB), BF16),
            pltpu.VMEM((128, WA), BF16),
            pltpu.VMEM((128, WB), BF16),
            pltpu.SemaphoreType.DMA((KINDS, N)),
            pltpu.SemaphoreType.DMA((KINDS, N)),
            pltpu.SemaphoreType.DMA((3,)),
            pltpu.SemaphoreType.DMA((3,)),
            pltpu.SemaphoreType.DMA((5, 6)),
            pltpu.SemaphoreType.DMA((5, 6)),
            pltpu.SemaphoreType.DMA((2,)),
            pltpu.SemaphoreType.DMA((2,)),
            pltpu.SemaphoreType.DMA((5,)),
            pltpu.SemaphoreType.DMA((4,)),
        ],
        compiler_params=pltpu.CompilerParams(
            collective_id=0, has_side_effects=True, vmem_limit_bytes=62 * 2**20
        ),
    )(
        layer_input.reshape(8, 128, T),
        query_proj,
        key_proj,
        value_proj,
        filter_taps,
        grad_out,
    )
    return tuple(
        pl.pallas_call(
            hand_over,
            out_shape=shapes,
            in_specs=[hbm] * 6,
            out_specs=[hbm] * 6,
            scratch_shapes=[pltpu.VMEM(shape.shape, shape.dtype) for shape in shapes]
            + [pltpu.SemaphoreType.DMA((2, 6))],
        )(*results)
    )


def solution(mesh):
    placed = (P("chan", "seq"),) * 6
    return jax.shard_map(
        per_device,
        mesh=mesh,
        in_specs=placed,
        out_specs=(P("chan", "seq"),) * 5 + (P("seq", "chan"),),
        check_vma=False,
    )
```

```python
import functools
import math

import jax
import jax.numpy as jnp
from jax import lax
from jax.experimental import pallas as pl
from jax.experimental.pallas import tpu as pltpu
from jax.sharding import PartitionSpec as P

GROUP = 512
F32 = jnp.float32
BF16 = jnp.bfloat16
MESH = pl.DeviceIdType.MESH

N = 32
CH = 32
T = 512
B = 256
NB = N * T // B
PAD = 8
ROWS = N * CH
WA = 384
WB = ROWS - WA
KINDS = 6
MIXED, UP, TAPS, CONV, BACK, FILT = range(KINDS)


def seq_copy(src, dst, kind, peer, sems, me):
    send, recv = sems
    return pltpu.make_async_remote_copy(
        src_ref=src,
        dst_ref=dst,
        send_sem=send.at[kind, peer],
        recv_sem=recv.at[kind, me],
        device_id={"seq": peer},
        device_id_type=MESH,
    )


def for_peers(me, body):
    def step(i, carry):
        body(lax.rem(me + i, N))
        return carry

    lax.fori_loop(1, N, step, 0)


def loop(n, body, start=0):
    def step(i, carry):
        body(i)
        return carry

    lax.fori_loop(start, n, step, 0)


def kernel(
    x_hbm,
    q_hbm,
    k_hbm,
    v_hbm,
    taps_ref,
    g_hbm,
    mixed_out_hbm,
    grad_query_hbm,
    grad_key_hbm,
    grad_value_hbm,
    filter_grad_ref,
    weight_grad_ref,
    q_ref,
    k_ref,
    v_ref,
    g_ref,
    mixed_out_ref,
    grad_query_ref,
    grad_key_ref,
    grad_value_ref,
    mixed_send,
    up_send,
    taps_send,
    taps_all,
    mixed_all,
    up_all,
    mixed_flip,
    toeplitz,
    acc,
    conv_send,
    back_send,
    conv_all,
    back_all,
    filt_part,
    filt_send,
    filt_all,
    x_all,
    part_a,
    part_b,
    first_in_a,
    first_in_b,
    first_out_a,
    first_out_b,
    second_in_a,
    second_in_b,
    second_out_a,
    second_out_b,
    third_in_a,
    third_in_b,
    send_sem,
    recv_sem,
    x_send_sem,
    x_recv_sem,
    r_send_sem,
    r_recv_sem,
    z_send_sem,
    z_recv_sem,
    in_sem,
    out_sem,
):
    me = lax.axis_index("seq")
    chan = lax.axis_index("chan")
    ix = me // 8
    iz = lax.rem(me // 4, 2)
    iy = lax.rem(me, 4)
    sems = (send_sem, recv_sem)

    own_x = pl.ds(chan * 8, 8)
    loads = [
        pltpu.make_async_copy(src, dst, in_sem.at[slot])
        for slot, (src, dst) in enumerate(
            (
                (k_hbm, k_ref),
                (v_hbm, v_ref),
                (g_hbm, g_ref),
                (q_hbm, q_ref),
                (x_hbm, x_all.at[own_x]),
            )
        )
    ]
    for load in loads:
        load.start()
    stores = [
        pltpu.make_async_copy(src, dst, out_sem.at[slot])
        for slot, (src, dst) in enumerate(
            (
                (mixed_out_ref, mixed_out_hbm),
                (grad_query_ref, grad_query_hbm),
                (grad_key_ref, grad_key_hbm),
                (grad_value_ref, grad_value_hbm),
            )
        )
    ]

    barrier = pltpu.get_barrier_semaphore()
    for_peers(
        me,
        lambda peer: pl.semaphore_signal(
            barrier, inc=1, device_id={"seq": peer}, device_id_type=MESH
        ),
    )
    core_peer = chan + 1 - 2 * lax.rem(chan, 2)
    near_peer = lax.rem(chan + 2, 4)
    for peer in (core_peer, near_peer):
        pl.semaphore_signal(barrier, inc=1, device_id={"chan": peer}, device_id_type=MESH)

    def make_mixed(r):
        rows = pl.ds(pl.multiple_of(r * 128, 128), 128)
        prod = (k_ref[rows, :].astype(F32) * v_ref[rows, :].astype(F32)).astype(BF16)
        mixed_send[0, rows, :] = prod[:, :B]
        mixed_send[1, rows, :] = prod[:, B:]

    def make_up(r):
        rows = pl.ds(pl.multiple_of(r * 128, 128), 128)
        prod = (g_ref[rows, :].astype(F32) * q_ref[rows, :].astype(F32)).astype(BF16)
        up_send[0, rows, :] = prod[:, :B]
        up_send[1, rows, :] = prod[:, B:]

    for g in range(2):
        for c in range(4):
            taps_send[g, c : c + 1, :] = taps_ref[g : g + 1, c * 128 : (c + 1) * 128]
        taps_send[g, 4:8, :] = jnp.zeros((4, 128), F32)
    loads[0].wait()
    loads[1].wait()
    loop(ROWS // 128, make_mixed)
    pl.semaphore_wait(barrier, N + 1)

    def chan_rows(peer):
        return pl.ds(pl.multiple_of(peer * CH, CH), CH)

    def taps_copy(peer):
        return seq_copy(taps_send.at[peer // 16], taps_all.at[me], TAPS, peer, sems, me)

    def mixed_copy(peer):
        return seq_copy(
            mixed_send.at[:, chan_rows(peer), :],
            mixed_all.at[pl.ds(PAD + 2 * me, 2)],
            MIXED,
            peer,
            sems,
            me,
        )

    def up_copy(peer):
        return seq_copy(
            up_send.at[:, chan_rows(peer), :],
            up_all.at[pl.ds(2 * me, 2)],
            UP,
            peer,
            sems,
            me,
        )

    def conv_copy(peer):
        return seq_copy(
            conv_send.at[pl.ds(2 * peer, 2)],
            conv_all.at[:, chan_rows(me), :],
            CONV,
            peer,
            sems,
            me,
        )

    def back_copy(peer):
        return seq_copy(
            back_send.at[pl.ds(2 * peer, 2)],
            back_all.at[:, chan_rows(me), :],
            BACK,
            peer,
            sems,
            me,
        )

    def filt_copy(peer):
        return seq_copy(filt_send.at[peer], filt_all.at[me], FILT, peer, sems, me)

    def wait_all(kind, dst_of, src_any):
        def one(peer):
            pltpu.make_async_remote_copy(
                src_ref=src_any,
                dst_ref=dst_of(peer),
                send_sem=send_sem.at[kind, peer],
                recv_sem=recv_sem.at[kind, peer],
                device_id={"seq": peer},
                device_id_type=MESH,
            ).wait_recv()

        for_peers(me, one)

    near_x = pl.ds(near_peer * 8, 8)

    def x_copy(slot, src, rows, peer):
        return pltpu.make_async_remote_copy(
            src_ref=src,
            dst_ref=x_all.at[rows],
            send_sem=x_send_sem.at[slot],
            recv_sem=x_recv_sem.at[slot],
            device_id={"chan": peer},
            device_id_type=MESH,
        )

    x_core = x_copy(0, x_hbm, own_x, core_peer)
    x_near = x_copy(1, x_hbm, own_x, near_peer)
    x_pass = x_copy(2, x_all.at[near_x], near_x, core_peer)

    for_peers(me, lambda peer: taps_copy(peer).start())
    for_peers(me, lambda peer: mixed_copy(peer).start())
    x_core.start()
    loads[2].wait()
    loads[3].wait()
    loop(ROWS // 128, make_up)

    taps_all[me] = taps_send[me // 16]
    mixed_all[pl.ds(PAD + 2 * me, 2)] = mixed_send[:, chan_rows(me), :]
    up_all[pl.ds(2 * me, 2)] = up_send[:, chan_rows(me), :]
    mixed_all[:PAD] = jnp.zeros((PAD, CH, B), BF16)
    up_all[NB:] = jnp.zeros((PAD, CH, B), BF16)

    for_peers(me, lambda peer: mixed_copy(peer).wait_send())
    x_near.start()

    wait_all(TAPS, lambda peer: taps_all.at[peer], taps_send.at[0])
    row_id = lax.broadcasted_iota(jnp.int32, (B, B), 0)
    col_id = lax.broadcasted_iota(jnp.int32, (B, B), 1)

    def sheared(src, half):
        piece = taps_all[src]
        wide = jnp.concatenate(
            [piece[2 * half : 2 * half + 1, :], piece[2 * half + 1 : 2 * half + 2, :]], axis=1
        )
        return pltpu.roll(jnp.broadcast_to(wide, (B, B)), 0, 1, stride=1, stride_axis=0)

    acc[:B] = jnp.zeros((B, B), F32)

    def make_tiles(s):
        for half in range(2):
            now = sheared(s, half)
            toeplitz[2 * s + half] = jnp.where(col_id >= row_id, now, acc[:B]).astype(BF16)
            acc[:B] = now

    loop(N, make_tiles)

    wait_all(MIXED, lambda peer: mixed_all.at[pl.ds(PAD + 2 * peer, 2)], mixed_send.at[:, :CH, :])

    def hand_back(i, copy, send, dest):
        for r in range(8):
            peer = 8 * i + r

            @pl.when(peer != me)
            def _():
                copy(peer).start()

            @pl.when(peer == me)
            def _():
                dest[:, chan_rows(me), :] = send[pl.ds(2 * me, 2)]

    def conv_chunk(step):
        i = lax.rem(ix + step, 4)
        acc[...] = jnp.zeros((2 * B, B), F32)

        def some(j, first, blocks):
            part = None
            for u in range(8):
                m = 8 * j + u
                lhs = mixed_all[pl.ds(PAD + first - m, blocks)].reshape(blocks * CH, B)
                term = jnp.dot(lhs, toeplitz[m], preferred_element_type=F32)
                part = term if part is None else part + term
            return part

        def full(j):
            acc[...] += some(j, 16 * i, 16)

        loop(2 * i + 1, full)
        acc[B:] += some(2 * i + 1, 16 * i + 8, 8)
        conv_send[pl.ds(16 * i, 16)] = acc[...].astype(BF16).reshape(16, CH, B)
        hand_back(i, conv_copy, conv_send, conv_all)

    loop(4, conv_chunk)

    for_peers(me, lambda peer: up_copy(peer).start())


    wait_all(CONV, lambda peer: conv_all.at[:, chan_rows(peer), :], conv_send.at[:2])

    def use_conv(r):
        rows = pl.ds(pl.multiple_of(r * 128, 128), 128)
        for half in range(2):
            cols = slice(half * B, (half + 1) * B)
            conv = conv_all[half, rows, :].astype(F32)
            grad_query_ref[rows, cols] = (g_ref[rows, cols].astype(F32) * conv).astype(BF16)
            mixed_out_ref[rows, cols] = (q_ref[rows, cols].astype(F32) * conv).astype(BF16)

    loop(ROWS // 128, use_conv)
    stores[0].start()
    stores[1].start()
    loads[4].wait()
    x_core.wait_recv()

    def share(lhs, first, count):
        return lax.dot_general(
            lhs,
            grad_query_ref[first : first + count, :],
            (((1,), (1,)), ((), ())),
            preferred_element_type=F32,
        ).astype(BF16)

    def share_a(px, pz):
        lhs = x_all[pl.ds(8 * px + 4 * pz, 4)].reshape(512, T)
        part_a[px, pz] = share(lhs, 0, WA).reshape(4, 128, WA)

    def share_b(py, pz, pair):
        lhs = jnp.concatenate([x_all[16 * pair + 8 * e + 4 * pz + py] for e in range(2)], axis=0)
        part_b[py, pz, pl.ds(2 * pair, 2)] = share(lhs, WA, WB).reshape(2, 128, WB)

    def x_peer(d):
        return lax.rem(ix + d, 4) * 8 + iz * 4 + iy

    def y_peer(d):
        return ix * 8 + iz * 4 + lax.rem(iy + d, 4)

    def ring_copies(bank, view, inbox, index, peer_of):
        up, down, far = (lax.rem(index + d, 4) for d in (1, 3, 2))

        def ring_copy(slot, target, side, hop):
            return pltpu.make_async_remote_copy(
                src_ref=view(target, side),
                dst_ref=inbox.at[slot],
                send_sem=r_send_sem.at[bank, slot],
                recv_sem=r_recv_sem.at[bank, slot],
                device_id={"seq": peer_of(hop)},
                device_id_type=MESH,
            )

        return (
            ring_copy(0, far, 0, 1),
            ring_copy(1, far, 1, 3),
            ring_copy(2, up, 1, 1),
            ring_copy(3, down, 0, 3),
            ring_copy(4, up, 0, 1),
            ring_copy(5, down, 1, 3),
        )

    def ring_start(copies, first=0, last=4):
        for c in copies[first:last]:
            c.start()

    def ring_middle(copies, view, inbox, index, blocks):
        for slot, there, side in ((0, 1, 0), (1, 3, 1)):
            copies[slot].wait_recv()
            held = view(lax.rem(index + there, 4), side)

            def add(e):
                total = held[e].astype(F32) + inbox[slot, e].astype(F32)
                held[e] = total.astype(BF16)

            loop(blocks, add)
            copies[4 + slot].start()

    def ring_end(copies, view, inbox, index, blocks, store):
        for slot in (2, 3, 4, 5):
            copies[slot].wait_recv()

        def add(e):
            for side, one, two in ((0, 4, 3), (1, 5, 2)):
                total = view(index, side)[e].astype(F32) + (
                    inbox[one, e].astype(F32) + inbox[two, e].astype(F32)
                )
                store(side, e, total)

        loop(blocks, add)

    def view_a(target, side):
        return part_a.at[target, side]

    def view_b(pair):
        return lambda target, side: part_b.at[target, side, pl.ds(2 * pair, 2)]

    here = chan // 2
    there = 1 - here
    ring_a = (view_a, first_in_a, ix)
    ring_b0 = (view_b(here), first_in_b.at[0], iy)
    ring_b1 = (view_b(there), first_in_b.at[1], iy)
    copies_a = ring_copies(0, *ring_a, x_peer)
    copies_b0 = ring_copies(1, *ring_b0, y_peer)
    copies_b1 = ring_copies(2, *ring_b1, y_peer)

    def shares_b(copies, pair):
        loop(2, lambda z: share_b(lax.rem(iy + 2, 4), z, pair))
        ring_start(copies, 0, 2)
        loop(2, lambda z: share_b(lax.rem(iy + 3 - 2 * z, 4), z, pair))
        ring_start(copies, 2, 4)
        loop(2, lambda z: share_b(lax.rem(iy + 1 + 2 * z, 4), z, pair))

    shares_b(copies_b0, here)
    loop(2, lambda z: share_b(iy, z, here))

    flip = (row_id + col_id == B - 1).astype(BF16)
    for c in range(8):
        piece = mixed_all[PAD + 8 * c : PAD + 8 * c + 8].reshape(B, B)
        mixed_flip[:, c * B : (c + 1) * B] = lax.dot_general(
            flip, piece, (((1,), (1,)), ((), ())), preferred_element_type=F32
        ).astype(BF16)

    def filter_tile(i, m):
        depth = (8 - i) * B
        corr = jnp.dot(
            mixed_flip[:, :depth],
            up_all[pl.ds(m, 8 * (8 - i))].reshape(depth, B),
            preferred_element_type=F32,
        )
        turned = pltpu.roll(corr, 1, 1, stride=1, stride_axis=0)
        above = jnp.where(col_id <= row_id, turned, 0.0)
        below = turned - above
        filt_part[0, m] = jnp.sum(above.reshape(B // 8, 8, B), axis=0)
        filt_part[1, m] = jnp.sum(below.reshape(B // 8, 8, B), axis=0)

    def filter_some(i):
        loop(8, lambda u: filter_tile(i, 8 * i + u))

    wait_all(UP, lambda peer: up_all.at[pl.ds(2 * peer, 2)], up_send.at[:, :CH, :])

    def back_chunk(step):
        i = lax.rem(ix + step, 4)
        acc[...] = jnp.zeros((2 * B, B), F32)

        def some(j, blocks):
            part = None
            for u in range(8):
                m = 8 * j + u
                lhs = up_all[pl.ds(16 * i + m, blocks)].reshape(blocks * CH, B)
                term = lax.dot_general(
                    lhs, toeplitz[m], (((1,), (1,)), ((), ())), preferred_element_type=F32
                )
                part = term if part is None else part + term
            return part

        def full(j):
            acc[...] += some(j, 16)

        loop(7 - 2 * i, full)
        acc[:B] += some(7 - 2 * i, 8)
        back_send[pl.ds(16 * i, 16)] = acc[...].astype(BF16).reshape(16, CH, B)

    loop(1, back_chunk)
    ring_middle(copies_b0, *ring_b0, 2)
    loop(2, back_chunk, 1)

    x_near.wait_recv()
    x_pass.start()
    loop(4, back_chunk, 2)
    x_pass.wait_recv()
    loop(2, lambda z: share_a(lax.rem(ix + 2, 4), z))
    ring_start(copies_a, 0, 2)
    loop(2, lambda z: share_a(lax.rem(ix + 3 - 2 * z, 4), z))
    ring_start(copies_a, 2, 4)
    loop(2, lambda z: share_a(lax.rem(ix + 1 + 2 * z, 4), z))
    shares_b(copies_b1, there)
    for_peers(me, lambda peer: back_copy(peer).start())
    back_all[:, chan_rows(me), :] = back_send[pl.ds(2 * me, 2)]
    loop(2, lambda z: share_a(ix, z))
    loop(2, lambda z: share_b(iy, z, there))
    filter_some(0)
    ring_middle(copies_a, *ring_a, 4)
    ring_middle(copies_b1, *ring_b1, 2)
    for i in range(1, 8):
        filter_some(i)

    filt_part[1, NB] = jnp.zeros((8, B), F32)
    taps_factor = 1.0 / math.sqrt(GROUP * N * T)

    def filter_rows(s):
        for half in range(2):
            m = 2 * s + half
            both = jnp.sum(filt_part[0, m] + filt_part[1, m + 1], axis=0, keepdims=True)
            filt_send[s, 2 * half : 2 * half + 1, :] = both[:, :128] * taps_factor
            filt_send[s, 2 * half + 1 : 2 * half + 2, :] = both[:, 128:] * taps_factor
        filt_send[s, 4:8, :] = jnp.zeros((4, 128), F32)

    loop(N, filter_rows)
    for_peers(me, lambda peer: filt_copy(peer).start())
    filt_all[me] = filt_send[me]

    wait_all(BACK, lambda peer: back_all.at[:, chan_rows(peer), :], back_send.at[:2])

    def use_back(r):
        rows = pl.ds(pl.multiple_of(r * 128, 128), 128)
        for half in range(2):
            cols = slice(half * B, (half + 1) * B)
            back = back_all[half, rows, :].astype(F32)
            grad_key_ref[rows, cols] = (v_ref[rows, cols].astype(F32) * back).astype(BF16)
            grad_value_ref[rows, cols] = (k_ref[rows, cols].astype(F32) * back).astype(BF16)

    loop(ROWS // 128, use_back)
    stores[2].start()
    stores[3].start()

    def second_view(held):
        return lambda target, side: held.at[target, side]

    ring_c = (second_view(first_out_a), second_in_a, iy)
    ring_d = (second_view(first_out_b), second_in_b, ix)
    copies_c = ring_copies(3, *ring_c, y_peer)
    copies_d = ring_copies(4, *ring_d, x_peer)

    def store_a(side, e, total):
        first_out_a[e, side, 0] = total.astype(BF16)

    def store_b(pair):
        def store(side, e, total):
            first_out_b[2 * pair + e, side, 0] = total.astype(BF16)

        return store

    ring_end(copies_b0, *ring_b0, 2, store_b(here))
    ring_end(copies_b1, *ring_b1, 2, store_b(there))
    ring_start(copies_d)
    ring_end(copies_a, *ring_a, 4, store_a)
    ring_start(copies_c)
    ring_middle(copies_d, *ring_d, 1)
    ring_middle(copies_c, *ring_c, 1)

    wait_all(FILT, lambda peer: filt_all.at[peer], filt_send.at[0])
    for g in range(2):
        total = jnp.sum(filt_all[16 * g : 16 * g + 16], axis=0)
        for c in range(4):
            filter_grad_ref[g : g + 1, c * 128 : (c + 1) * 128] = total[c : c + 1, :]

    other = ix * 8 + (1 - iz) * 4 + iy

    def z_copy(slot, held, inbox):
        return pltpu.make_async_remote_copy(
            src_ref=held.at[1 - iz],
            dst_ref=inbox,
            send_sem=z_send_sem.at[slot],
            recv_sem=z_recv_sem.at[slot],
            device_id={"seq": other},
            device_id_type=MESH,
        )

    def keep(held):
        def store(side, e, total):
            held[side] = total.astype(BF16)

        return store

    copy_b = z_copy(1, second_out_b, third_in_b)
    copy_a = z_copy(0, second_out_a, third_in_a)
    ring_end(copies_d, *ring_d, 1, keep(second_out_b))
    copy_b.start()
    ring_end(copies_c, *ring_c, 1, keep(second_out_a))
    copy_a.start()
    weight_factor = 1.0 / math.sqrt(N * T)
    copy_b.wait_recv()
    total = second_out_b[iz].astype(F32) + third_in_b[...].astype(F32)
    weight_grad_ref[:, WA:] = total * weight_factor
    copy_a.wait_recv()
    total = second_out_a[iz].astype(F32) + third_in_a[...].astype(F32)
    weight_grad_ref[:, :WA] = total * weight_factor

    for store_out in stores:
        store_out.wait()
    for make in (taps_copy, up_copy, conv_copy, back_copy, filt_copy):
        for_peers(me, lambda peer: make(peer).wait_send())
    rings = (*copies_a, *copies_b0, *copies_b1, *copies_c, *copies_d)
    for c in (x_core, x_near, x_pass, *rings, copy_a, copy_b):
        c.wait_send()


def hand_over(*refs):
    count = len(refs) // 3
    sources, targets, held = refs[:count], refs[count : 2 * count], refs[2 * count : 3 * count]
    sems = refs[3 * count]
    loads = [pltpu.make_async_copy(sources[c], held[c], sems.at[0, c]) for c in range(count)]
    stores = [pltpu.make_async_copy(held[c], targets[c], sems.at[1, c]) for c in range(count)]
    for load in loads:
        load.start()
    for load, store in zip(loads, stores):
        load.wait()
        store.start()
    for store in stores:
        store.wait()


def per_device(layer_input, query_proj, key_proj, value_proj, filter_taps, grad_out):
    vmem = pl.BlockSpec(memory_space=pltpu.VMEM)
    hbm = pl.BlockSpec(memory_space=pl.ANY)
    rows = jax.ShapeDtypeStruct((ROWS, T), BF16)
    shapes = (
        rows,
        rows,
        rows,
        rows,
        jax.ShapeDtypeStruct((2, T), F32),
        jax.ShapeDtypeStruct((128, ROWS), F32),
    )
    results = pl.pallas_call(
        kernel,
        out_shape=shapes,
        in_specs=[hbm] * 4 + [vmem, hbm],
        out_specs=[hbm] * 4 + [vmem] * 2,
        scratch_shapes=[pltpu.VMEM((ROWS, T), BF16)] * 8
        + [
            pltpu.VMEM((2, ROWS, B), BF16),
            pltpu.VMEM((2, ROWS, B), BF16),
            pltpu.VMEM((2, 8, 128), F32),
            pltpu.VMEM((N, 8, 128), F32),
            pltpu.VMEM((PAD + NB, CH, B), BF16),
            pltpu.VMEM((NB + PAD, CH, B), BF16),
            pltpu.VMEM((B, NB * CH), BF16),
            pltpu.VMEM((NB, B, B), BF16),
            pltpu.VMEM((2 * B, B), F32),
            pltpu.VMEM((NB, CH, B), BF16),
            pltpu.VMEM((NB, CH, B), BF16),
            pltpu.VMEM((2, ROWS, B), BF16),
            pltpu.VMEM((2, ROWS, B), BF16),
            pltpu.VMEM((2, NB + 1, 8, B), F32),
            pltpu.VMEM((N, 8, 128), F32),
            pltpu.VMEM((N, 8, 128), F32),
            pltpu.VMEM((N, 128, T), BF16),
            pltpu.VMEM((4, 2, 4, 128, WA), BF16),
            pltpu.VMEM((4, 2, 4, 128, WB), BF16),
            pltpu.VMEM((6, 4, 128, WA), BF16),
            pltpu.VMEM((2, 6, 2, 128, WB), BF16),
            pltpu.VMEM((4, 2, 1, 128, WA), BF16),
            pltpu.VMEM((4, 2, 1, 128, WB), BF16),
            pltpu.VMEM((6, 1, 128, WA), BF16),
            pltpu.VMEM((6, 1, 128, WB), BF16),
            pltpu.VMEM((2, 128, WA), BF16),
            pltpu.VMEM((2, 128, WB), BF16),
            pltpu.VMEM((128, WA), BF16),
            pltpu.VMEM((128, WB), BF16),
            pltpu.SemaphoreType.DMA((KINDS, N)),
            pltpu.SemaphoreType.DMA((KINDS, N)),
            pltpu.SemaphoreType.DMA((3,)),
            pltpu.SemaphoreType.DMA((3,)),
            pltpu.SemaphoreType.DMA((5, 6)),
            pltpu.SemaphoreType.DMA((5, 6)),
            pltpu.SemaphoreType.DMA((2,)),
            pltpu.SemaphoreType.DMA((2,)),
            pltpu.SemaphoreType.DMA((5,)),
            pltpu.SemaphoreType.DMA((4,)),
        ],
        compiler_params=pltpu.CompilerParams(
            collective_id=0, has_side_effects=True, vmem_limit_bytes=62 * 2**20
        ),
    )(
        layer_input.reshape(8, 128, T),
        query_proj,
        key_proj,
        value_proj,
        filter_taps,
        grad_out,
    )
    return tuple(
        pl.pallas_call(
            hand_over,
            out_shape=shapes,
            in_specs=[hbm] * 6,
            out_specs=[hbm] * 6,
            scratch_shapes=[pltpu.VMEM(shape.shape, shape.dtype) for shape in shapes]
            + [pltpu.SemaphoreType.DMA((2, 6))],
        )(*results)
    )


def solution(mesh):
    placed = (P("chan", "seq"),) * 6
    return jax.shard_map(
        per_device,
        mesh=mesh,
        in_specs=placed,
        out_specs=(P("chan", "seq"),) * 5 + (P("seq", "chan"),),
        check_vma=False,
    )
```

```python
import functools
import math

import jax
import jax.numpy as jnp
from jax import lax
from jax.experimental import pallas as pl
from jax.experimental.pallas import tpu as pltpu
from jax.sharding import PartitionSpec as P

GROUP = 512
F32 = jnp.float32
BF16 = jnp.bfloat16
MESH = pl.DeviceIdType.MESH

N = 32
CH = 32
T = 512
B = 256
NB = N * T // B
PAD = 8
ROWS = N * CH
WA = 256
WB = 512
WC = (ROWS - WA - WB) // 2
KINDS = 6
MIXED, UP, TAPS, CONV, BACK, FILT = range(KINDS)


def seq_copy(src, dst, kind, peer, sems, me):
    send, recv = sems
    return pltpu.make_async_remote_copy(
        src_ref=src,
        dst_ref=dst,
        send_sem=send.at[kind, peer],
        recv_sem=recv.at[kind, me],
        device_id={"seq": peer},
        device_id_type=MESH,
    )


def for_peers(me, body):
    def step(i, carry):
        body(lax.rem(me + i, N))
        return carry

    lax.fori_loop(1, N, step, 0)


def loop(n, body, start=0):
    def step(i, carry):
        body(i)
        return carry

    lax.fori_loop(start, n, step, 0)


def kernel(
    x_hbm,
    q_hbm,
    k_hbm,
    v_hbm,
    taps_ref,
    g_hbm,
    mixed_out_hbm,
    grad_query_hbm,
    grad_key_hbm,
    grad_value_hbm,
    filter_grad_ref,
    weight_grad_ref,
    q_ref,
    k_ref,
    v_ref,
    g_ref,
    mixed_out_ref,
    grad_query_ref,
    grad_key_ref,
    grad_value_ref,
    mixed_send,
    up_send,
    taps_send,
    taps_all,
    mixed_all,
    up_all,
    mixed_flip,
    toeplitz,
    acc,
    conv_send,
    back_send,
    conv_all,
    back_all,
    filt_part,
    filt_send,
    filt_all,
    x_all,
    part_a,
    part_b,
    first_in_a,
    first_in_b,
    first_out_a,
    first_out_b,
    second_in_a,
    second_in_b,
    second_out_a,
    second_out_b,
    third_in_a,
    third_in_b,
    part_c,
    across_in,
    first_in_c,
    first_out_c,
    second_in_c,
    send_sem,
    recv_sem,
    x_send_sem,
    x_recv_sem,
    r_send_sem,
    r_recv_sem,
    z_send_sem,
    z_recv_sem,
    in_sem,
    out_sem,
):
    me = lax.axis_index("seq")
    chan = lax.axis_index("chan")
    ix = me // 8
    iz = lax.rem(me // 4, 2)
    iy = lax.rem(me, 4)
    sems = (send_sem, recv_sem)

    own_x = pl.ds(chan * 8, 8)
    loads = [
        pltpu.make_async_copy(src, dst, in_sem.at[slot])
        for slot, (src, dst) in enumerate(
            (
                (k_hbm, k_ref),
                (v_hbm, v_ref),
                (g_hbm, g_ref),
                (q_hbm, q_ref),
                (x_hbm, x_all.at[own_x]),
            )
        )
    ]
    for load in loads:
        load.start()
    stores = [
        pltpu.make_async_copy(src, dst, out_sem.at[slot])
        for slot, (src, dst) in enumerate(
            (
                (mixed_out_ref, mixed_out_hbm),
                (grad_query_ref, grad_query_hbm),
                (grad_key_ref, grad_key_hbm),
                (grad_value_ref, grad_value_hbm),
            )
        )
    ]

    barrier = pltpu.get_barrier_semaphore()
    for_peers(
        me,
        lambda peer: pl.semaphore_signal(
            barrier, inc=1, device_id={"seq": peer}, device_id_type=MESH
        ),
    )
    core_peer = chan + 1 - 2 * lax.rem(chan, 2)
    near_peer = lax.rem(chan + 2, 4)
    for peer in (core_peer, near_peer):
        pl.semaphore_signal(barrier, inc=1, device_id={"chan": peer}, device_id_type=MESH)

    def make_mixed(r):
        rows = pl.ds(pl.multiple_of(r * 128, 128), 128)
        prod = (k_ref[rows, :].astype(F32) * v_ref[rows, :].astype(F32)).astype(BF16)
        mixed_send[0, rows, :] = prod[:, :B]
        mixed_send[1, rows, :] = prod[:, B:]

    def make_up(r):
        rows = pl.ds(pl.multiple_of(r * 128, 128), 128)
        prod = (g_ref[rows, :].astype(F32) * q_ref[rows, :].astype(F32)).astype(BF16)
        up_send[0, rows, :] = prod[:, :B]
        up_send[1, rows, :] = prod[:, B:]

    for g in range(2):
        for c in range(4):
            taps_send[g, c : c + 1, :] = taps_ref[g : g + 1, c * 128 : (c + 1) * 128]
        taps_send[g, 4:8, :] = jnp.zeros((4, 128), F32)
    loads[0].wait()
    loads[1].wait()
    loop(ROWS // 128, make_mixed)
    pl.semaphore_wait(barrier, N + 1)

    def chan_rows(peer):
        return pl.ds(pl.multiple_of(peer * CH, CH), CH)

    def taps_copy(peer):
        return seq_copy(taps_send.at[peer // 16], taps_all.at[me], TAPS, peer, sems, me)

    def mixed_copy(peer):
        return seq_copy(
            mixed_send.at[:, chan_rows(peer), :],
            mixed_all.at[pl.ds(PAD + 2 * me, 2)],
            MIXED,
            peer,
            sems,
            me,
        )

    def up_copy(peer):
        return seq_copy(
            up_send.at[:, chan_rows(peer), :],
            up_all.at[pl.ds(2 * me, 2)],
            UP,
            peer,
            sems,
            me,
        )

    def conv_copy(peer):
        return seq_copy(
            conv_send.at[pl.ds(2 * peer, 2)],
            conv_all.at[:, chan_rows(me), :],
            CONV,
            peer,
            sems,
            me,
        )

    def back_copy(peer):
        return seq_copy(
            back_send.at[pl.ds(2 * peer, 2)],
            back_all.at[:, chan_rows(me), :],
            BACK,
            peer,
            sems,
            me,
        )

    def filt_copy(peer):
        return seq_copy(filt_send.at[peer], filt_all.at[me], FILT, peer, sems, me)

    def wait_all(kind, dst_of, src_any):
        def one(peer):
            pltpu.make_async_remote_copy(
                src_ref=src_any,
                dst_ref=dst_of(peer),
                send_sem=send_sem.at[kind, peer],
                recv_sem=recv_sem.at[kind, peer],
                device_id={"seq": peer},
                device_id_type=MESH,
            ).wait_recv()

        for_peers(me, one)

    near_x = pl.ds(near_peer * 8, 8)

    def x_copy(slot, src, rows, peer):
        return pltpu.make_async_remote_copy(
            src_ref=src,
            dst_ref=x_all.at[rows],
            send_sem=x_send_sem.at[slot],
            recv_sem=x_recv_sem.at[slot],
            device_id={"chan": peer},
            device_id_type=MESH,
        )

    x_core = x_copy(0, x_hbm, own_x, core_peer)
    x_near = x_copy(1, x_hbm, own_x, near_peer)
    x_pass = x_copy(2, x_all.at[near_x], near_x, core_peer)

    for_peers(me, lambda peer: taps_copy(peer).start())
    for_peers(me, lambda peer: mixed_copy(peer).start())
    x_core.start()
    loads[2].wait()
    loads[3].wait()
    loop(ROWS // 128, make_up)

    taps_all[me] = taps_send[me // 16]
    mixed_all[pl.ds(PAD + 2 * me, 2)] = mixed_send[:, chan_rows(me), :]
    up_all[pl.ds(2 * me, 2)] = up_send[:, chan_rows(me), :]
    mixed_all[:PAD] = jnp.zeros((PAD, CH, B), BF16)
    up_all[NB:] = jnp.zeros((PAD, CH, B), BF16)

    for_peers(me, lambda peer: mixed_copy(peer).wait_send())
    for_peers(me, lambda peer: up_copy(peer).start())

    wait_all(TAPS, lambda peer: taps_all.at[peer], taps_send.at[0])
    row_id = lax.broadcasted_iota(jnp.int32, (B, B), 0)
    col_id = lax.broadcasted_iota(jnp.int32, (B, B), 1)

    def sheared(src, half):
        piece = taps_all[src]
        wide = jnp.concatenate(
            [piece[2 * half : 2 * half + 1, :], piece[2 * half + 1 : 2 * half + 2, :]], axis=1
        )
        return pltpu.roll(jnp.broadcast_to(wide, (B, B)), 0, 1, stride=1, stride_axis=0)

    acc[:B] = jnp.zeros((B, B), F32)

    def make_tiles(s):
        for half in range(2):
            now = sheared(s, half)
            toeplitz[2 * s + half] = jnp.where(col_id >= row_id, now, acc[:B]).astype(BF16)
            acc[:B] = now

    loop(N, make_tiles)

    wait_all(MIXED, lambda peer: mixed_all.at[pl.ds(PAD + 2 * peer, 2)], mixed_send.at[:, :CH, :])

    def hand_back(i, copy, send, dest):
        for r in range(8):
            peer = 8 * i + r

            @pl.when(peer != me)
            def _():
                copy(peer).start()

            @pl.when(peer == me)
            def _():
                dest[:, chan_rows(me), :] = send[pl.ds(2 * me, 2)]

    def conv_chunk(step):
        i = lax.rem(ix + step, 4)
        acc[...] = jnp.zeros((2 * B, B), F32)

        def some(j, first, blocks):
            part = None
            for u in range(8):
                m = 8 * j + u
                lhs = mixed_all[pl.ds(PAD + first - m, blocks)].reshape(blocks * CH, B)
                term = jnp.dot(lhs, toeplitz[m], preferred_element_type=F32)
                part = term if part is None else part + term
            return part

        def full(j):
            acc[...] += some(j, 16 * i, 16)

        loop(2 * i + 1, full)
        acc[B:] += some(2 * i + 1, 16 * i + 8, 8)
        conv_send[pl.ds(16 * i, 16)] = acc[...].astype(BF16).reshape(16, CH, B)
        hand_back(i, conv_copy, conv_send, conv_all)

    loop(4, conv_chunk)
    x_near.start()

    wait_all(UP, lambda peer: up_all.at[pl.ds(2 * peer, 2)], up_send.at[:, :CH, :])

    def back_chunk(step):
        i = lax.rem(ix + step, 4)
        acc[...] = jnp.zeros((2 * B, B), F32)

        def some(j, blocks):
            part = None
            for u in range(8):
                m = 8 * j + u
                lhs = up_all[pl.ds(16 * i + m, blocks)].reshape(blocks * CH, B)
                term = lax.dot_general(
                    lhs, toeplitz[m], (((1,), (1,)), ((), ())), preferred_element_type=F32
                )
                part = term if part is None else part + term
            return part

        def full(j):
            acc[...] += some(j, 16)

        loop(7 - 2 * i, full)
        acc[:B] += some(7 - 2 * i, 8)
        back_send[pl.ds(16 * i, 16)] = acc[...].astype(BF16).reshape(16, CH, B)

    loop(4, back_chunk)

    wait_all(CONV, lambda peer: conv_all.at[:, chan_rows(peer), :], conv_send.at[:2])

    def use_conv(r):
        rows = pl.ds(pl.multiple_of(r * 128, 128), 128)
        for half in range(2):
            cols = slice(half * B, (half + 1) * B)
            conv = conv_all[half, rows, :].astype(F32)
            grad_query_ref[rows, cols] = (g_ref[rows, cols].astype(F32) * conv).astype(BF16)
            mixed_out_ref[rows, cols] = (q_ref[rows, cols].astype(F32) * conv).astype(BF16)

    loop(ROWS // 128, use_conv)
    stores[0].start()
    stores[1].start()
    loads[4].wait()
    x_core.wait_recv()

    def share(lhs, first, count):
        return lax.dot_general(
            lhs,
            grad_query_ref[first : first + count, :],
            (((1,), (1,)), ((), ())),
            preferred_element_type=F32,
        ).astype(BF16)

    def share_a(px, pz):
        lhs = x_all[pl.ds(8 * px + 4 * pz, 4)].reshape(512, T)
        part_a[px, pz] = share(lhs, 0, WA).reshape(4, 128, WA)

    def share_b(py, pz, pair):
        lhs = jnp.concatenate([x_all[16 * pair + 8 * e + 4 * pz + py] for e in range(2)], axis=0)
        part_b[py, pz, pl.ds(2 * pair, 2)] = share(lhs, WA, WB).reshape(2, 128, WB)

    def share_c(pz, px):
        lhs = x_all[pl.ds(8 * px + 4 * pz, 4)].reshape(512, T)
        both = share(lhs, WA + WB, 2 * WC)
        part_c[0, pz, px] = both[:, :WC].reshape(4, 128, WC)
        for py in range(4):
            part_c[1, pz, py, px] = both[py * 128 : (py + 1) * 128, WC:]

    def x_peer(d):
        return lax.rem(ix + d, 4) * 8 + iz * 4 + iy

    def y_peer(d):
        return ix * 8 + iz * 4 + lax.rem(iy + d, 4)

    def ring_copies(bank, view, inbox, index, peer_of):
        up, down, far = (lax.rem(index + d, 4) for d in (1, 3, 2))

        def ring_copy(slot, target, side, hop):
            return pltpu.make_async_remote_copy(
                src_ref=view(target, side),
                dst_ref=inbox.at[slot],
                send_sem=r_send_sem.at[bank, slot],
                recv_sem=r_recv_sem.at[bank, slot],
                device_id={"seq": peer_of(hop)},
                device_id_type=MESH,
            )

        return (
            ring_copy(0, far, 0, 1),
            ring_copy(1, far, 1, 3),
            ring_copy(2, up, 1, 1),
            ring_copy(3, down, 0, 3),
            ring_copy(4, up, 0, 1),
            ring_copy(5, down, 1, 3),
        )

    def ring_start(copies, first=0, last=4):
        for c in copies[first:last]:
            c.start()

    def ring_middle(copies, view, inbox, index, blocks):
        for slot, there, side in ((0, 1, 0), (1, 3, 1)):
            copies[slot].wait_recv()
            held = view(lax.rem(index + there, 4), side)

            def add(e):
                total = held[e].astype(F32) + inbox[slot, e].astype(F32)
                held[e] = total.astype(BF16)

            loop(blocks, add)
            copies[4 + slot].start()

    def ring_end(copies, view, inbox, index, blocks, store):
        for slot in (2, 3, 4, 5):
            copies[slot].wait_recv()

        def add(e):
            for side, one, two in ((0, 4, 3), (1, 5, 2)):
                total = view(index, side)[e].astype(F32) + (
                    inbox[one, e].astype(F32) + inbox[two, e].astype(F32)
                )
                store(side, e, total)

        loop(blocks, add)

    def view_a(target, side):
        return part_a.at[target, side]

    def view_b(pair):
        return lambda target, side: part_b.at[target, side, pl.ds(2 * pair, 2)]

    here = chan // 2
    there = 1 - here
    ring_a = (view_a, first_in_a, ix)
    ring_b0 = (view_b(here), first_in_b.at[0], iy)
    ring_b1 = (view_b(there), first_in_b.at[1], iy)
    copies_a = ring_copies(0, *ring_a, x_peer)
    copies_b0 = ring_copies(1, *ring_b0, y_peer)
    copies_b1 = ring_copies(2, *ring_b1, y_peer)

    other = ix * 8 + (1 - iz) * 4 + iy

    def z_copy(slot, held, inbox):
        return pltpu.make_async_remote_copy(
            src_ref=held.at[1 - iz],
            dst_ref=inbox,
            send_sem=z_send_sem.at[slot],
            recv_sem=z_recv_sem.at[slot],
            device_id={"seq": other},
            device_id_type=MESH,
        )

    across = [z_copy(2 + c, part_c.at[c], across_in.at[c]) for c in range(2)]

    def view_c(c):
        return lambda target, side: part_c.at[c, iz, target, pl.ds(2 * side, 2)]

    def second_c(c):
        return lambda target, side: first_out_c.at[c, target, side]

    rings_c = (
        (view_c(0), first_in_c.at[0], ix),
        (view_c(1), first_in_c.at[1], iy),
    )
    rings_e = (
        (second_c(0), second_in_c.at[0], iy),
        (second_c(1), second_in_c.at[1], ix),
    )
    peers_c = (x_peer, y_peer)
    first_c = [ring_copies(5 + c, *rings_c[c], peers_c[c]) for c in range(2)]
    last_c = [ring_copies(7 + c, *rings_e[c], peers_c[1 - c]) for c in range(2)]

    def merge_c(c):
        across[c].wait_recv()

        def add(d):
            total = part_c[c, iz, d].astype(F32) + across_in[c, d].astype(F32)
            part_c[c, iz, d] = total.astype(BF16)

        loop(4, add)
        ring_start(first_c[c])

    def store_c(c):
        def store(side, e, total):
            first_out_c[c, 2 * side + e, 0, 0] = total[:64].astype(BF16)
            first_out_c[c, 2 * side + e, 1, 0] = total[64:].astype(BF16)

        return store

    def final_c(c):
        def store(side, e, total):
            first = WA + WB + c * WC
            rows = slice(64 * side, 64 * side + 64)
            weight_grad_ref[rows, first : first + WC] = total * weight_factor

        return store

    weight_factor = 1.0 / math.sqrt(N * T)

    def shares_b(copies, pair):
        loop(2, lambda z: share_b(lax.rem(iy + 2, 4), z, pair))
        ring_start(copies, 0, 2)
        loop(2, lambda z: share_b(lax.rem(iy + 3 - 2 * z, 4), z, pair))
        ring_start(copies, 2, 4)
        loop(2, lambda z: share_b(lax.rem(iy + 1 + 2 * z, 4), z, pair))

    shares_b(copies_b0, here)
    loop(2, lambda z: share_b(iy, z, here))

    flip = (row_id + col_id == B - 1).astype(BF16)
    for c in range(8):
        piece = mixed_all[PAD + 8 * c : PAD + 8 * c + 8].reshape(B, B)
        mixed_flip[:, c * B : (c + 1) * B] = lax.dot_general(
            flip, piece, (((1,), (1,)), ((), ())), preferred_element_type=F32
        ).astype(BF16)

    def filter_tile(i, m):
        depth = (8 - i) * B
        corr = jnp.dot(
            mixed_flip[:, :depth],
            up_all[pl.ds(m, 8 * (8 - i))].reshape(depth, B),
            preferred_element_type=F32,
        )
        turned = pltpu.roll(corr, 1, 1, stride=1, stride_axis=0)
        above = jnp.where(col_id <= row_id, turned, 0.0)
        below = turned - above
        filt_part[0, m] = jnp.sum(above.reshape(B // 8, 8, B), axis=0)
        filt_part[1, m] = jnp.sum(below.reshape(B // 8, 8, B), axis=0)

    def filter_some(i):
        loop(8, lambda u: filter_tile(i, 8 * i + u))

    filter_some(0)
    ring_middle(copies_b0, *ring_b0, 2)

    x_near.wait_recv()
    x_pass.start()
    filter_some(7)
    filter_some(6)
    x_pass.wait_recv()
    loop(4, lambda px: share_c(1 - iz, px))
    across[0].start()
    across[1].start()
    loop(2, lambda z: share_a(lax.rem(ix + 2, 4), z))
    ring_start(copies_a, 0, 2)
    loop(2, lambda z: share_a(lax.rem(ix + 3 - 2 * z, 4), z))
    ring_start(copies_a, 2, 4)
    loop(2, lambda z: share_a(lax.rem(ix + 1 + 2 * z, 4), z))
    shares_b(copies_b1, there)
    for_peers(me, lambda peer: back_copy(peer).start())
    back_all[:, chan_rows(me), :] = back_send[pl.ds(2 * me, 2)]
    loop(2, lambda z: share_a(ix, z))
    loop(2, lambda z: share_b(iy, z, there))
    loop(4, lambda px: share_c(iz, px))
    filter_some(1)
    ring_middle(copies_a, *ring_a, 4)
    ring_middle(copies_b1, *ring_b1, 2)
    for i in range(2, 6):
        filter_some(i)
    merge_c(0)
    merge_c(1)

    filt_part[1, NB] = jnp.zeros((8, B), F32)
    taps_factor = 1.0 / math.sqrt(GROUP * N * T)

    def filter_rows(s):
        for half in range(2):
            m = 2 * s + half
            both = jnp.sum(filt_part[0, m] + filt_part[1, m + 1], axis=0, keepdims=True)
            filt_send[s, 2 * half : 2 * half + 1, :] = both[:, :128] * taps_factor
            filt_send[s, 2 * half + 1 : 2 * half + 2, :] = both[:, 128:] * taps_factor
        filt_send[s, 4:8, :] = jnp.zeros((4, 128), F32)

    loop(N, filter_rows)
    for_peers(me, lambda peer: filt_copy(peer).start())
    filt_all[me] = filt_send[me]

    wait_all(BACK, lambda peer: back_all.at[:, chan_rows(peer), :], back_send.at[:2])

    def use_back(r):
        rows = pl.ds(pl.multiple_of(r * 128, 128), 128)
        for half in range(2):
            cols = slice(half * B, (half + 1) * B)
            back = back_all[half, rows, :].astype(F32)
            grad_key_ref[rows, cols] = (v_ref[rows, cols].astype(F32) * back).astype(BF16)
            grad_value_ref[rows, cols] = (k_ref[rows, cols].astype(F32) * back).astype(BF16)

    loop(ROWS // 128, use_back)
    stores[2].start()
    stores[3].start()

    def second_view(held):
        return lambda target, side: held.at[target, side]

    ring_c = (second_view(first_out_a), second_in_a, iy)
    ring_d = (second_view(first_out_b), second_in_b, ix)
    copies_c = ring_copies(3, *ring_c, y_peer)
    copies_d = ring_copies(4, *ring_d, x_peer)

    def store_a(side, e, total):
        first_out_a[e, side, 0] = total.astype(BF16)

    def store_b(pair):
        def store(side, e, total):
            first_out_b[2 * pair + e, side, 0] = total.astype(BF16)

        return store

    for c in range(2):
        ring_middle(first_c[c], *rings_c[c], 2)
    ring_end(copies_b0, *ring_b0, 2, store_b(here))
    ring_end(copies_b1, *ring_b1, 2, store_b(there))
    ring_start(copies_d)
    ring_end(copies_a, *ring_a, 4, store_a)
    ring_start(copies_c)
    ring_middle(copies_d, *ring_d, 1)
    ring_middle(copies_c, *ring_c, 1)
    for c in range(2):
        ring_end(first_c[c], *rings_c[c], 2, store_c(c))
        ring_start(last_c[c])

    wait_all(FILT, lambda peer: filt_all.at[peer], filt_send.at[0])
    for g in range(2):
        total = jnp.sum(filt_all[16 * g : 16 * g + 16], axis=0)
        for c in range(4):
            filter_grad_ref[g : g + 1, c * 128 : (c + 1) * 128] = total[c : c + 1, :]

    def keep(held):
        def store(side, e, total):
            held[side] = total.astype(BF16)

        return store

    copy_b = z_copy(1, second_out_b, third_in_b)
    copy_a = z_copy(0, second_out_a, third_in_a)
    ring_end(copies_d, *ring_d, 1, keep(second_out_b))
    copy_b.start()
    ring_end(copies_c, *ring_c, 1, keep(second_out_a))
    copy_a.start()
    for c in range(2):
        ring_middle(last_c[c], *rings_e[c], 1)
    for c in range(2):
        ring_end(last_c[c], *rings_e[c], 1, final_c(c))
    copy_b.wait_recv()
    total = second_out_b[iz].astype(F32) + third_in_b[...].astype(F32)
    weight_grad_ref[:, WA : WA + WB] = total * weight_factor
    copy_a.wait_recv()
    total = second_out_a[iz].astype(F32) + third_in_a[...].astype(F32)
    weight_grad_ref[:, :WA] = total * weight_factor

    for store_out in stores:
        store_out.wait()
    for make in (taps_copy, up_copy, conv_copy, back_copy, filt_copy):
        for_peers(me, lambda peer: make(peer).wait_send())
    rings = (*copies_a, *copies_b0, *copies_b1, *copies_c, *copies_d)
    rings += (*first_c[0], *first_c[1], *last_c[0], *last_c[1], *across)
    for c in (x_core, x_near, x_pass, *rings, copy_a, copy_b):
        c.wait_send()


def hand_over(*refs):
    count = len(refs) // 3
    sources, targets, held = refs[:count], refs[count : 2 * count], refs[2 * count : 3 * count]
    sems = refs[3 * count]
    loads = [pltpu.make_async_copy(sources[c], held[c], sems.at[0, c]) for c in range(count)]
    stores = [pltpu.make_async_copy(held[c], targets[c], sems.at[1, c]) for c in range(count)]
    for load in loads:
        load.start()
    for load, store in zip(loads, stores):
        load.wait()
        store.start()
    for store in stores:
        store.wait()


def per_device(layer_input, query_proj, key_proj, value_proj, filter_taps, grad_out):
    vmem = pl.BlockSpec(memory_space=pltpu.VMEM)
    hbm = pl.BlockSpec(memory_space=pl.ANY)
    rows = jax.ShapeDtypeStruct((ROWS, T), BF16)
    shapes = (
        rows,
        rows,
        rows,
        rows,
        jax.ShapeDtypeStruct((2, T), F32),
        jax.ShapeDtypeStruct((128, ROWS), F32),
    )
    results = pl.pallas_call(
        kernel,
        out_shape=shapes,
        in_specs=[hbm] * 4 + [vmem, hbm],
        out_specs=[hbm] * 4 + [vmem] * 2,
        scratch_shapes=[pltpu.VMEM((ROWS, T), BF16)] * 8
        + [
            pltpu.VMEM((2, ROWS, B), BF16),
            pltpu.VMEM((2, ROWS, B), BF16),
            pltpu.VMEM((2, 8, 128), F32),
            pltpu.VMEM((N, 8, 128), F32),
            pltpu.VMEM((PAD + NB, CH, B), BF16),
            pltpu.VMEM((NB + PAD, CH, B), BF16),
            pltpu.VMEM((B, NB * CH), BF16),
            pltpu.VMEM((NB, B, B), BF16),
            pltpu.VMEM((2 * B, B), F32),
            pltpu.VMEM((NB, CH, B), BF16),
            pltpu.VMEM((NB, CH, B), BF16),
            pltpu.VMEM((2, ROWS, B), BF16),
            pltpu.VMEM((2, ROWS, B), BF16),
            pltpu.VMEM((2, NB + 1, 8, B), F32),
            pltpu.VMEM((N, 8, 128), F32),
            pltpu.VMEM((N, 8, 128), F32),
            pltpu.VMEM((N, 128, T), BF16),
            pltpu.VMEM((4, 2, 4, 128, WA), BF16),
            pltpu.VMEM((4, 2, 4, 128, WB), BF16),
            pltpu.VMEM((6, 4, 128, WA), BF16),
            pltpu.VMEM((2, 6, 2, 128, WB), BF16),
            pltpu.VMEM((4, 2, 1, 128, WA), BF16),
            pltpu.VMEM((4, 2, 1, 128, WB), BF16),
            pltpu.VMEM((6, 1, 128, WA), BF16),
            pltpu.VMEM((6, 1, 128, WB), BF16),
            pltpu.VMEM((2, 128, WA), BF16),
            pltpu.VMEM((2, 128, WB), BF16),
            pltpu.VMEM((128, WA), BF16),
            pltpu.VMEM((128, WB), BF16),
            pltpu.VMEM((2, 2, 4, 4, 128, WC), BF16),
            pltpu.VMEM((2, 4, 4, 128, WC), BF16),
            pltpu.VMEM((2, 6, 2, 128, WC), BF16),
            pltpu.VMEM((2, 4, 2, 1, 64, WC), BF16),
            pltpu.VMEM((2, 6, 1, 64, WC), BF16),
            pltpu.SemaphoreType.DMA((KINDS, N)),
            pltpu.SemaphoreType.DMA((KINDS, N)),
            pltpu.SemaphoreType.DMA((3,)),
            pltpu.SemaphoreType.DMA((3,)),
            pltpu.SemaphoreType.DMA((9, 6)),
            pltpu.SemaphoreType.DMA((9, 6)),
            pltpu.SemaphoreType.DMA((4,)),
            pltpu.SemaphoreType.DMA((4,)),
            pltpu.SemaphoreType.DMA((5,)),
            pltpu.SemaphoreType.DMA((4,)),
        ],
        compiler_params=pltpu.CompilerParams(
            collective_id=0, has_side_effects=True, vmem_limit_bytes=62 * 2**20
        ),
    )(
        layer_input.reshape(8, 128, T),
        query_proj,
        key_proj,
        value_proj,
        filter_taps,
        grad_out,
    )
    return tuple(
        pl.pallas_call(
            hand_over,
            out_shape=shapes,
            in_specs=[hbm] * 6,
            out_specs=[hbm] * 6,
            scratch_shapes=[pltpu.VMEM(shape.shape, shape.dtype) for shape in shapes]
            + [pltpu.SemaphoreType.DMA((2, 6))],
        )(*results)
    )


def solution(mesh):
    placed = (P("chan", "seq"),) * 6
    return jax.shard_map(
        per_device,
        mesh=mesh,
        in_specs=placed,
        out_specs=(P("chan", "seq"),) * 5 + (P("seq", "chan"),),
        check_vma=False,
    )
```

```python
import functools
import math

import jax
import jax.numpy as jnp
from jax import lax
from jax.experimental import pallas as pl
from jax.experimental.pallas import tpu as pltpu
from jax.sharding import PartitionSpec as P

GROUP = 512
F32 = jnp.float32
BF16 = jnp.bfloat16
MESH = pl.DeviceIdType.MESH

N = 32
CH = 32
T = 512
B = 256
NB = N * T // B
PAD = 8
ROWS = N * CH
WA = 384
WB = ROWS - WA
KINDS = 6
MIXED, UP, TAPS, CONV, BACK, FILT = range(KINDS)


def seq_copy(src, dst, kind, peer, sems, me):
    send, recv = sems
    return pltpu.make_async_remote_copy(
        src_ref=src,
        dst_ref=dst,
        send_sem=send.at[kind, peer],
        recv_sem=recv.at[kind, me],
        device_id={"seq": peer},
        device_id_type=MESH,
    )


def for_peers(me, body):
    def step(i, carry):
        body(lax.rem(me + i, N))
        return carry

    lax.fori_loop(1, N, step, 0)


def loop(n, body, start=0):
    def step(i, carry):
        body(i)
        return carry

    lax.fori_loop(start, n, step, 0)


def kernel(
    x_hbm,
    q_hbm,
    k_hbm,
    v_hbm,
    taps_ref,
    g_hbm,
    mixed_out_hbm,
    grad_query_hbm,
    grad_key_hbm,
    grad_value_hbm,
    filter_grad_ref,
    weight_grad_ref,
    q_ref,
    k_ref,
    v_ref,
    g_ref,
    mixed_out_ref,
    grad_query_ref,
    grad_key_ref,
    grad_value_ref,
    mixed_send,
    up_send,
    taps_send,
    taps_all,
    mixed_all,
    up_all,
    mixed_flip,
    toeplitz,
    acc,
    conv_send,
    back_send,
    conv_all,
    back_all,
    filt_part,
    filt_send,
    filt_all,
    x_all,
    part_a,
    part_b,
    first_in_a,
    first_in_b,
    first_out_a,
    first_out_b,
    second_in_a,
    second_in_b,
    second_out_a,
    second_out_b,
    third_in_a,
    third_in_b,
    send_sem,
    recv_sem,
    x_send_sem,
    x_recv_sem,
    r_send_sem,
    r_recv_sem,
    z_send_sem,
    z_recv_sem,
    in_sem,
    out_sem,
):
    me = lax.axis_index("seq")
    chan = lax.axis_index("chan")
    ix = me // 8
    iz = lax.rem(me // 4, 2)
    iy = lax.rem(me, 4)
    sems = (send_sem, recv_sem)

    own_x = pl.ds(chan * 8, 8)
    loads = [
        pltpu.make_async_copy(src, dst, in_sem.at[slot])
        for slot, (src, dst) in enumerate(
            (
                (k_hbm, k_ref),
                (v_hbm, v_ref),
                (g_hbm, g_ref),
                (q_hbm, q_ref),
                (x_hbm, x_all.at[own_x]),
            )
        )
    ]
    for load in loads:
        load.start()
    stores = [
        pltpu.make_async_copy(src, dst, out_sem.at[slot])
        for slot, (src, dst) in enumerate(
            (
                (mixed_out_ref, mixed_out_hbm),
                (grad_query_ref, grad_query_hbm),
                (grad_key_ref, grad_key_hbm),
                (grad_value_ref, grad_value_hbm),
            )
        )
    ]

    barrier = pltpu.get_barrier_semaphore()
    for_peers(
        me,
        lambda peer: pl.semaphore_signal(
            barrier, inc=1, device_id={"seq": peer}, device_id_type=MESH
        ),
    )
    core_peer = chan + 1 - 2 * lax.rem(chan, 2)
    near_peer = lax.rem(chan + 2, 4)
    for peer in (core_peer, near_peer):
        pl.semaphore_signal(barrier, inc=1, device_id={"chan": peer}, device_id_type=MESH)

    def make_mixed(r):
        rows = pl.ds(pl.multiple_of(r * 128, 128), 128)
        prod = (k_ref[rows, :].astype(F32) * v_ref[rows, :].astype(F32)).astype(BF16)
        mixed_send[0, rows, :] = prod[:, :B]
        mixed_send[1, rows, :] = prod[:, B:]

    def make_up(r):
        rows = pl.ds(pl.multiple_of(r * 128, 128), 128)
        prod = (g_ref[rows, :].astype(F32) * q_ref[rows, :].astype(F32)).astype(BF16)
        up_send[0, rows, :] = prod[:, :B]
        up_send[1, rows, :] = prod[:, B:]

    for g in range(2):
        for c in range(4):
            taps_send[g, c : c + 1, :] = taps_ref[g : g + 1, c * 128 : (c + 1) * 128]
        taps_send[g, 4:8, :] = jnp.zeros((4, 128), F32)
    loads[0].wait()
    loads[1].wait()
    loop(ROWS // 128, make_mixed)
    pl.semaphore_wait(barrier, N + 1)

    def chan_rows(peer):
        return pl.ds(pl.multiple_of(peer * CH, CH), CH)

    def taps_copy(peer):
        return seq_copy(taps_send.at[peer // 16], taps_all.at[me], TAPS, peer, sems, me)

    def mixed_copy(peer):
        return seq_copy(
            mixed_send.at[:, chan_rows(peer), :],
            mixed_all.at[pl.ds(PAD + 2 * me, 2)],
            MIXED,
            peer,
            sems,
            me,
        )

    def up_copy(peer):
        return seq_copy(
            up_send.at[:, chan_rows(peer), :],
            up_all.at[pl.ds(2 * me, 2)],
            UP,
            peer,
            sems,
            me,
        )

    def conv_copy(peer):
        return seq_copy(
            conv_send.at[pl.ds(2 * peer, 2)],
            conv_all.at[:, chan_rows(me), :],
            CONV,
            peer,
            sems,
            me,
        )

    def back_copy(peer):
        return seq_copy(
            back_send.at[pl.ds(2 * peer, 2)],
            back_all.at[:, chan_rows(me), :],
            BACK,
            peer,
            sems,
            me,
        )

    def filt_copy(peer):
        return seq_copy(filt_send.at[peer], filt_all.at[me], FILT, peer, sems, me)

    def wait_all(kind, dst_of, src_any):
        def one(peer):
            pltpu.make_async_remote_copy(
                src_ref=src_any,
                dst_ref=dst_of(peer),
                send_sem=send_sem.at[kind, peer],
                recv_sem=recv_sem.at[kind, peer],
                device_id={"seq": peer},
                device_id_type=MESH,
            ).wait_recv()

        for_peers(me, one)

    near_x = pl.ds(near_peer * 8, 8)

    def x_copy(slot, src, rows, peer):
        return pltpu.make_async_remote_copy(
            src_ref=src,
            dst_ref=x_all.at[rows],
            send_sem=x_send_sem.at[slot],
            recv_sem=x_recv_sem.at[slot],
            device_id={"chan": peer},
            device_id_type=MESH,
        )

    x_core = x_copy(0, x_hbm, own_x, core_peer)
    x_near = x_copy(1, x_hbm, own_x, near_peer)
    x_pass = x_copy(2, x_all.at[near_x], near_x, core_peer)

    for_peers(me, lambda peer: taps_copy(peer).start())
    for_peers(me, lambda peer: mixed_copy(peer).start())
    x_core.start()
    loads[2].wait()
    loads[3].wait()
    loop(ROWS // 128, make_up)

    taps_all[me] = taps_send[me // 16]
    mixed_all[pl.ds(PAD + 2 * me, 2)] = mixed_send[:, chan_rows(me), :]
    up_all[pl.ds(2 * me, 2)] = up_send[:, chan_rows(me), :]
    mixed_all[:PAD] = jnp.zeros((PAD, CH, B), BF16)
    up_all[NB:] = jnp.zeros((PAD, CH, B), BF16)

    wait_all(TAPS, lambda peer: taps_all.at[peer], taps_send.at[0])
    row_id = lax.broadcasted_iota(jnp.int32, (B, B), 0)
    col_id = lax.broadcasted_iota(jnp.int32, (B, B), 1)

    def sheared(src, half):
        piece = taps_all[src]
        wide = jnp.concatenate(
            [piece[2 * half : 2 * half + 1, :], piece[2 * half + 1 : 2 * half + 2, :]], axis=1
        )
        return pltpu.roll(jnp.broadcast_to(wide, (B, B)), 0, 1, stride=1, stride_axis=0)

    acc[:B] = jnp.zeros((B, B), F32)

    def make_tiles(s):
        for half in range(2):
            now = sheared(s, half)
            toeplitz[2 * s + half] = jnp.where(col_id >= row_id, now, acc[:B]).astype(BF16)
            acc[:B] = now

    loop(N, make_tiles)

    for_peers(me, lambda peer: mixed_copy(peer).wait_send())
    for_peers(me, lambda peer: up_copy(peer).start())

    wait_all(MIXED, lambda peer: mixed_all.at[pl.ds(PAD + 2 * peer, 2)], mixed_send.at[:, :CH, :])

    def hand_back(i, copy, send, dest):
        for r in range(8):
            peer = 8 * i + r

            @pl.when(peer != me)
            def _():
                copy(peer).start()

            @pl.when(peer == me)
            def _():
                dest[:, chan_rows(me), :] = send[pl.ds(2 * me, 2)]

    def conv_chunk(step):
        i = lax.rem(ix + step, 4)
        acc[...] = jnp.zeros((2 * B, B), F32)

        def some(j, first, blocks):
            part = None
            for u in range(8):
                m = 8 * j + u
                lhs = mixed_all[pl.ds(PAD + first - m, blocks)].reshape(blocks * CH, B)
                term = jnp.dot(lhs, toeplitz[m], preferred_element_type=F32)
                part = term if part is None else part + term
            return part

        def full(j):
            acc[...] += some(j, 16 * i, 16)

        loop(2 * i + 1, full)
        acc[B:] += some(2 * i + 1, 16 * i + 8, 8)
        conv_send[pl.ds(16 * i, 16)] = acc[...].astype(BF16).reshape(16, CH, B)
        hand_back(i, conv_copy, conv_send, conv_all)

    loop(4, conv_chunk)
    x_near.start()

    wait_all(UP, lambda peer: up_all.at[pl.ds(2 * peer, 2)], up_send.at[:, :CH, :])

    def back_chunk(step):
        i = lax.rem(ix + step, 4)
        acc[...] = jnp.zeros((2 * B, B), F32)

        def some(j, blocks):
            part = None
            for u in range(8):
                m = 8 * j + u
                lhs = up_all[pl.ds(16 * i + m, blocks)].reshape(blocks * CH, B)
                term = lax.dot_general(
                    lhs, toeplitz[m], (((1,), (1,)), ((), ())), preferred_element_type=F32
                )
                part = term if part is None else part + term
            return part

        def full(j):
            acc[...] += some(j, 16)

        loop(7 - 2 * i, full)
        acc[:B] += some(7 - 2 * i, 8)
        back_send[pl.ds(16 * i, 16)] = acc[...].astype(BF16).reshape(16, CH, B)

    loop(4, back_chunk)

    wait_all(CONV, lambda peer: conv_all.at[:, chan_rows(peer), :], conv_send.at[:2])
    for_peers(me, lambda peer: back_copy(peer).start())
    back_all[:, chan_rows(me), :] = back_send[pl.ds(2 * me, 2)]

    def use_conv(r):
        rows = pl.ds(pl.multiple_of(r * 128, 128), 128)
        for half in range(2):
            cols = slice(half * B, (half + 1) * B)
            conv = conv_all[half, rows, :].astype(F32)
            grad_query_ref[rows, cols] = (g_ref[rows, cols].astype(F32) * conv).astype(BF16)
            mixed_out_ref[rows, cols] = (q_ref[rows, cols].astype(F32) * conv).astype(BF16)

    loop(ROWS // 128, use_conv)
    stores[0].start()
    stores[1].start()
    loads[4].wait()
    x_core.wait_recv()

    def share(lhs, first, count):
        return lax.dot_general(
            lhs,
            grad_query_ref[first : first + count, :],
            (((1,), (1,)), ((), ())),
            preferred_element_type=F32,
        ).astype(BF16)

    def share_a(px, pz):
        lhs = x_all[pl.ds(8 * px + 4 * pz, 4)].reshape(512, T)
        part_a[px, pz] = share(lhs, 0, WA).reshape(4, 128, WA)

    def share_b(py, pz, pair):
        lhs = jnp.concatenate([x_all[16 * pair + 8 * e + 4 * pz + py] for e in range(2)], axis=0)
        part_b[py, pz, pl.ds(2 * pair, 2)] = share(lhs, WA, WB).reshape(2, 128, WB)

    def x_peer(d):
        return lax.rem(ix + d, 4) * 8 + iz * 4 + iy

    def y_peer(d):
        return ix * 8 + iz * 4 + lax.rem(iy + d, 4)

    def ring_copies(bank, view, inbox, index, peer_of):
        up, down, far = (lax.rem(index + d, 4) for d in (1, 3, 2))

        def ring_copy(slot, target, side, hop):
            return pltpu.make_async_remote_copy(
                src_ref=view(target, side),
                dst_ref=inbox.at[slot],
                send_sem=r_send_sem.at[bank, slot],
                recv_sem=r_recv_sem.at[bank, slot],
                device_id={"seq": peer_of(hop)},
                device_id_type=MESH,
            )

        return (
            ring_copy(0, far, 0, 1),
            ring_copy(1, far, 1, 3),
            ring_copy(2, up, 1, 1),
            ring_copy(3, down, 0, 3),
            ring_copy(4, up, 0, 1),
            ring_copy(5, down, 1, 3),
        )

    def ring_start(copies, first=0, last=4):
        for c in copies[first:last]:
            c.start()

    def ring_middle(copies, view, inbox, index, blocks):
        for slot, there, side in ((0, 1, 0), (1, 3, 1)):
            copies[slot].wait_recv()
            held = view(lax.rem(index + there, 4), side)

            def add(e):
                total = held[e].astype(F32) + inbox[slot, e].astype(F32)
                held[e] = total.astype(BF16)

            loop(blocks, add)
            copies[4 + slot].start()

    def ring_end(copies, view, inbox, index, blocks, store):
        for slot in (2, 3, 4, 5):
            copies[slot].wait_recv()

        def add(e):
            for side, one, two in ((0, 4, 3), (1, 5, 2)):
                total = view(index, side)[e].astype(F32) + (
                    inbox[one, e].astype(F32) + inbox[two, e].astype(F32)
                )
                store(side, e, total)

        loop(blocks, add)

    def view_a(target, side):
        return part_a.at[target, side]

    def view_b(pair):
        return lambda target, side: part_b.at[target, side, pl.ds(2 * pair, 2)]

    here = chan // 2
    there = 1 - here
    ring_a = (view_a, first_in_a, ix)
    ring_b0 = (view_b(here), first_in_b.at[0], iy)
    ring_b1 = (view_b(there), first_in_b.at[1], iy)
    copies_a = ring_copies(0, *ring_a, x_peer)
    copies_b0 = ring_copies(1, *ring_b0, y_peer)
    copies_b1 = ring_copies(2, *ring_b1, y_peer)

    def shares_b(copies, pair):
        loop(2, lambda z: share_b(lax.rem(iy + 2, 4), z, pair))
        ring_start(copies, 0, 2)
        loop(2, lambda z: share_b(lax.rem(iy + 3 - 2 * z, 4), z, pair))
        ring_start(copies, 2, 4)
        loop(2, lambda z: share_b(lax.rem(iy + 1 + 2 * z, 4), z, pair))

    shares_b(copies_b0, here)
    loop(2, lambda z: share_b(iy, z, here))

    flip = (row_id + col_id == B - 1).astype(BF16)
    for c in range(8):
        piece = mixed_all[PAD + 8 * c : PAD + 8 * c + 8].reshape(B, B)
        mixed_flip[:, c * B : (c + 1) * B] = lax.dot_general(
            flip, piece, (((1,), (1,)), ((), ())), preferred_element_type=F32
        ).astype(BF16)

    def filter_tile(i, m):
        depth = (8 - i) * B
        corr = jnp.dot(
            mixed_flip[:, :depth],
            up_all[pl.ds(m, 8 * (8 - i))].reshape(depth, B),
            preferred_element_type=F32,
        )
        turned = pltpu.roll(corr, 1, 1, stride=1, stride_axis=0)
        above = jnp.where(col_id <= row_id, turned, 0.0)
        below = turned - above
        filt_part[0, m] = jnp.sum(above.reshape(B // 8, 8, B), axis=0)
        filt_part[1, m] = jnp.sum(below.reshape(B // 8, 8, B), axis=0)

    def filter_some(i):
        loop(8, lambda u: filter_tile(i, 8 * i + u))


    x_near.wait_recv()
    x_pass.start()
    filter_some(7)
    filter_some(6)
    x_pass.wait_recv()
    loop(2, lambda z: share_a(lax.rem(ix + 2, 4), z))
    ring_start(copies_a, 0, 2)
    loop(2, lambda z: share_a(lax.rem(ix + 3 - 2 * z, 4), z))
    ring_start(copies_a, 2, 4)
    loop(2, lambda z: share_a(lax.rem(ix + 1 + 2 * z, 4), z))
    shares_b(copies_b1, there)
    loop(2, lambda z: share_a(ix, z))
    loop(2, lambda z: share_b(iy, z, there))
    ring_middle(copies_b0, *ring_b0, 2)
    filter_some(0)
    filter_some(4)
    ring_middle(copies_a, *ring_a, 4)
    ring_middle(copies_b1, *ring_b1, 2)
    for i in (1, 2, 3, 5):
        filter_some(i)

    filt_part[1, NB] = jnp.zeros((8, B), F32)
    taps_factor = 1.0 / math.sqrt(GROUP * N * T)

    def filter_rows(s):
        for half in range(2):
            m = 2 * s + half
            both = jnp.sum(filt_part[0, m] + filt_part[1, m + 1], axis=0, keepdims=True)
            filt_send[s, 2 * half : 2 * half + 1, :] = both[:, :128] * taps_factor
            filt_send[s, 2 * half + 1 : 2 * half + 2, :] = both[:, 128:] * taps_factor
        filt_send[s, 4:8, :] = jnp.zeros((4, 128), F32)

    loop(N, filter_rows)
    for_peers(me, lambda peer: filt_copy(peer).start())
    filt_all[me] = filt_send[me]

    wait_all(BACK, lambda peer: back_all.at[:, chan_rows(peer), :], back_send.at[:2])

    def use_back(r):
        rows = pl.ds(pl.multiple_of(r * 128, 128), 128)
        for half in range(2):
            cols = slice(half * B, (half + 1) * B)
            back = back_all[half, rows, :].astype(F32)
            grad_key_ref[rows, cols] = (v_ref[rows, cols].astype(F32) * back).astype(BF16)
            grad_value_ref[rows, cols] = (k_ref[rows, cols].astype(F32) * back).astype(BF16)

    loop(ROWS // 128, use_back)
    stores[2].start()
    stores[3].start()

    def second_view(held):
        return lambda target, side: held.at[target, side]

    ring_c = (second_view(first_out_a), second_in_a, iy)
    ring_d = (second_view(first_out_b), second_in_b, ix)
    copies_c = ring_copies(3, *ring_c, y_peer)
    copies_d = ring_copies(4, *ring_d, x_peer)

    def store_a(side, e, total):
        first_out_a[e, side, 0] = total.astype(BF16)

    def store_b(pair):
        def store(side, e, total):
            first_out_b[2 * pair + e, side, 0] = total.astype(BF16)

        return store

    ring_end(copies_b0, *ring_b0, 2, store_b(here))
    ring_end(copies_b1, *ring_b1, 2, store_b(there))
    ring_start(copies_d)
    ring_end(copies_a, *ring_a, 4, store_a)
    ring_start(copies_c)
    ring_middle(copies_d, *ring_d, 1)
    ring_middle(copies_c, *ring_c, 1)

    wait_all(FILT, lambda peer: filt_all.at[peer], filt_send.at[0])
    for g in range(2):
        total = jnp.sum(filt_all[16 * g : 16 * g + 16], axis=0)
        for c in range(4):
            filter_grad_ref[g : g + 1, c * 128 : (c + 1) * 128] = total[c : c + 1, :]

    other = ix * 8 + (1 - iz) * 4 + iy

    def z_copy(slot, held, inbox):
        return pltpu.make_async_remote_copy(
            src_ref=held.at[1 - iz],
            dst_ref=inbox,
            send_sem=z_send_sem.at[slot],
            recv_sem=z_recv_sem.at[slot],
            device_id={"seq": other},
            device_id_type=MESH,
        )

    def keep(held):
        def store(side, e, total):
            held[side] = total.astype(BF16)

        return store

    copy_b = z_copy(1, second_out_b, third_in_b)
    copy_a = z_copy(0, second_out_a, third_in_a)
    ring_end(copies_d, *ring_d, 1, keep(second_out_b))
    copy_b.start()
    ring_end(copies_c, *ring_c, 1, keep(second_out_a))
    copy_a.start()
    weight_factor = 1.0 / math.sqrt(N * T)
    copy_b.wait_recv()
    total = second_out_b[iz].astype(F32) + third_in_b[...].astype(F32)
    weight_grad_ref[:, WA:] = total * weight_factor
    copy_a.wait_recv()
    total = second_out_a[iz].astype(F32) + third_in_a[...].astype(F32)
    weight_grad_ref[:, :WA] = total * weight_factor

    for store_out in stores:
        store_out.wait()
    for make in (taps_copy, up_copy, conv_copy, back_copy, filt_copy):
        for_peers(me, lambda peer: make(peer).wait_send())
    rings = (*copies_a, *copies_b0, *copies_b1, *copies_c, *copies_d)
    for c in (x_core, x_near, x_pass, *rings, copy_a, copy_b):
        c.wait_send()


def hand_over(*refs):
    count = len(refs) // 3
    sources, targets, held = refs[:count], refs[count : 2 * count], refs[2 * count : 3 * count]
    sems = refs[3 * count]
    loads = [pltpu.make_async_copy(sources[c], held[c], sems.at[0, c]) for c in range(count)]
    stores = [pltpu.make_async_copy(held[c], targets[c], sems.at[1, c]) for c in range(count)]
    for load in loads:
        load.start()
    for load, store in zip(loads, stores):
        load.wait()
        store.start()
    for store in stores:
        store.wait()


def per_device(layer_input, query_proj, key_proj, value_proj, filter_taps, grad_out):
    vmem = pl.BlockSpec(memory_space=pltpu.VMEM)
    hbm = pl.BlockSpec(memory_space=pl.ANY)
    rows = jax.ShapeDtypeStruct((ROWS, T), BF16)
    shapes = (
        rows,
        rows,
        rows,
        rows,
        jax.ShapeDtypeStruct((2, T), F32),
        jax.ShapeDtypeStruct((128, ROWS), F32),
    )
    results = pl.pallas_call(
        kernel,
        out_shape=shapes,
        in_specs=[hbm] * 4 + [vmem, hbm],
        out_specs=[hbm] * 4 + [vmem] * 2,
        scratch_shapes=[pltpu.VMEM((ROWS, T), BF16)] * 8
        + [
            pltpu.VMEM((2, ROWS, B), BF16),
            pltpu.VMEM((2, ROWS, B), BF16),
            pltpu.VMEM((2, 8, 128), F32),
            pltpu.VMEM((N, 8, 128), F32),
            pltpu.VMEM((PAD + NB, CH, B), BF16),
            pltpu.VMEM((NB + PAD, CH, B), BF16),
            pltpu.VMEM((B, NB * CH), BF16),
            pltpu.VMEM((NB, B, B), BF16),
            pltpu.VMEM((2 * B, B), F32),
            pltpu.VMEM((NB, CH, B), BF16),
            pltpu.VMEM((NB, CH, B), BF16),
            pltpu.VMEM((2, ROWS, B), BF16),
            pltpu.VMEM((2, ROWS, B), BF16),
            pltpu.VMEM((2, NB + 1, 8, B), F32),
            pltpu.VMEM((N, 8, 128), F32),
            pltpu.VMEM((N, 8, 128), F32),
            pltpu.VMEM((N, 128, T), BF16),
            pltpu.VMEM((4, 2, 4, 128, WA), BF16),
            pltpu.VMEM((4, 2, 4, 128, WB), BF16),
            pltpu.VMEM((6, 4, 128, WA), BF16),
            pltpu.VMEM((2, 6, 2, 128, WB), BF16),
            pltpu.VMEM((4, 2, 1, 128, WA), BF16),
            pltpu.VMEM((4, 2, 1, 128, WB), BF16),
            pltpu.VMEM((6, 1, 128, WA), BF16),
            pltpu.VMEM((6, 1, 128, WB), BF16),
            pltpu.VMEM((2, 128, WA), BF16),
            pltpu.VMEM((2, 128, WB), BF16),
            pltpu.VMEM((128, WA), BF16),
            pltpu.VMEM((128, WB), BF16),
            pltpu.SemaphoreType.DMA((KINDS, N)),
            pltpu.SemaphoreType.DMA((KINDS, N)),
            pltpu.SemaphoreType.DMA((3,)),
            pltpu.SemaphoreType.DMA((3,)),
            pltpu.SemaphoreType.DMA((5, 6)),
            pltpu.SemaphoreType.DMA((5, 6)),
            pltpu.SemaphoreType.DMA((2,)),
            pltpu.SemaphoreType.DMA((2,)),
            pltpu.SemaphoreType.DMA((5,)),
            pltpu.SemaphoreType.DMA((4,)),
        ],
        compiler_params=pltpu.CompilerParams(
            collective_id=0, has_side_effects=True, vmem_limit_bytes=62 * 2**20
        ),
    )(
        layer_input.reshape(8, 128, T),
        query_proj,
        key_proj,
        value_proj,
        filter_taps,
        grad_out,
    )
    return tuple(
        pl.pallas_call(
            hand_over,
            out_shape=shapes,
            in_specs=[hbm] * 6,
            out_specs=[hbm] * 6,
            scratch_shapes=[pltpu.VMEM(shape.shape, shape.dtype) for shape in shapes]
            + [pltpu.SemaphoreType.DMA((2, 6))],
        )(*results)
    )


def solution(mesh):
    placed = (P("chan", "seq"),) * 6
    return jax.shard_map(
        per_device,
        mesh=mesh,
        in_specs=placed,
        out_specs=(P("chan", "seq"),) * 5 + (P("seq", "chan"),),
        check_vma=False,
    )
```

```python
import functools
import math

import jax
import jax.numpy as jnp
from jax import lax
from jax.experimental import pallas as pl
from jax.experimental.pallas import tpu as pltpu
from jax.sharding import PartitionSpec as P

GROUP = 512
F32 = jnp.float32
BF16 = jnp.bfloat16
MESH = pl.DeviceIdType.MESH

N = 32
CH = 32
T = 512
B = 256
NB = N * T // B
PAD = 8
ROWS = N * CH
WA = 256
WB = 512
WC = (ROWS - WA - WB) // 2
KINDS = 6
MIXED, UP, TAPS, CONV, BACK, FILT = range(KINDS)


def seq_copy(src, dst, kind, peer, sems, me):
    send, recv = sems
    return pltpu.make_async_remote_copy(
        src_ref=src,
        dst_ref=dst,
        send_sem=send.at[kind, peer],
        recv_sem=recv.at[kind, me],
        device_id={"seq": peer},
        device_id_type=MESH,
    )


def for_peers(me, body):
    def step(i, carry):
        body(lax.rem(me + i, N))
        return carry

    lax.fori_loop(1, N, step, 0)


def loop(n, body, start=0):
    def step(i, carry):
        body(i)
        return carry

    lax.fori_loop(start, n, step, 0)


def kernel(
    x_hbm,
    q_hbm,
    k_hbm,
    v_hbm,
    taps_ref,
    g_hbm,
    mixed_out_hbm,
    grad_query_hbm,
    grad_key_hbm,
    grad_value_hbm,
    filter_grad_ref,
    weight_grad_ref,
    q_ref,
    k_ref,
    v_ref,
    g_ref,
    mixed_out_ref,
    grad_query_ref,
    grad_key_ref,
    grad_value_ref,
    mixed_send,
    up_send,
    taps_send,
    taps_all,
    mixed_all,
    up_all,
    mixed_flip,
    toeplitz,
    acc,
    conv_send,
    back_send,
    conv_all,
    back_all,
    filt_part,
    filt_send,
    filt_all,
    x_all,
    part_a,
    part_b,
    first_in_a,
    first_in_b,
    first_out_a,
    first_out_b,
    second_in_a,
    second_in_b,
    second_out_a,
    second_out_b,
    third_in_a,
    third_in_b,
    part_c,
    across_in,
    first_in_c,
    first_out_c,
    second_in_c,
    send_sem,
    recv_sem,
    x_send_sem,
    x_recv_sem,
    r_send_sem,
    r_recv_sem,
    z_send_sem,
    z_recv_sem,
    in_sem,
    out_sem,
):
    me = lax.axis_index("seq")
    chan = lax.axis_index("chan")
    ix = me // 8
    iz = lax.rem(me // 4, 2)
    iy = lax.rem(me, 4)
    sems = (send_sem, recv_sem)

    own_x = pl.ds(chan * 8, 8)
    loads = [
        pltpu.make_async_copy(src, dst, in_sem.at[slot])
        for slot, (src, dst) in enumerate(
            (
                (k_hbm, k_ref),
                (v_hbm, v_ref),
                (g_hbm, g_ref),
                (q_hbm, q_ref),
                (x_hbm, x_all.at[own_x]),
            )
        )
    ]
    for load in loads:
        load.start()
    stores = [
        pltpu.make_async_copy(src, dst, out_sem.at[slot])
        for slot, (src, dst) in enumerate(
            (
                (mixed_out_ref, mixed_out_hbm),
                (grad_query_ref, grad_query_hbm),
                (grad_key_ref, grad_key_hbm),
                (grad_value_ref, grad_value_hbm),
            )
        )
    ]

    barrier = pltpu.get_barrier_semaphore()
    for_peers(
        me,
        lambda peer: pl.semaphore_signal(
            barrier, inc=1, device_id={"seq": peer}, device_id_type=MESH
        ),
    )
    core_peer = chan + 1 - 2 * lax.rem(chan, 2)
    near_peer = lax.rem(chan + 2, 4)
    for peer in (core_peer, near_peer):
        pl.semaphore_signal(barrier, inc=1, device_id={"chan": peer}, device_id_type=MESH)

    def make_mixed(r):
        rows = pl.ds(pl.multiple_of(r * 128, 128), 128)
        prod = (k_ref[rows, :].astype(F32) * v_ref[rows, :].astype(F32)).astype(BF16)
        mixed_send[0, rows, :] = prod[:, :B]
        mixed_send[1, rows, :] = prod[:, B:]

    def make_up(r):
        rows = pl.ds(pl.multiple_of(r * 128, 128), 128)
        prod = (g_ref[rows, :].astype(F32) * q_ref[rows, :].astype(F32)).astype(BF16)
        up_send[0, rows, :] = prod[:, :B]
        up_send[1, rows, :] = prod[:, B:]

    for g in range(2):
        for c in range(4):
            taps_send[g, c : c + 1, :] = taps_ref[g : g + 1, c * 128 : (c + 1) * 128]
        taps_send[g, 4:8, :] = jnp.zeros((4, 128), F32)
    loads[0].wait()
    loads[1].wait()
    loop(ROWS // 128, make_mixed)
    pl.semaphore_wait(barrier, N + 1)

    def chan_rows(peer):
        return pl.ds(pl.multiple_of(peer * CH, CH), CH)

    def taps_copy(peer):
        return seq_copy(taps_send.at[peer // 16], taps_all.at[me], TAPS, peer, sems, me)

    def mixed_copy(peer):
        return seq_copy(
            mixed_send.at[:, chan_rows(peer), :],
            mixed_all.at[pl.ds(PAD + 2 * me, 2)],
            MIXED,
            peer,
            sems,
            me,
        )

    def up_copy(peer):
        return seq_copy(
            up_send.at[:, chan_rows(peer), :],
            up_all.at[pl.ds(2 * me, 2)],
            UP,
            peer,
            sems,
            me,
        )

    def conv_copy(peer):
        return seq_copy(
            conv_send.at[pl.ds(2 * peer, 2)],
            conv_all.at[:, chan_rows(me), :],
            CONV,
            peer,
            sems,
            me,
        )

    def back_copy(peer):
        return seq_copy(
            back_send.at[pl.ds(2 * peer, 2)],
            back_all.at[:, chan_rows(me), :],
            BACK,
            peer,
            sems,
            me,
        )

    def filt_copy(peer):
        return seq_copy(filt_send.at[peer], filt_all.at[me], FILT, peer, sems, me)

    def wait_all(kind, dst_of, src_any):
        def one(peer):
            pltpu.make_async_remote_copy(
                src_ref=src_any,
                dst_ref=dst_of(peer),
                send_sem=send_sem.at[kind, peer],
                recv_sem=recv_sem.at[kind, peer],
                device_id={"seq": peer},
                device_id_type=MESH,
            ).wait_recv()

        for_peers(me, one)

    near_x = pl.ds(near_peer * 8, 8)

    def x_copy(slot, src, rows, peer):
        return pltpu.make_async_remote_copy(
            src_ref=src,
            dst_ref=x_all.at[rows],
            send_sem=x_send_sem.at[slot],
            recv_sem=x_recv_sem.at[slot],
            device_id={"chan": peer},
            device_id_type=MESH,
        )

    x_core = x_copy(0, x_hbm, own_x, core_peer)
    x_near = x_copy(1, x_hbm, own_x, near_peer)
    x_pass = x_copy(2, x_all.at[near_x], near_x, core_peer)

    for_peers(me, lambda peer: taps_copy(peer).start())
    for_peers(me, lambda peer: mixed_copy(peer).start())
    x_core.start()
    loads[2].wait()
    loads[3].wait()
    loop(ROWS // 128, make_up)

    taps_all[me] = taps_send[me // 16]
    mixed_all[pl.ds(PAD + 2 * me, 2)] = mixed_send[:, chan_rows(me), :]
    up_all[pl.ds(2 * me, 2)] = up_send[:, chan_rows(me), :]
    mixed_all[:PAD] = jnp.zeros((PAD, CH, B), BF16)
    up_all[NB:] = jnp.zeros((PAD, CH, B), BF16)

    for_peers(me, lambda peer: mixed_copy(peer).wait_send())
    for_peers(me, lambda peer: up_copy(peer).start())

    wait_all(TAPS, lambda peer: taps_all.at[peer], taps_send.at[0])
    row_id = lax.broadcasted_iota(jnp.int32, (B, B), 0)
    col_id = lax.broadcasted_iota(jnp.int32, (B, B), 1)

    def sheared(src, half):
        piece = taps_all[src]
        wide = jnp.concatenate(
            [piece[2 * half : 2 * half + 1, :], piece[2 * half + 1 : 2 * half + 2, :]], axis=1
        )
        return pltpu.roll(jnp.broadcast_to(wide, (B, B)), 0, 1, stride=1, stride_axis=0)

    acc[:B] = jnp.zeros((B, B), F32)

    def make_tiles(s):
        for half in range(2):
            now = sheared(s, half)
            toeplitz[2 * s + half] = jnp.where(col_id >= row_id, now, acc[:B]).astype(BF16)
            acc[:B] = now

    loop(N, make_tiles)

    wait_all(MIXED, lambda peer: mixed_all.at[pl.ds(PAD + 2 * peer, 2)], mixed_send.at[:, :CH, :])

    def hand_back(i, copy, send, dest):
        for r in range(8):
            peer = 8 * i + r

            @pl.when(peer != me)
            def _():
                copy(peer).start()

            @pl.when(peer == me)
            def _():
                dest[:, chan_rows(me), :] = send[pl.ds(2 * me, 2)]

    def conv_chunk(step):
        i = lax.rem(ix + step, 4)
        acc[...] = jnp.zeros((2 * B, B), F32)

        def some(j, first, blocks):
            part = None
            for u in range(8):
                m = 8 * j + u
                lhs = mixed_all[pl.ds(PAD + first - m, blocks)].reshape(blocks * CH, B)
                term = jnp.dot(lhs, toeplitz[m], preferred_element_type=F32)
                part = term if part is None else part + term
            return part

        def full(j):
            acc[...] += some(j, 16 * i, 16)

        loop(2 * i + 1, full)
        acc[B:] += some(2 * i + 1, 16 * i + 8, 8)
        conv_send[pl.ds(16 * i, 16)] = acc[...].astype(BF16).reshape(16, CH, B)
        hand_back(i, conv_copy, conv_send, conv_all)

    loop(4, conv_chunk)
    x_near.start()

    wait_all(UP, lambda peer: up_all.at[pl.ds(2 * peer, 2)], up_send.at[:, :CH, :])

    def back_chunk(step):
        i = lax.rem(ix + step, 4)
        acc[...] = jnp.zeros((2 * B, B), F32)

        def some(j, blocks):
            part = None
            for u in range(8):
                m = 8 * j + u
                lhs = up_all[pl.ds(16 * i + m, blocks)].reshape(blocks * CH, B)
                term = lax.dot_general(
                    lhs, toeplitz[m], (((1,), (1,)), ((), ())), preferred_element_type=F32
                )
                part = term if part is None else part + term
            return part

        def full(j):
            acc[...] += some(j, 16)

        loop(7 - 2 * i, full)
        acc[:B] += some(7 - 2 * i, 8)
        back_send[pl.ds(16 * i, 16)] = acc[...].astype(BF16).reshape(16, CH, B)

    loop(4, back_chunk)

    wait_all(CONV, lambda peer: conv_all.at[:, chan_rows(peer), :], conv_send.at[:2])

    def use_conv(r):
        rows = pl.ds(pl.multiple_of(r * 128, 128), 128)
        for half in range(2):
            cols = slice(half * B, (half + 1) * B)
            conv = conv_all[half, rows, :].astype(F32)
            grad_query_ref[rows, cols] = (g_ref[rows, cols].astype(F32) * conv).astype(BF16)
            mixed_out_ref[rows, cols] = (q_ref[rows, cols].astype(F32) * conv).astype(BF16)

    loop(ROWS // 128, use_conv)
    stores[0].start()
    stores[1].start()
    loads[4].wait()
    x_core.wait_recv()

    def share(lhs, first, count):
        return lax.dot_general(
            lhs,
            grad_query_ref[first : first + count, :],
            (((1,), (1,)), ((), ())),
            preferred_element_type=F32,
        ).astype(BF16)

    def share_a(px, pz):
        lhs = x_all[pl.ds(8 * px + 4 * pz, 4)].reshape(512, T)
        part_a[px, pz] = share(lhs, 0, WA).reshape(4, 128, WA)

    def share_b(py, pz, pair):
        lhs = jnp.concatenate([x_all[16 * pair + 8 * e + 4 * pz + py] for e in range(2)], axis=0)
        part_b[py, pz, pl.ds(2 * pair, 2)] = share(lhs, WA, WB).reshape(2, 128, WB)

    def share_c(pz, px):
        lhs = x_all[pl.ds(8 * px + 4 * pz, 4)].reshape(512, T)
        both = share(lhs, WA + WB, 2 * WC)
        part_c[0, pz, px] = both[:, :WC].reshape(4, 128, WC)
        for py in range(4):
            part_c[1, pz, py, px] = both[py * 128 : (py + 1) * 128, WC:]

    def x_peer(d):
        return lax.rem(ix + d, 4) * 8 + iz * 4 + iy

    def y_peer(d):
        return ix * 8 + iz * 4 + lax.rem(iy + d, 4)

    def ring_copies(bank, view, inbox, index, peer_of):
        up, down, far = (lax.rem(index + d, 4) for d in (1, 3, 2))

        def ring_copy(slot, target, side, hop):
            return pltpu.make_async_remote_copy(
                src_ref=view(target, side),
                dst_ref=inbox.at[slot],
                send_sem=r_send_sem.at[bank, slot],
                recv_sem=r_recv_sem.at[bank, slot],
                device_id={"seq": peer_of(hop)},
                device_id_type=MESH,
            )

        return (
            ring_copy(0, far, 0, 1),
            ring_copy(1, far, 1, 3),
            ring_copy(2, up, 1, 1),
            ring_copy(3, down, 0, 3),
            ring_copy(4, up, 0, 1),
            ring_copy(5, down, 1, 3),
        )

    def ring_start(copies, first=0, last=4):
        for c in copies[first:last]:
            c.start()

    def ring_middle(copies, view, inbox, index, blocks):
        for slot, there, side in ((0, 1, 0), (1, 3, 1)):
            copies[slot].wait_recv()
            held = view(lax.rem(index + there, 4), side)

            def add(e):
                total = held[e].astype(F32) + inbox[slot, e].astype(F32)
                held[e] = total.astype(BF16)

            loop(blocks, add)
            copies[4 + slot].start()

    def ring_end(copies, view, inbox, index, blocks, store):
        for slot in (2, 3, 4, 5):
            copies[slot].wait_recv()

        def add(e):
            for side, one, two in ((0, 4, 3), (1, 5, 2)):
                total = view(index, side)[e].astype(F32) + (
                    inbox[one, e].astype(F32) + inbox[two, e].astype(F32)
                )
                store(side, e, total)

        loop(blocks, add)

    def view_a(target, side):
        return part_a.at[target, side]

    def view_b(pair):
        return lambda target, side: part_b.at[target, side, pl.ds(2 * pair, 2)]

    here = chan // 2
    there = 1 - here
    ring_a = (view_a, first_in_a, ix)
    ring_b0 = (view_b(here), first_in_b.at[0], iy)
    ring_b1 = (view_b(there), first_in_b.at[1], iy)
    copies_a = ring_copies(0, *ring_a, x_peer)
    copies_b0 = ring_copies(1, *ring_b0, y_peer)
    copies_b1 = ring_copies(2, *ring_b1, y_peer)

    other = ix * 8 + (1 - iz) * 4 + iy

    def z_copy(slot, held, inbox):
        return pltpu.make_async_remote_copy(
            src_ref=held.at[1 - iz],
            dst_ref=inbox,
            send_sem=z_send_sem.at[slot],
            recv_sem=z_recv_sem.at[slot],
            device_id={"seq": other},
            device_id_type=MESH,
        )

    across = [z_copy(2 + c, part_c.at[c], across_in.at[c]) for c in range(2)]

    def view_c(c):
        return lambda target, side: part_c.at[c, iz, target, pl.ds(2 * side, 2)]

    def second_c(c):
        return lambda target, side: first_out_c.at[c, target, side]

    rings_c = (
        (view_c(0), first_in_c.at[0], ix),
        (view_c(1), first_in_c.at[1], iy),
    )
    rings_e = (
        (second_c(0), second_in_c.at[0], iy),
        (second_c(1), second_in_c.at[1], ix),
    )
    peers_c = (x_peer, y_peer)
    first_c = [ring_copies(5 + c, *rings_c[c], peers_c[c]) for c in range(2)]
    last_c = [ring_copies(7 + c, *rings_e[c], peers_c[1 - c]) for c in range(2)]

    def merge_c(c):
        across[c].wait_recv()

        def add(d):
            total = part_c[c, iz, d].astype(F32) + across_in[c, d].astype(F32)
            part_c[c, iz, d] = total.astype(BF16)

        loop(4, add)
        ring_start(first_c[c])

    def store_c(c):
        def store(side, e, total):
            first_out_c[c, 2 * side + e, 0, 0] = total[:64].astype(BF16)
            first_out_c[c, 2 * side + e, 1, 0] = total[64:].astype(BF16)

        return store

    def final_c(c):
        def store(side, e, total):
            first = WA + WB + c * WC
            rows = slice(64 * side, 64 * side + 64)
            weight_grad_ref[rows, first : first + WC] = total * weight_factor

        return store

    weight_factor = 1.0 / math.sqrt(N * T)

    def shares_b(copies, pair):
        loop(2, lambda z: share_b(lax.rem(iy + 2, 4), z, pair))
        ring_start(copies, 0, 2)
        loop(2, lambda z: share_b(lax.rem(iy + 3 - 2 * z, 4), z, pair))
        ring_start(copies, 2, 4)
        loop(2, lambda z: share_b(lax.rem(iy + 1 + 2 * z, 4), z, pair))

    shares_b(copies_b0, here)
    loop(2, lambda z: share_b(iy, z, here))

    flip = (row_id + col_id == B - 1).astype(BF16)
    for c in range(8):
        piece = mixed_all[PAD + 8 * c : PAD + 8 * c + 8].reshape(B, B)
        mixed_flip[:, c * B : (c + 1) * B] = lax.dot_general(
            flip, piece, (((1,), (1,)), ((), ())), preferred_element_type=F32
        ).astype(BF16)

    def filter_tile(i, m):
        depth = (8 - i) * B
        corr = jnp.dot(
            mixed_flip[:, :depth],
            up_all[pl.ds(m, 8 * (8 - i))].reshape(depth, B),
            preferred_element_type=F32,
        )
        turned = pltpu.roll(corr, 1, 1, stride=1, stride_axis=0)
        above = jnp.where(col_id <= row_id, turned, 0.0)
        below = turned - above
        filt_part[0, m] = jnp.sum(above.reshape(B // 8, 8, B), axis=0)
        filt_part[1, m] = jnp.sum(below.reshape(B // 8, 8, B), axis=0)

    def filter_some(i):
        loop(8, lambda u: filter_tile(i, 8 * i + u))

    filter_some(0)
    ring_middle(copies_b0, *ring_b0, 2)

    x_near.wait_recv()
    x_pass.start()
    filter_some(7)
    filter_some(6)
    x_pass.wait_recv()
    loop(4, lambda px: share_c(1 - iz, px))
    across[0].start()
    across[1].start()
    loop(2, lambda z: share_a(lax.rem(ix + 2, 4), z))
    ring_start(copies_a, 0, 2)
    loop(2, lambda z: share_a(lax.rem(ix + 3 - 2 * z, 4), z))
    ring_start(copies_a, 2, 4)
    loop(2, lambda z: share_a(lax.rem(ix + 1 + 2 * z, 4), z))
    shares_b(copies_b1, there)
    for_peers(me, lambda peer: back_copy(peer).start())
    back_all[:, chan_rows(me), :] = back_send[pl.ds(2 * me, 2)]
    loop(2, lambda z: share_a(ix, z))
    loop(2, lambda z: share_b(iy, z, there))
    loop(4, lambda px: share_c(iz, px))
    filter_some(1)
    ring_middle(copies_a, *ring_a, 4)
    ring_middle(copies_b1, *ring_b1, 2)
    for i in range(2, 6):
        filter_some(i)
    merge_c(0)
    merge_c(1)

    filt_part[1, NB] = jnp.zeros((8, B), F32)
    taps_factor = 1.0 / math.sqrt(GROUP * N * T)

    def filter_rows(s):
        for half in range(2):
            m = 2 * s + half
            both = jnp.sum(filt_part[0, m] + filt_part[1, m + 1], axis=0, keepdims=True)
            filt_send[s, 2 * half : 2 * half + 1, :] = both[:, :128] * taps_factor
            filt_send[s, 2 * half + 1 : 2 * half + 2, :] = both[:, 128:] * taps_factor
        filt_send[s, 4:8, :] = jnp.zeros((4, 128), F32)

    loop(N, filter_rows)
    for_peers(me, lambda peer: filt_copy(peer).start())
    filt_all[me] = filt_send[me]

    def second_view(held):
        return lambda target, side: held.at[target, side]

    ring_c = (second_view(first_out_a), second_in_a, iy)
    ring_d = (second_view(first_out_b), second_in_b, ix)
    copies_c = ring_copies(3, *ring_c, y_peer)
    copies_d = ring_copies(4, *ring_d, x_peer)

    def store_a(side, e, total):
        first_out_a[e, side, 0] = total.astype(BF16)

    def store_b(pair):
        def store(side, e, total):
            first_out_b[2 * pair + e, side, 0] = total.astype(BF16)

        return store

    ring_end(copies_b0, *ring_b0, 2, store_b(here))
    ring_end(copies_b1, *ring_b1, 2, store_b(there))
    ring_start(copies_d)
    ring_end(copies_a, *ring_a, 4, store_a)
    ring_start(copies_c)
    for c in range(2):
        ring_middle(first_c[c], *rings_c[c], 2)
    wait_all(BACK, lambda peer: back_all.at[:, chan_rows(peer), :], back_send.at[:2])

    def use_back(r):
        rows = pl.ds(pl.multiple_of(r * 128, 128), 128)
        for half in range(2):
            cols = slice(half * B, (half + 1) * B)
            back = back_all[half, rows, :].astype(F32)
            grad_key_ref[rows, cols] = (v_ref[rows, cols].astype(F32) * back).astype(BF16)
            grad_value_ref[rows, cols] = (k_ref[rows, cols].astype(F32) * back).astype(BF16)

    loop(ROWS // 128, use_back)
    stores[2].start()
    stores[3].start()

    ring_middle(copies_d, *ring_d, 1)
    ring_middle(copies_c, *ring_c, 1)
    for c in range(2):
        ring_end(first_c[c], *rings_c[c], 2, store_c(c))
        ring_start(last_c[c])

    wait_all(FILT, lambda peer: filt_all.at[peer], filt_send.at[0])
    for g in range(2):
        total = jnp.sum(filt_all[16 * g : 16 * g + 16], axis=0)
        for c in range(4):
            filter_grad_ref[g : g + 1, c * 128 : (c + 1) * 128] = total[c : c + 1, :]

    def keep(held):
        def store(side, e, total):
            held[side] = total.astype(BF16)

        return store

    copy_b = z_copy(1, second_out_b, third_in_b)
    copy_a = z_copy(0, second_out_a, third_in_a)
    ring_end(copies_d, *ring_d, 1, keep(second_out_b))
    copy_b.start()
    ring_end(copies_c, *ring_c, 1, keep(second_out_a))
    copy_a.start()
    for c in range(2):
        ring_middle(last_c[c], *rings_e[c], 1)
    for c in range(2):
        ring_end(last_c[c], *rings_e[c], 1, final_c(c))
    copy_b.wait_recv()
    total = second_out_b[iz].astype(F32) + third_in_b[...].astype(F32)
    weight_grad_ref[:, WA : WA + WB] = total * weight_factor
    copy_a.wait_recv()
    total = second_out_a[iz].astype(F32) + third_in_a[...].astype(F32)
    weight_grad_ref[:, :WA] = total * weight_factor

    for store_out in stores:
        store_out.wait()
    for make in (taps_copy, up_copy, conv_copy, back_copy, filt_copy):
        for_peers(me, lambda peer: make(peer).wait_send())
    rings = (*copies_a, *copies_b0, *copies_b1, *copies_c, *copies_d)
    rings += (*first_c[0], *first_c[1], *last_c[0], *last_c[1], *across)
    for c in (x_core, x_near, x_pass, *rings, copy_a, copy_b):
        c.wait_send()


def hand_over(*refs):
    count = len(refs) // 3
    sources, targets, held = refs[:count], refs[count : 2 * count], refs[2 * count : 3 * count]
    sems = refs[3 * count]
    loads = [pltpu.make_async_copy(sources[c], held[c], sems.at[0, c]) for c in range(count)]
    stores = [pltpu.make_async_copy(held[c], targets[c], sems.at[1, c]) for c in range(count)]
    for load in loads:
        load.start()
    for load, store in zip(loads, stores):
        load.wait()
        store.start()
    for store in stores:
        store.wait()


def per_device(layer_input, query_proj, key_proj, value_proj, filter_taps, grad_out):
    vmem = pl.BlockSpec(memory_space=pltpu.VMEM)
    hbm = pl.BlockSpec(memory_space=pl.ANY)
    rows = jax.ShapeDtypeStruct((ROWS, T), BF16)
    shapes = (
        rows,
        rows,
        rows,
        rows,
        jax.ShapeDtypeStruct((2, T), F32),
        jax.ShapeDtypeStruct((128, ROWS), F32),
    )
    results = pl.pallas_call(
        kernel,
        out_shape=shapes,
        in_specs=[hbm] * 4 + [vmem, hbm],
        out_specs=[hbm] * 4 + [vmem] * 2,
        scratch_shapes=[pltpu.VMEM((ROWS, T), BF16)] * 8
        + [
            pltpu.VMEM((2, ROWS, B), BF16),
            pltpu.VMEM((2, ROWS, B), BF16),
            pltpu.VMEM((2, 8, 128), F32),
            pltpu.VMEM((N, 8, 128), F32),
            pltpu.VMEM((PAD + NB, CH, B), BF16),
            pltpu.VMEM((NB + PAD, CH, B), BF16),
            pltpu.VMEM((B, NB * CH), BF16),
            pltpu.VMEM((NB, B, B), BF16),
            pltpu.VMEM((2 * B, B), F32),
            pltpu.VMEM((NB, CH, B), BF16),
            pltpu.VMEM((NB, CH, B), BF16),
            pltpu.VMEM((2, ROWS, B), BF16),
            pltpu.VMEM((2, ROWS, B), BF16),
            pltpu.VMEM((2, NB + 1, 8, B), F32),
            pltpu.VMEM((N, 8, 128), F32),
            pltpu.VMEM((N, 8, 128), F32),
            pltpu.VMEM((N, 128, T), BF16),
            pltpu.VMEM((4, 2, 4, 128, WA), BF16),
            pltpu.VMEM((4, 2, 4, 128, WB), BF16),
            pltpu.VMEM((6, 4, 128, WA), BF16),
            pltpu.VMEM((2, 6, 2, 128, WB), BF16),
            pltpu.VMEM((4, 2, 1, 128, WA), BF16),
            pltpu.VMEM((4, 2, 1, 128, WB), BF16),
            pltpu.VMEM((6, 1, 128, WA), BF16),
            pltpu.VMEM((6, 1, 128, WB), BF16),
            pltpu.VMEM((2, 128, WA), BF16),
            pltpu.VMEM((2, 128, WB), BF16),
            pltpu.VMEM((128, WA), BF16),
            pltpu.VMEM((128, WB), BF16),
            pltpu.VMEM((2, 2, 4, 4, 128, WC), BF16),
            pltpu.VMEM((2, 4, 4, 128, WC), BF16),
            pltpu.VMEM((2, 6, 2, 128, WC), BF16),
            pltpu.VMEM((2, 4, 2, 1, 64, WC), BF16),
            pltpu.VMEM((2, 6, 1, 64, WC), BF16),
            pltpu.SemaphoreType.DMA((KINDS, N)),
            pltpu.SemaphoreType.DMA((KINDS, N)),
            pltpu.SemaphoreType.DMA((3,)),
            pltpu.SemaphoreType.DMA((3,)),
            pltpu.SemaphoreType.DMA((9, 6)),
            pltpu.SemaphoreType.DMA((9, 6)),
            pltpu.SemaphoreType.DMA((4,)),
            pltpu.SemaphoreType.DMA((4,)),
            pltpu.SemaphoreType.DMA((5,)),
            pltpu.SemaphoreType.DMA((4,)),
        ],
        compiler_params=pltpu.CompilerParams(
            collective_id=0, has_side_effects=True, vmem_limit_bytes=62 * 2**20
        ),
    )(
        layer_input.reshape(8, 128, T),
        query_proj,
        key_proj,
        value_proj,
        filter_taps,
        grad_out,
    )
    return tuple(
        pl.pallas_call(
            hand_over,
            out_shape=shapes,
            in_specs=[hbm] * 6,
            out_specs=[hbm] * 6,
            scratch_shapes=[pltpu.VMEM(shape.shape, shape.dtype) for shape in shapes]
            + [pltpu.SemaphoreType.DMA((2, 6))],
        )(*results)
    )


def solution(mesh):
    placed = (P("chan", "seq"),) * 6
    return jax.shard_map(
        per_device,
        mesh=mesh,
        in_specs=placed,
        out_specs=(P("chan", "seq"),) * 5 + (P("seq", "chan"),),
        check_vma=False,
    )
```

```python
import functools
import math

import jax
import jax.numpy as jnp
from jax import lax
from jax.experimental import pallas as pl
from jax.experimental.pallas import tpu as pltpu
from jax.sharding import PartitionSpec as P

GROUP = 512
F32 = jnp.float32
BF16 = jnp.bfloat16
MESH = pl.DeviceIdType.MESH

N = 32
CH = 32
T = 512
B = 256
NB = N * T // B
PAD = 8
ROWS = N * CH
WA = 256
WB = 512
WC = (ROWS - WA - WB) // 2
KINDS = 6
MIXED, UP, TAPS, CONV, BACK, FILT = range(KINDS)


def seq_copy(src, dst, kind, peer, sems, me):
    send, recv = sems
    return pltpu.make_async_remote_copy(
        src_ref=src,
        dst_ref=dst,
        send_sem=send.at[kind, peer],
        recv_sem=recv.at[kind, me],
        device_id={"seq": peer},
        device_id_type=MESH,
    )


def for_peers(me, body):
    def step(i, carry):
        body(lax.rem(me + i, N))
        return carry

    lax.fori_loop(1, N, step, 0)


def loop(n, body, start=0):
    def step(i, carry):
        body(i)
        return carry

    lax.fori_loop(start, n, step, 0)


def kernel(
    x_hbm,
    q_hbm,
    k_hbm,
    v_hbm,
    taps_ref,
    g_hbm,
    mixed_out_hbm,
    grad_query_hbm,
    grad_key_hbm,
    grad_value_hbm,
    filter_grad_ref,
    weight_grad_ref,
    q_ref,
    k_ref,
    v_ref,
    g_ref,
    mixed_out_ref,
    grad_query_ref,
    grad_key_ref,
    grad_value_ref,
    mixed_send,
    up_send,
    taps_send,
    taps_all,
    mixed_all,
    up_all,
    mixed_flip,
    toeplitz,
    acc,
    conv_send,
    back_send,
    conv_all,
    back_all,
    filt_part,
    filt_send,
    filt_all,
    x_all,
    part_a,
    part_b,
    first_in_a,
    first_in_b,
    first_out_a,
    first_out_b,
    second_in_a,
    second_in_b,
    second_out_a,
    second_out_b,
    third_in_a,
    third_in_b,
    part_c,
    across_in,
    first_in_c,
    first_out_c,
    second_in_c,
    send_sem,
    recv_sem,
    x_send_sem,
    x_recv_sem,
    r_send_sem,
    r_recv_sem,
    z_send_sem,
    z_recv_sem,
    in_sem,
    out_sem,
):
    me = lax.axis_index("seq")
    chan = lax.axis_index("chan")
    ix = me // 8
    iz = lax.rem(me // 4, 2)
    iy = lax.rem(me, 4)
    sems = (send_sem, recv_sem)

    own_x = pl.ds(chan * 8, 8)
    loads = [
        pltpu.make_async_copy(src, dst, in_sem.at[slot])
        for slot, (src, dst) in enumerate(
            (
                (k_hbm, k_ref),
                (v_hbm, v_ref),
                (g_hbm, g_ref),
                (q_hbm, q_ref),
                (x_hbm, x_all.at[own_x]),
            )
        )
    ]
    for load in loads:
        load.start()
    stores = [
        pltpu.make_async_copy(src, dst, out_sem.at[slot])
        for slot, (src, dst) in enumerate(
            (
                (mixed_out_ref, mixed_out_hbm),
                (grad_query_ref, grad_query_hbm),
                (grad_key_ref, grad_key_hbm),
                (grad_value_ref, grad_value_hbm),
            )
        )
    ]

    barrier = pltpu.get_barrier_semaphore()
    for_peers(
        me,
        lambda peer: pl.semaphore_signal(
            barrier, inc=1, device_id={"seq": peer}, device_id_type=MESH
        ),
    )
    core_peer = chan + 1 - 2 * lax.rem(chan, 2)
    near_peer = lax.rem(chan + 2, 4)
    for peer in (core_peer, near_peer):
        pl.semaphore_signal(barrier, inc=1, device_id={"chan": peer}, device_id_type=MESH)

    def make_mixed(r):
        rows = pl.ds(pl.multiple_of(r * 128, 128), 128)
        prod = (k_ref[rows, :].astype(F32) * v_ref[rows, :].astype(F32)).astype(BF16)
        mixed_send[0, rows, :] = prod[:, :B]
        mixed_send[1, rows, :] = prod[:, B:]

    def make_up(r):
        rows = pl.ds(pl.multiple_of(r * 128, 128), 128)
        prod = (g_ref[rows, :].astype(F32) * q_ref[rows, :].astype(F32)).astype(BF16)
        up_send[0, rows, :] = prod[:, :B]
        up_send[1, rows, :] = prod[:, B:]

    for g in range(2):
        for c in range(4):
            taps_send[g, c : c + 1, :] = taps_ref[g : g + 1, c * 128 : (c + 1) * 128]
        taps_send[g, 4:8, :] = jnp.zeros((4, 128), F32)
    loads[0].wait()
    loads[1].wait()
    loop(ROWS // 128, make_mixed)
    pl.semaphore_wait(barrier, N + 1)

    def chan_rows(peer):
        return pl.ds(pl.multiple_of(peer * CH, CH), CH)

    def taps_copy(peer):
        return seq_copy(taps_send.at[peer // 16], taps_all.at[me], TAPS, peer, sems, me)

    def mixed_copy(peer):
        return seq_copy(
            mixed_send.at[:, chan_rows(peer), :],
            mixed_all.at[pl.ds(PAD + 2 * me, 2)],
            MIXED,
            peer,
            sems,
            me,
        )

    def up_copy(peer):
        return seq_copy(
            up_send.at[:, chan_rows(peer), :],
            up_all.at[pl.ds(2 * me, 2)],
            UP,
            peer,
            sems,
            me,
        )

    def conv_copy(peer):
        return seq_copy(
            conv_send.at[pl.ds(2 * peer, 2)],
            conv_all.at[:, chan_rows(me), :],
            CONV,
            peer,
            sems,
            me,
        )

    def back_copy(peer):
        return seq_copy(
            back_send.at[pl.ds(2 * peer, 2)],
            back_all.at[:, chan_rows(me), :],
            BACK,
            peer,
            sems,
            me,
        )

    def filt_copy(peer):
        return seq_copy(filt_send.at[peer], filt_all.at[me], FILT, peer, sems, me)

    def wait_all(kind, dst_of, src_any):
        def one(peer):
            pltpu.make_async_remote_copy(
                src_ref=src_any,
                dst_ref=dst_of(peer),
                send_sem=send_sem.at[kind, peer],
                recv_sem=recv_sem.at[kind, peer],
                device_id={"seq": peer},
                device_id_type=MESH,
            ).wait_recv()

        for_peers(me, one)

    near_x = pl.ds(near_peer * 8, 8)

    def x_copy(slot, src, rows, peer):
        return pltpu.make_async_remote_copy(
            src_ref=src,
            dst_ref=x_all.at[rows],
            send_sem=x_send_sem.at[slot],
            recv_sem=x_recv_sem.at[slot],
            device_id={"chan": peer},
            device_id_type=MESH,
        )

    x_core = x_copy(0, x_hbm, own_x, core_peer)
    x_near = x_copy(1, x_hbm, own_x, near_peer)
    x_pass = x_copy(2, x_all.at[near_x], near_x, core_peer)

    for_peers(me, lambda peer: taps_copy(peer).start())
    for_peers(me, lambda peer: mixed_copy(peer).start())
    x_core.start()
    loads[2].wait()
    loads[3].wait()
    loop(ROWS // 128, make_up)

    taps_all[me] = taps_send[me // 16]
    mixed_all[pl.ds(PAD + 2 * me, 2)] = mixed_send[:, chan_rows(me), :]
    up_all[pl.ds(2 * me, 2)] = up_send[:, chan_rows(me), :]
    mixed_all[:PAD] = jnp.zeros((PAD, CH, B), BF16)
    up_all[NB:] = jnp.zeros((PAD, CH, B), BF16)

    for_peers(me, lambda peer: mixed_copy(peer).wait_send())
    for_peers(me, lambda peer: up_copy(peer).start())

    wait_all(TAPS, lambda peer: taps_all.at[peer], taps_send.at[0])
    row_id = lax.broadcasted_iota(jnp.int32, (B, B), 0)
    col_id = lax.broadcasted_iota(jnp.int32, (B, B), 1)

    def sheared(src, half):
        piece = taps_all[src]
        wide = jnp.concatenate(
            [piece[2 * half : 2 * half + 1, :], piece[2 * half + 1 : 2 * half + 2, :]], axis=1
        )
        return pltpu.roll(jnp.broadcast_to(wide, (B, B)), 0, 1, stride=1, stride_axis=0)

    acc[:B] = jnp.zeros((B, B), F32)

    def make_tiles(s):
        for half in range(2):
            now = sheared(s, half)
            toeplitz[2 * s + half] = jnp.where(col_id >= row_id, now, acc[:B]).astype(BF16)
            acc[:B] = now

    loop(N, make_tiles)

    wait_all(MIXED, lambda peer: mixed_all.at[pl.ds(PAD + 2 * peer, 2)], mixed_send.at[:, :CH, :])

    def hand_back(i, copy, send, dest):
        for r in range(8):
            peer = 8 * i + r

            @pl.when(peer != me)
            def _():
                copy(peer).start()

            @pl.when(peer == me)
            def _():
                dest[:, chan_rows(me), :] = send[pl.ds(2 * me, 2)]

    def conv_chunk(step):
        i = lax.rem(ix + step, 4)
        acc[...] = jnp.zeros((2 * B, B), F32)

        def some(j, first, blocks):
            part = None
            for u in range(8):
                m = 8 * j + u
                lhs = mixed_all[pl.ds(PAD + first - m, blocks)].reshape(blocks * CH, B)
                term = jnp.dot(lhs, toeplitz[m], preferred_element_type=F32)
                part = term if part is None else part + term
            return part

        def full(j):
            acc[...] += some(j, 16 * i, 16)

        loop(2 * i + 1, full)
        acc[B:] += some(2 * i + 1, 16 * i + 8, 8)
        conv_send[pl.ds(16 * i, 16)] = acc[...].astype(BF16).reshape(16, CH, B)
        hand_back(i, conv_copy, conv_send, conv_all)

    loop(4, conv_chunk)
    x_near.start()

    wait_all(UP, lambda peer: up_all.at[pl.ds(2 * peer, 2)], up_send.at[:, :CH, :])

    def back_chunk(step):
        i = lax.rem(ix + step, 4)
        acc[...] = jnp.zeros((2 * B, B), F32)

        def some(j, blocks):
            part = None
            for u in range(8):
                m = 8 * j + u
                lhs = up_all[pl.ds(16 * i + m, blocks)].reshape(blocks * CH, B)
                term = lax.dot_general(
                    lhs, toeplitz[m], (((1,), (1,)), ((), ())), preferred_element_type=F32
                )
                part = term if part is None else part + term
            return part

        def full(j):
            acc[...] += some(j, 16)

        loop(7 - 2 * i, full)
        acc[:B] += some(7 - 2 * i, 8)
        back_send[pl.ds(16 * i, 16)] = acc[...].astype(BF16).reshape(16, CH, B)

    loop(4, back_chunk)

    wait_all(CONV, lambda peer: conv_all.at[:, chan_rows(peer), :], conv_send.at[:2])

    def use_conv(r):
        rows = pl.ds(pl.multiple_of(r * 128, 128), 128)
        for half in range(2):
            cols = slice(half * B, (half + 1) * B)
            conv = conv_all[half, rows, :].astype(F32)
            grad_query_ref[rows, cols] = (g_ref[rows, cols].astype(F32) * conv).astype(BF16)
            mixed_out_ref[rows, cols] = (q_ref[rows, cols].astype(F32) * conv).astype(BF16)

    loop(ROWS // 128, use_conv)
    stores[0].start()
    stores[1].start()
    loads[4].wait()
    x_core.wait_recv()

    def share(lhs, first, count):
        return lax.dot_general(
            lhs,
            grad_query_ref[first : first + count, :],
            (((1,), (1,)), ((), ())),
            preferred_element_type=F32,
        ).astype(BF16)

    def share_a(px, pz):
        lhs = x_all[pl.ds(8 * px + 4 * pz, 4)].reshape(512, T)
        part_a[px, pz] = share(lhs, 0, WA).reshape(4, 128, WA)

    def share_b(py, pz, pair):
        lhs = jnp.concatenate([x_all[16 * pair + 8 * e + 4 * pz + py] for e in range(2)], axis=0)
        part_b[py, pz, pl.ds(2 * pair, 2)] = share(lhs, WA, WB).reshape(2, 128, WB)

    def share_c(pz, px):
        lhs = x_all[pl.ds(8 * px + 4 * pz, 4)].reshape(512, T)
        both = share(lhs, WA + WB, 2 * WC)
        part_c[0, pz, px] = both[:, :WC].reshape(4, 128, WC)
        for py in range(4):
            part_c[1, pz, py, px] = both[py * 128 : (py + 1) * 128, WC:]

    def x_peer(d):
        return lax.rem(ix + d, 4) * 8 + iz * 4 + iy

    def y_peer(d):
        return ix * 8 + iz * 4 + lax.rem(iy + d, 4)

    def ring_copies(bank, view, inbox, index, peer_of):
        up, down, far = (lax.rem(index + d, 4) for d in (1, 3, 2))

        def ring_copy(slot, target, side, hop):
            return pltpu.make_async_remote_copy(
                src_ref=view(target, side),
                dst_ref=inbox.at[slot],
                send_sem=r_send_sem.at[bank, slot],
                recv_sem=r_recv_sem.at[bank, slot],
                device_id={"seq": peer_of(hop)},
                device_id_type=MESH,
            )

        return (
            ring_copy(0, far, 0, 1),
            ring_copy(1, far, 1, 3),
            ring_copy(2, up, 1, 1),
            ring_copy(3, down, 0, 3),
            ring_copy(4, up, 0, 1),
            ring_copy(5, down, 1, 3),
        )

    def ring_start(copies, first=0, last=4):
        for c in copies[first:last]:
            c.start()

    def ring_middle(copies, view, inbox, index, blocks):
        for slot, there, side in ((0, 1, 0), (1, 3, 1)):
            copies[slot].wait_recv()
            held = view(lax.rem(index + there, 4), side)

            def add(e):
                total = held[e].astype(F32) + inbox[slot, e].astype(F32)
                held[e] = total.astype(BF16)

            loop(blocks, add)
            copies[4 + slot].start()

    def ring_end(copies, view, inbox, index, blocks, store):
        for slot in (2, 3, 4, 5):
            copies[slot].wait_recv()

        def add(e):
            for side, one, two in ((0, 4, 3), (1, 5, 2)):
                total = view(index, side)[e].astype(F32) + (
                    inbox[one, e].astype(F32) + inbox[two, e].astype(F32)
                )
                store(side, e, total)

        loop(blocks, add)

    def view_a(target, side):
        return part_a.at[target, side]

    def view_b(pair):
        return lambda target, side: part_b.at[target, side, pl.ds(2 * pair, 2)]

    here = chan // 2
    there = 1 - here
    ring_a = (view_a, first_in_a, ix)
    ring_b0 = (view_b(here), first_in_b.at[0], iy)
    ring_b1 = (view_b(there), first_in_b.at[1], iy)
    copies_a = ring_copies(0, *ring_a, x_peer)
    copies_b0 = ring_copies(1, *ring_b0, y_peer)
    copies_b1 = ring_copies(2, *ring_b1, y_peer)

    other = ix * 8 + (1 - iz) * 4 + iy

    def z_copy(slot, held, inbox):
        return pltpu.make_async_remote_copy(
            src_ref=held.at[1 - iz],
            dst_ref=inbox,
            send_sem=z_send_sem.at[slot],
            recv_sem=z_recv_sem.at[slot],
            device_id={"seq": other},
            device_id_type=MESH,
        )

    across = [z_copy(2 + c, part_c.at[c], across_in.at[c]) for c in range(2)]

    def view_c(c):
        return lambda target, side: part_c.at[c, iz, target, pl.ds(2 * side, 2)]

    def second_c(c):
        return lambda target, side: first_out_c.at[c, target, side]

    rings_c = (
        (view_c(0), first_in_c.at[0], ix),
        (view_c(1), first_in_c.at[1], iy),
    )
    rings_e = (
        (second_c(0), second_in_c.at[0], iy),
        (second_c(1), second_in_c.at[1], ix),
    )
    peers_c = (x_peer, y_peer)
    first_c = [ring_copies(5 + c, *rings_c[c], peers_c[c]) for c in range(2)]
    last_c = [ring_copies(7 + c, *rings_e[c], peers_c[1 - c]) for c in range(2)]

    def merge_c(c):
        across[c].wait_recv()

        def add(d):
            total = part_c[c, iz, d].astype(F32) + across_in[c, d].astype(F32)
            part_c[c, iz, d] = total.astype(BF16)

        loop(4, add)
        ring_start(first_c[c])

    def store_c(c):
        def store(side, e, total):
            first_out_c[c, 2 * side + e, 0, 0] = total[:64].astype(BF16)
            first_out_c[c, 2 * side + e, 1, 0] = total[64:].astype(BF16)

        return store

    def final_c(c):
        def store(side, e, total):
            first = WA + WB + c * WC
            rows = slice(64 * side, 64 * side + 64)
            weight_grad_ref[rows, first : first + WC] = total * weight_factor

        return store

    weight_factor = 1.0 / math.sqrt(N * T)

    def shares_b(copies, pair):
        loop(2, lambda z: share_b(lax.rem(iy + 2, 4), z, pair))
        ring_start(copies, 0, 2)
        loop(2, lambda z: share_b(lax.rem(iy + 3 - 2 * z, 4), z, pair))
        ring_start(copies, 2, 4)
        loop(2, lambda z: share_b(lax.rem(iy + 1 + 2 * z, 4), z, pair))

    shares_b(copies_b0, here)
    loop(2, lambda z: share_b(iy, z, here))

    flip = (row_id + col_id == B - 1).astype(BF16)
    for c in range(8):
        piece = mixed_all[PAD + 8 * c : PAD + 8 * c + 8].reshape(B, B)
        mixed_flip[:, c * B : (c + 1) * B] = lax.dot_general(
            flip, piece, (((1,), (1,)), ((), ())), preferred_element_type=F32
        ).astype(BF16)

    def filter_tile(i, m):
        depth = (8 - i) * B
        corr = jnp.dot(
            mixed_flip[:, :depth],
            up_all[pl.ds(m, 8 * (8 - i))].reshape(depth, B),
            preferred_element_type=F32,
        )
        turned = pltpu.roll(corr, 1, 1, stride=1, stride_axis=0)
        above = jnp.where(col_id <= row_id, turned, 0.0)
        below = turned - above
        filt_part[0, m] = jnp.sum(above.reshape(B // 8, 8, B), axis=0)
        filt_part[1, m] = jnp.sum(below.reshape(B // 8, 8, B), axis=0)

    def filter_some(i):
        loop(8, lambda u: filter_tile(i, 8 * i + u))

    filter_some(0)
    ring_middle(copies_b0, *ring_b0, 2)

    x_near.wait_recv()
    x_pass.start()
    filter_some(7)
    filter_some(6)
    x_pass.wait_recv()
    loop(4, lambda px: share_c(1 - iz, px))
    across[0].start()
    across[1].start()
    loop(2, lambda z: share_a(lax.rem(ix + 2, 4), z))
    ring_start(copies_a, 0, 2)
    loop(2, lambda z: share_a(lax.rem(ix + 3 - 2 * z, 4), z))
    ring_start(copies_a, 2, 4)
    loop(2, lambda z: share_a(lax.rem(ix + 1 + 2 * z, 4), z))
    shares_b(copies_b1, there)
    loop(2, lambda z: share_a(ix, z))
    loop(2, lambda z: share_b(iy, z, there))
    loop(4, lambda px: share_c(iz, px))
    filter_some(1)
    ring_middle(copies_a, *ring_a, 4)
    ring_middle(copies_b1, *ring_b1, 2)
    for_peers(me, lambda peer: back_copy(peer).start())
    back_all[:, chan_rows(me), :] = back_send[pl.ds(2 * me, 2)]
    for i in range(2, 6):
        filter_some(i)
    merge_c(0)
    merge_c(1)

    filt_part[1, NB] = jnp.zeros((8, B), F32)
    taps_factor = 1.0 / math.sqrt(GROUP * N * T)

    def filter_rows(s):
        for half in range(2):
            m = 2 * s + half
            both = jnp.sum(filt_part[0, m] + filt_part[1, m + 1], axis=0, keepdims=True)
            filt_send[s, 2 * half : 2 * half + 1, :] = both[:, :128] * taps_factor
            filt_send[s, 2 * half + 1 : 2 * half + 2, :] = both[:, 128:] * taps_factor
        filt_send[s, 4:8, :] = jnp.zeros((4, 128), F32)

    loop(N, filter_rows)
    for_peers(me, lambda peer: filt_copy(peer).start())
    filt_all[me] = filt_send[me]

    def second_view(held):
        return lambda target, side: held.at[target, side]

    ring_c = (second_view(first_out_a), second_in_a, iy)
    ring_d = (second_view(first_out_b), second_in_b, ix)
    copies_c = ring_copies(3, *ring_c, y_peer)
    copies_d = ring_copies(4, *ring_d, x_peer)

    def store_a(side, e, total):
        first_out_a[e, side, 0] = total.astype(BF16)

    def store_b(pair):
        def store(side, e, total):
            first_out_b[2 * pair + e, side, 0] = total.astype(BF16)

        return store

    ring_end(copies_b0, *ring_b0, 2, store_b(here))
    ring_end(copies_b1, *ring_b1, 2, store_b(there))
    ring_start(copies_d)
    ring_end(copies_a, *ring_a, 4, store_a)
    ring_start(copies_c)
    for c in range(2):
        ring_middle(first_c[c], *rings_c[c], 2)
    ring_middle(copies_d, *ring_d, 1)
    ring_middle(copies_c, *ring_c, 1)
    for c in range(2):
        ring_end(first_c[c], *rings_c[c], 2, store_c(c))
        ring_start(last_c[c])

    wait_all(FILT, lambda peer: filt_all.at[peer], filt_send.at[0])
    for g in range(2):
        total = jnp.sum(filt_all[16 * g : 16 * g + 16], axis=0)
        for c in range(4):
            filter_grad_ref[g : g + 1, c * 128 : (c + 1) * 128] = total[c : c + 1, :]

    def keep(held):
        def store(side, e, total):
            held[side] = total.astype(BF16)

        return store

    copy_b = z_copy(1, second_out_b, third_in_b)
    copy_a = z_copy(0, second_out_a, third_in_a)
    ring_end(copies_d, *ring_d, 1, keep(second_out_b))
    copy_b.start()
    ring_end(copies_c, *ring_c, 1, keep(second_out_a))
    copy_a.start()

    wait_all(BACK, lambda peer: back_all.at[:, chan_rows(peer), :], back_send.at[:2])

    def use_back(r):
        rows = pl.ds(pl.multiple_of(r * 128, 128), 128)
        for half in range(2):
            cols = slice(half * B, (half + 1) * B)
            back = back_all[half, rows, :].astype(F32)
            grad_key_ref[rows, cols] = (v_ref[rows, cols].astype(F32) * back).astype(BF16)
            grad_value_ref[rows, cols] = (k_ref[rows, cols].astype(F32) * back).astype(BF16)

    loop(ROWS // 128, use_back)
    stores[2].start()
    stores[3].start()

    for c in range(2):
        ring_middle(last_c[c], *rings_e[c], 1)
    for c in range(2):
        ring_end(last_c[c], *rings_e[c], 1, final_c(c))
    copy_b.wait_recv()
    total = second_out_b[iz].astype(F32) + third_in_b[...].astype(F32)
    weight_grad_ref[:, WA : WA + WB] = total * weight_factor
    copy_a.wait_recv()
    total = second_out_a[iz].astype(F32) + third_in_a[...].astype(F32)
    weight_grad_ref[:, :WA] = total * weight_factor

    for store_out in stores:
        store_out.wait()
    for make in (taps_copy, up_copy, conv_copy, back_copy, filt_copy):
        for_peers(me, lambda peer: make(peer).wait_send())
    rings = (*copies_a, *copies_b0, *copies_b1, *copies_c, *copies_d)
    rings += (*first_c[0], *first_c[1], *last_c[0], *last_c[1], *across)
    for c in (x_core, x_near, x_pass, *rings, copy_a, copy_b):
        c.wait_send()


def hand_over(*refs):
    count = len(refs) // 3
    sources, targets, held = refs[:count], refs[count : 2 * count], refs[2 * count : 3 * count]
    sems = refs[3 * count]
    loads = [pltpu.make_async_copy(sources[c], held[c], sems.at[0, c]) for c in range(count)]
    stores = [pltpu.make_async_copy(held[c], targets[c], sems.at[1, c]) for c in range(count)]
    for load in loads:
        load.start()
    for load, store in zip(loads, stores):
        load.wait()
        store.start()
    for store in stores:
        store.wait()


def per_device(layer_input, query_proj, key_proj, value_proj, filter_taps, grad_out):
    vmem = pl.BlockSpec(memory_space=pltpu.VMEM)
    hbm = pl.BlockSpec(memory_space=pl.ANY)
    rows = jax.ShapeDtypeStruct((ROWS, T), BF16)
    shapes = (
        rows,
        rows,
        rows,
        rows,
        jax.ShapeDtypeStruct((2, T), F32),
        jax.ShapeDtypeStruct((128, ROWS), F32),
    )
    results = pl.pallas_call(
        kernel,
        out_shape=shapes,
        in_specs=[hbm] * 4 + [vmem, hbm],
        out_specs=[hbm] * 4 + [vmem] * 2,
        scratch_shapes=[pltpu.VMEM((ROWS, T), BF16)] * 8
        + [
            pltpu.VMEM((2, ROWS, B), BF16),
            pltpu.VMEM((2, ROWS, B), BF16),
            pltpu.VMEM((2, 8, 128), F32),
            pltpu.VMEM((N, 8, 128), F32),
            pltpu.VMEM((PAD + NB, CH, B), BF16),
            pltpu.VMEM((NB + PAD, CH, B), BF16),
            pltpu.VMEM((B, NB * CH), BF16),
            pltpu.VMEM((NB, B, B), BF16),
            pltpu.VMEM((2 * B, B), F32),
            pltpu.VMEM((NB, CH, B), BF16),
            pltpu.VMEM((NB, CH, B), BF16),
            pltpu.VMEM((2, ROWS, B), BF16),
            pltpu.VMEM((2, ROWS, B), BF16),
            pltpu.VMEM((2, NB + 1, 8, B), F32),
            pltpu.VMEM((N, 8, 128), F32),
            pltpu.VMEM((N, 8, 128), F32),
            pltpu.VMEM((N, 128, T), BF16),
            pltpu.VMEM((4, 2, 4, 128, WA), BF16),
            pltpu.VMEM((4, 2, 4, 128, WB), BF16),
            pltpu.VMEM((6, 4, 128, WA), BF16),
            pltpu.VMEM((2, 6, 2, 128, WB), BF16),
            pltpu.VMEM((4, 2, 1, 128, WA), BF16),
            pltpu.VMEM((4, 2, 1, 128, WB), BF16),
            pltpu.VMEM((6, 1, 128, WA), BF16),
            pltpu.VMEM((6, 1, 128, WB), BF16),
            pltpu.VMEM((2, 128, WA), BF16),
            pltpu.VMEM((2, 128, WB), BF16),
            pltpu.VMEM((128, WA), BF16),
            pltpu.VMEM((128, WB), BF16),
            pltpu.VMEM((2, 2, 4, 4, 128, WC), BF16),
            pltpu.VMEM((2, 4, 4, 128, WC), BF16),
            pltpu.VMEM((2, 6, 2, 128, WC), BF16),
            pltpu.VMEM((2, 4, 2, 1, 64, WC), BF16),
            pltpu.VMEM((2, 6, 1, 64, WC), BF16),
            pltpu.SemaphoreType.DMA((KINDS, N)),
            pltpu.SemaphoreType.DMA((KINDS, N)),
            pltpu.SemaphoreType.DMA((3,)),
            pltpu.SemaphoreType.DMA((3,)),
            pltpu.SemaphoreType.DMA((9, 6)),
            pltpu.SemaphoreType.DMA((9, 6)),
            pltpu.SemaphoreType.DMA((4,)),
            pltpu.SemaphoreType.DMA((4,)),
            pltpu.SemaphoreType.DMA((5,)),
            pltpu.SemaphoreType.DMA((4,)),
        ],
        compiler_params=pltpu.CompilerParams(
            collective_id=0, has_side_effects=True, vmem_limit_bytes=62 * 2**20
        ),
    )(
        layer_input.reshape(8, 128, T),
        query_proj,
        key_proj,
        value_proj,
        filter_taps,
        grad_out,
    )
    return tuple(
        pl.pallas_call(
            hand_over,
            out_shape=shapes,
            in_specs=[hbm] * 6,
            out_specs=[hbm] * 6,
            scratch_shapes=[pltpu.VMEM(shape.shape, shape.dtype) for shape in shapes]
            + [pltpu.SemaphoreType.DMA((2, 6))],
        )(*results)
    )


def solution(mesh):
    placed = (P("chan", "seq"),) * 6
    return jax.shard_map(
        per_device,
        mesh=mesh,
        in_specs=placed,
        out_specs=(P("chan", "seq"),) * 5 + (P("seq", "chan"),),
        check_vma=False,
    )
```
